32 devices in a mesh: clip: 4 (over z), seq: 8 (over y, x, core).
Axes of the slice: x: 2, y: 2, z: 4, core: 2. Of those that a mesh axis runs over, the one named last changes fastest.
Arguments:
- patches: bfloat16 [4, 1568, 1024], P('clip', 'seq'), may hold values from -6 to 12
- segment: int32 [4, 1568], P('clip', 'seq'), may hold values from 0 to 191, as said below
- dest_shard: int32 [4, 1536], P('clip', 'seq'), may hold values from -1 to 7, as said below
- dest_slot: int32 [4, 1536], P('clip', 'seq'), may hold values from -1 to 63, as said below
- w_qkv: bfloat16 [1024, 1536], replicated, may hold values from -1 to 4
- out_grad: bfloat16 [4, 512, 512], P('clip', 'seq'), may hold values from -6 to 6
Outputs:
- attended: bfloat16 [4, 512, 512], P('clip', 'seq')
- patch_grad: bfloat16 [4, 1568, 1024], P('clip', 'seq')
- weight_grad: float32 [1024, 1536], P('seq', 'clip')
The draws below stay inside these ranges and needn't reach their ends.
Inputs may be any that keep to these rules, and one draw needn't show every extreme that they name: `segment`: within each block of 196 patches the ids start at 0, never fall and skip no value; every id names one or more patches. The number of tokens of a block is one more than its largest id. `dest_shard`: -1 exactly on the rows of a block past its number of tokens. A block of 192 rows sends at most 24 rows to each receiving block of its clip, and every receiving block gets exactly 64 rows. `dest_slot`: -1 exactly where dest_shard is -1; the rows sent to one receiving block take its rows 0 to 63 once each.
All inputs are finite; a program needn't handle non-finite values.
Results may differ from the reference program's by a relative error of at most 0.024.
Values may be sent and summed in bfloat16 or wider, within the bound.
No kernel may reach another device: no remote copies, remote signals or barrier semaphores. Data moves between devices by JAX's collectives and lax.ppermute only.
A program may use at most 64 MiB of HBM per device.

```python
import jax
import jax.numpy as jnp
from jax import lax

D = 1024
HEADS = 8
HEAD_DIM = 64
R_DEV = 64
INNER = 512
P_DEV = 196
TOK_MAX = 192
CLIPS = 4
PATCHES = 1568
ROWS = 512
TOK_ROWS = 1536
N_SEQ = 8


base_tokens = 16


def clip_plan(key):
    shard_count = PATCHES // P_DEV
    total_rows = shard_count * R_DEV
    shard_index = jnp.arange(shard_count, dtype=jnp.int32)
    planted = jax.random.randint(jax.random.fold_in(key, 1), (), 0, shard_count)
    raw_weight = jax.random.randint(jax.random.fold_in(key, 2), (shard_count,), 1, 4)
    weighting = jnp.where(shard_index == planted, 0, raw_weight)
    surplus = total_rows - TOK_MAX - (shard_count - 1) * base_tokens
    upper = jnp.cumsum(weighting)
    lower = upper - weighting
    weight_sum = upper[-1]
    shares = surplus * upper // weight_sum - surplus * lower // weight_sum
    loads = jnp.where(shard_index == planted, TOK_MAX, base_tokens + shares).astype(jnp.int32)

    def shard_segments(index):
        ranking = jnp.argsort(jax.random.permutation(jax.random.fold_in(key, 100 + index), P_DEV - 1))
        cutting = (ranking < loads[index] - 1).astype(jnp.int32)
        return jnp.concatenate([jnp.zeros((1,), jnp.int32), jnp.cumsum(cutting).astype(jnp.int32)])
    segments = jax.vmap(shard_segments)(shard_index).reshape(-1)
    offsets = jnp.cumsum(loads) - loads
    local_rows = jnp.arange(TOK_MAX, dtype=jnp.int32)
    global_rows = offsets[:, None] + local_rows[None, :]
    living = local_rows[None, :] < loads[:, None]
    turning = jax.random.randint(jax.random.fold_in(key, 3), (), 0, shard_count)
    targets = (global_rows + turning) % shard_count
    ranks = (global_rows - (targets - turning) % shard_count) // shard_count
    ranks = jnp.clip(ranks, 0, R_DEV - 1)

    def slot_order(subkey):
        return jax.random.permutation(subkey, R_DEV)
    orders = jax.vmap(slot_order)(jax.random.split(jax.random.fold_in(key, 4), shard_count))
    slots = orders[targets, ranks]
    shard_dest = jnp.where(living, targets, -1).reshape(-1).astype(jnp.int32)
    shard_slot = jnp.where(living, slots, -1).reshape(-1).astype(jnp.int32)
    return (segments.astype(jnp.int32), shard_dest, shard_slot)


def plan_all(key):
    clip_keys = jax.random.split(jax.random.fold_in(key, 7), CLIPS)
    return jax.vmap(clip_plan)(clip_keys)


def plant_plan(key):
    features = jax.random.permutation(jax.random.fold_in(key, 11), D)[:HEADS].astype(jnp.int32)
    columns = jax.random.randint(jax.random.fold_in(key, 12), (HEADS,), 0, HEAD_DIM).astype(jnp.int32)
    return (features, columns)


def draw_segment(key, part):
    return plan_all(key)[0]


def draw_dest_shard(key, part):
    return plan_all(key)[1]


def draw_dest_slot(key, part):
    return plan_all(key)[2]


def draw_w_qkv(key, part):
    features, columns = plant_plan(key)
    weight_key = jax.random.fold_in(key, 13)
    random_part = jax.random.truncated_normal(weight_key, -6.0, 6.0, (D, 3 * INNER), jnp.float32)
    random_part = random_part * D ** (-0.5)
    strength = 4.0
    head_columns = jnp.arange(HEADS, dtype=jnp.int32) * HEAD_DIM + columns
    special = jnp.concatenate([head_columns, head_columns + INNER])
    special_rows = jnp.concatenate([features, features])
    matching = jnp.arange(3 * INNER, dtype=jnp.int32)[:, None] == special[None, :]
    is_special = jnp.any(matching, axis=1)
    row_of = jnp.sum(jnp.where(matching, special_rows[None, :], 0), axis=1)
    planted = jnp.where(jnp.arange(D, dtype=jnp.int32)[:, None] == row_of[None, :], strength, 0.0)
    return jnp.where(is_special[None, :], planted, random_part).astype(jnp.bfloat16)


def draw_patches(key, part):
    segments = plan_all(key)[0]
    features, columns = plant_plan(key)
    shard_count = PATCHES // P_DEV
    feature_ids = jnp.arange(D, dtype=jnp.int32)
    marked = jnp.any(feature_ids[:, None] == features[None, :], axis=1)
    feature_scale = jnp.where(marked, 1.0 / 64.0, 1.0)
    block_of = jnp.arange(PATCHES, dtype=jnp.int32) // P_DEV
    clip_keys = jax.random.split(jax.random.fold_in(key, 14), CLIPS)

    def one_clip(inputs):
        clip_key, clip_segments = inputs
        noise_rows = jax.random.truncated_normal(clip_key, -6.0, 6.0, (PATCHES, D), jnp.float32)
        item_index = clip_segments * shard_count + block_of
        planted = item_index < 6 * HEADS
        head_of = jnp.minimum(item_index // 6, HEADS - 1)
        strength = item_index % 6 // 2
        partner = (item_index % 2).astype(jnp.float32)
        amount = 8.0 + 2.0 * strength.astype(jnp.float32) - partner * jnp.where(strength == 0, 0.125, 0.0625)
        row_scale = jnp.where(planted, 0.5, 1.0)
        noisy_rows = noise_rows * feature_scale[None, :] * row_scale[:, None]
        planted_cell = planted[:, None] & (feature_ids[None, :] == features[head_of][:, None])
        return jnp.where(planted_cell, amount[:, None], noisy_rows)
    return lax.map(one_clip, (clip_keys, segments)).astype(jnp.bfloat16)


def draw_out_grad(key, part):
    segments, dests, slots = plan_all(key)
    shard_count = PATCHES // P_DEV
    token_rows = jnp.arange(TOK_ROWS, dtype=jnp.int32)
    item_index = token_rows % TOK_MAX * shard_count + token_rows // TOK_MAX
    clip_keys = jax.random.split(jax.random.fold_in(key, 21), CLIPS)

    def one_clip(inputs):
        clip_key, clip_dest, clip_slot = inputs
        planted = (item_index < 6 * HEADS) & (clip_dest >= 0)
        target = jnp.where(clip_dest >= 0, clip_dest * R_DEV + clip_slot, -1)
        hit = jnp.any((target[None, :] == jnp.arange(ROWS, dtype=jnp.int32)[:, None]) & planted[None, :], axis=1)
        row_scale = jnp.where(hit, 1.0 / 16.0, 1.0)
        noise_rows = jax.random.truncated_normal(clip_key, -6.0, 6.0, (ROWS, INNER), jnp.float32)
        return noise_rows * row_scale[:, None]
    return lax.map(one_clip, (clip_keys, dests, slots)).astype(jnp.bfloat16)


def setup_inputs(seed: int = 0) -> dict:
    splits = jax.random.split(jax.random.key(seed), 7)
    patches = draw_patches(jax.random.fold_in(splits[6], 71), 0)
    segment = draw_segment(jax.random.fold_in(splits[6], 71), 0)
    dest_shard = draw_dest_shard(jax.random.fold_in(splits[6], 71), 0)
    dest_slot = draw_dest_slot(jax.random.fold_in(splits[6], 71), 0)
    w_qkv = draw_w_qkv(jax.random.fold_in(splits[6], 71), 0)
    out_grad = draw_out_grad(jax.random.fold_in(splits[6], 71), 0)
    return dict(patches=patches, segment=segment, dest_shard=dest_shard, dest_slot=dest_slot, w_qkv=w_qkv, out_grad=out_grad)


def one_clip(w_qkv, clip_patches, clip_segment, clip_dest, clip_slot, clip_grad):
    scaling = HEAD_DIM ** -0.5
    shard_of = jnp.arange(PATCHES, dtype=jnp.int32) // P_DEV
    token_id = (shard_of * TOK_MAX + clip_segment).astype(jnp.int32)
    token_sums = jax.ops.segment_sum(clip_patches.astype(jnp.float32), token_id, num_segments=TOK_ROWS)
    counts = jax.ops.segment_sum(jnp.ones((PATCHES,), jnp.float32), token_id, num_segments=TOK_ROWS)
    tokens = (token_sums / jnp.maximum(counts, 1.0)[:, None]).astype(jnp.bfloat16)
    target = jnp.where(clip_dest >= 0, clip_dest * R_DEV + clip_slot, ROWS).astype(jnp.int32)
    placed = jnp.zeros((ROWS, D), jnp.bfloat16).at[target].set(tokens, mode="drop")
    projected = jnp.dot(placed, w_qkv, preferred_element_type=jnp.float32).astype(jnp.bfloat16)

    def by_heads(matrix):
        return matrix.reshape(ROWS, HEADS, HEAD_DIM).transpose(1, 0, 2)

    head_query = by_heads(projected[:, :INNER])
    head_key = by_heads(projected[:, INNER:2 * INNER])
    head_value = by_heads(projected[:, 2 * INNER:])
    head_grad = by_heads(clip_grad)

    def per_head(inputs):
        query, keys_in, values, grads = inputs
        scores = jnp.dot(query, keys_in.T, preferred_element_type=jnp.float32) * scaling
        row_max = jnp.max(scores, axis=1, keepdims=True)
        weights = jnp.exp(scores - row_max)
        row_total = jnp.sum(weights, axis=1, keepdims=True)
        output = jnp.dot(weights.astype(jnp.bfloat16), values, preferred_element_type=jnp.float32)
        output = (output / row_total).astype(jnp.bfloat16)
        log_total = row_max + jnp.log(row_total)
        grad_dot = jnp.sum(grads.astype(jnp.float32) * output.astype(jnp.float32), axis=1, keepdims=True)
        probability = jnp.exp(scores - log_total)
        prob_grad = jnp.dot(grads, values.T, preferred_element_type=jnp.float32)
        score_grad = (probability * (prob_grad - grad_dot)).astype(jnp.bfloat16)
        query_grad = jnp.dot(score_grad, keys_in, preferred_element_type=jnp.float32) * scaling
        key_grad = jnp.dot(score_grad.T, query, preferred_element_type=jnp.float32) * scaling
        value_grad = jnp.dot(probability.astype(jnp.bfloat16).T, grads, preferred_element_type=jnp.float32)
        return output, query_grad, key_grad, value_grad

    results = lax.map(per_head, (head_query, head_key, head_value, head_grad))

    def to_rows(matrix):
        return matrix.transpose(1, 0, 2).reshape(ROWS, INNER)

    attended = to_rows(results[0])
    proj_grad = jnp.concatenate([to_rows(results[1]), to_rows(results[2]), to_rows(results[3])], axis=1).astype(jnp.bfloat16)
    placed_grad = jnp.dot(proj_grad, w_qkv.T, preferred_element_type=jnp.float32).astype(jnp.bfloat16)

    def add_shard(running, inputs):
        shard_rows, shard_grads = inputs
        partial_value = jnp.dot(shard_rows.T, shard_grads, preferred_element_type=jnp.float32).astype(jnp.bfloat16)
        return running + partial_value.astype(jnp.float32), None

    clip_weight, _ = lax.scan(add_shard, jnp.zeros((D, 3 * INNER), jnp.float32),
                              (placed.reshape(N_SEQ, R_DEV, D), proj_grad.reshape(N_SEQ, R_DEV, 3 * INNER)))
    fetched = jnp.take(placed_grad, jnp.minimum(target, ROWS - 1), axis=0)
    token_grad = jnp.where((clip_dest >= 0)[:, None], fetched, jnp.zeros_like(fetched))
    patch_grad = (token_grad[token_id].astype(jnp.float32) / counts[token_id][:, None]).astype(jnp.bfloat16)
    return attended, patch_grad, clip_weight


def reference(patches, segment, dest_shard, dest_slot, w_qkv, out_grad):
    def per_clip(running, inputs):
        attended, patch_grad, clip_weight = one_clip(w_qkv, *inputs)
        return running + clip_weight, (attended, patch_grad)

    weight_grad, (attended, patch_grad) = lax.scan(
        per_clip, jnp.zeros((D, 3 * INNER), jnp.float32), (patches, segment, dest_shard, dest_slot, out_grad))
    return attended, patch_grad, weight_grad
```

```python
import jax
import jax.numpy as jnp
from jax import lax
from jax.experimental import pallas as pl
from jax.experimental.pallas import tpu as pltpu
from jax.sharding import PartitionSpec as P

HEADS = 8
HEAD_DIM = 64


neg_large = -1e30


def split_heads(rows_in):
    return rows_in.reshape(rows_in.shape[0], HEADS, HEAD_DIM)


def forward_fold(query_heads, running, pieces):
    scaling = HEAD_DIM ** (-0.5)
    row_max, row_total, weighted = running
    key_heads = split_heads(pieces[0])
    value_heads = split_heads(pieces[1])
    scores = (
        jnp.einsum("rhd,khd->hrk", query_heads, key_heads, preferred_element_type=jnp.float32)
        * scaling
    )
    new_max = jnp.maximum(row_max, jnp.max(scores, axis=2))
    weights = jnp.exp(scores - new_max[:, :, None])
    row_total = jnp.sum(weights, axis=2)
    weighted = jnp.einsum(
        "hrk,khd->hrd",
        weights.astype(jnp.bfloat16),
        value_heads,
        preferred_element_type=jnp.float32,
    )
    return (new_max, row_total, weighted)


def query_fold(query_heads, grad_heads, log_total, grad_dot):
    scaling = HEAD_DIM ** (-0.5)

    def combine_piece(running, pieces, offset):
        key_heads = split_heads(pieces[0])
        value_heads = split_heads(pieces[1])
        scores = (
            jnp.einsum("rhd,khd->hrk", query_heads, key_heads, preferred_element_type=jnp.float32)
            * scaling
        )
        probability = jnp.exp(scores - log_total[:, :, None])
        prob_grad = jnp.einsum(
            "rhd,khd->hrk", grad_heads, value_heads, preferred_element_type=jnp.float32
        )
        score_grad = (probability * (prob_grad - grad_dot[:, :, None])).astype(jnp.bfloat16)
        return (
            jnp.einsum("hrk,khd->hrd", score_grad, key_heads, preferred_element_type=jnp.float32)
            * scaling
        )

    return combine_piece


def key_fold(key_heads, value_heads, all_log, all_dot, pieces):
    scaling = HEAD_DIM ** (-0.5)
    piece_query = split_heads(pieces[0])
    piece_grad = split_heads(pieces[1])
    piece_log = all_log.T
    piece_dot = all_dot.T
    scores = (
        jnp.einsum("qhd,khd->hqk", piece_query, key_heads, preferred_element_type=jnp.float32)
        * scaling
    )
    probability = jnp.exp(scores - piece_log[:, :, None])
    value_grad = jnp.einsum(
        "hqk,qhd->hkd",
        probability.astype(jnp.bfloat16),
        piece_grad,
        preferred_element_type=jnp.float32,
    )
    prob_grad = jnp.einsum(
        "qhd,khd->hqk", piece_grad, value_heads, preferred_element_type=jnp.float32
    )
    score_grad = (probability * (prob_grad - piece_dot[:, :, None])).astype(jnp.bfloat16)
    key_grad = (
        jnp.einsum("hqk,qhd->hkd", score_grad, piece_query, preferred_element_type=jnp.float32)
        * scaling
    )
    return (key_grad, value_grad)


def head_rows(matrix):
    return matrix.transpose(1, 0, 2).reshape(matrix.shape[1], HEADS * HEAD_DIM)


def rows_plan(patches, segment, dest_shard, dest_slot, w_qkv, out_grad):
    shard_count = lax.axis_size("seq")
    patch_rows = patches[0]
    patch_token = segment[0]
    targets = dest_shard[0]
    slot_ids = dest_slot[0]
    token_cap = targets.shape[0]
    pair_cap = token_cap // shard_count
    local_rows = out_grad.shape[1]
    inner_width = HEADS * HEAD_DIM
    member = (
        lax.broadcasted_iota(jnp.int32, (token_cap, patch_token.shape[0]), 0)
        == patch_token[None, :]
    )
    member_half = member.astype(jnp.bfloat16)
    counts = jnp.sum(member.astype(jnp.float32), axis=1)
    token_sums = jnp.dot(member_half, patch_rows, preferred_element_type=jnp.float32)
    tokens = (token_sums / jnp.maximum(counts, 1.0)[:, None]).astype(jnp.bfloat16)
    to_shard = (
        targets[:, None] == lax.broadcasted_iota(jnp.int32, (token_cap, shard_count), 1)
    ).astype(jnp.int32)
    ranking = jnp.sum((jnp.cumsum(to_shard, axis=0) - 1) * to_shard, axis=1)
    position = jnp.where(targets >= 0, targets * pair_cap + ranking, -1)
    chooser = position[None, :] == lax.broadcasted_iota(
        jnp.int32, (shard_count * pair_cap, token_cap), 0
    )
    chooser_half = chooser.astype(jnp.bfloat16)
    send_rows = jnp.dot(chooser_half, tokens, preferred_element_type=jnp.float32).astype(
        jnp.bfloat16
    )
    send_slot = jnp.sum(chooser.astype(jnp.int32) * (slot_ids + 1)[None, :], axis=1) - 1
    came_rows, came_slot = (
        lax.all_to_all(
            send_rows.reshape(shard_count, pair_cap, -1),
            "seq",
            split_axis=0,
            concat_axis=0,
            tiled=True,
        ),
        lax.all_to_all(
            send_slot.reshape(shard_count, pair_cap), "seq", split_axis=0, concat_axis=0, tiled=True
        ),
    )
    came_slot = came_slot.reshape(-1)
    placer = (
        came_slot[None, :]
        == lax.broadcasted_iota(jnp.int32, (local_rows, shard_count * pair_cap), 0)
    ).astype(jnp.bfloat16)
    placed = jnp.dot(
        placer, came_rows.reshape(shard_count * pair_cap, -1), preferred_element_type=jnp.float32
    ).astype(jnp.bfloat16)
    projected = jnp.dot(placed, w_qkv, preferred_element_type=jnp.float32).astype(jnp.bfloat16)
    query_rows = projected[:, :inner_width]
    key_rows = projected[:, inner_width : 2 * inner_width]
    value_rows = projected[:, 2 * inner_width :]
    query_heads = split_heads(query_rows)
    initial = (
        jnp.full((HEADS, local_rows), neg_large, jnp.float32),
        jnp.zeros((HEADS, local_rows), jnp.float32),
        jnp.zeros((HEADS, local_rows, HEAD_DIM), jnp.float32),
    )
    row_max, row_total, weighted = forward_fold(
        query_heads,
        initial,
        (
            lax.all_gather(key_rows, "seq", axis=0, tiled=True),
            lax.all_gather(value_rows, "seq", axis=0, tiled=True),
        ),
    )
    attended_rows = head_rows((weighted / row_total[:, :, None]).astype(jnp.bfloat16))
    grad_rows = out_grad[0]
    grad_heads = split_heads(grad_rows)
    log_total = row_max + jnp.log(row_total)
    grad_dot = jnp.sum(
        grad_heads.astype(jnp.float32) * split_heads(attended_rows).astype(jnp.float32), axis=2
    )
    blank = jnp.zeros((HEADS, local_rows, HEAD_DIM), jnp.float32)
    query_step = query_fold(query_heads, grad_heads, log_total, grad_dot.T)
    query_grad = query_step(
        blank,
        (
            lax.all_gather(key_rows, "seq", axis=0, tiled=True),
            lax.all_gather(value_rows, "seq", axis=0, tiled=True),
        ),
        jnp.int32(0),
    )
    all_log, all_dot = (
        lax.all_gather(log_total.T, "seq", axis=0, tiled=True),
        lax.all_gather(grad_dot, "seq", axis=0, tiled=True),
    )
    key_grad, value_grad = key_fold(
        split_heads(key_rows),
        split_heads(value_rows),
        all_log,
        all_dot,
        (
            lax.all_gather(query_rows, "seq", axis=0, tiled=True),
            lax.all_gather(grad_rows, "seq", axis=0, tiled=True),
        ),
    )
    proj_grad = jnp.concatenate(
        [head_rows(query_grad), head_rows(key_grad), head_rows(value_grad)], axis=1
    ).astype(jnp.bfloat16)
    placed_grad = jnp.einsum(
        "rc,dc->rd", proj_grad, w_qkv, preferred_element_type=jnp.float32
    ).astype(jnp.bfloat16)
    partial_value = jnp.einsum(
        "rd,rc->dc", placed, proj_grad, preferred_element_type=jnp.float32
    ).astype(jnp.bfloat16)
    across = lax.psum_scatter(partial_value, "seq", scatter_dimension=0, tiled=True).astype(
        jnp.float32
    )
    weight_grad = lax.psum_scatter(
        across.astype(jnp.bfloat16), "clip", scatter_dimension=1, tiled=True
    ).astype(jnp.float32)
    back_rows = jnp.einsum(
        "rj,rd->jd", placer, placed_grad, preferred_element_type=jnp.float32
    ).astype(jnp.bfloat16)
    returned = lax.all_to_all(
        back_rows.reshape(shard_count, pair_cap, -1), "seq", split_axis=0, concat_axis=0, tiled=True
    )
    token_grad = jnp.einsum(
        "jt,jd->td",
        chooser_half,
        returned.reshape(shard_count * pair_cap, -1),
        preferred_element_type=jnp.float32,
    ).astype(jnp.bfloat16)
    patch_sums = jnp.einsum(
        "tp,td->pd", member_half, token_grad, preferred_element_type=jnp.float32
    )
    patch_count = jnp.sum(member.astype(jnp.float32) * counts[:, None], axis=0)
    patch_grad = (patch_sums / patch_count[:, None]).astype(jnp.bfloat16)
    return (attended_rows[None], patch_grad[None], weight_grad)


VMEM_LIMIT = 40 * 1024 * 1024
NN = (((1,), (0,)), ((), ()))
NT = (((1,), (1,)), ((), ()))
TN = (((0,), (0,)), ((), ()))


def dot(left, right, dims=NN):
    return lax.dot_general(left, right, dims, preferred_element_type=jnp.float32)


def call(body, outs, *args, scratch=()):
    return pl.pallas_call(
        body,
        out_shape=outs,
        scratch_shapes=scratch,
        compiler_params=pltpu.CompilerParams(vmem_limit_bytes=VMEM_LIMIT),
    )(*args)


def one_hot(condition):
    return jnp.where(condition, 1.0, 0.0).astype(jnp.bfloat16)


def fold_half(rows):
    half = rows.shape[0] // 2
    return jnp.concatenate([rows[:half], rows[half:]], axis=1)


def unfold_half(rows):
    width = rows.shape[1] // 2
    return jnp.concatenate([rows[:, :width], rows[:, width:]], axis=0)


def wide_row(row):
    short = 256 - row.shape[1]
    wide = row.astype(jnp.float32)
    wide = jnp.concatenate([wide, jnp.full((1, short), -1.0, jnp.float32)], axis=1)
    return wide[:, :128], wide[:, 128:]


def token_kernel(patch_ref, segment_ref, shard_ref, slot_ref, w_ref, grad_ref, send_ref, block_ref):
    token_cap = shard_ref.shape[1]
    local_rows, inner = grad_ref.shape
    devices = send_ref.shape[0]
    width = block_ref.shape[2]
    member = (
        lax.broadcasted_iota(jnp.int32, (token_cap, segment_ref.shape[1]), 0) == segment_ref[...]
    )
    counts = jnp.sum(jnp.where(member, 1.0, 0.0), axis=1, keepdims=True)
    token_sums = dot(one_hot(member), patch_ref[...])
    tokens = (token_sums / jnp.maximum(counts, 1.0)).astype(jnp.bfloat16)
    for place in range(devices):
        block_ref[place] = tokens[:, place * width : (place + 1) * width]
    projected = dot(tokens, w_ref[...]).astype(jnp.bfloat16)
    shard_low, shard_high = wide_row(shard_ref[...])
    slot_low, slot_high = wide_row(slot_ref[...])
    line = lax.broadcasted_iota(jnp.int32, (16, 128), 0)
    where_to = jnp.where(
        line == 0,
        shard_low,
        jnp.where(line == 1, shard_high, jnp.where(line == 2, slot_low, slot_high)),
    ).astype(jnp.bfloat16)
    grads = grad_ref[...]
    for head in range(devices):
        first = head * HEAD_DIM
        query, key, value = (
            projected[:, part * inner + first : part * inner + first + HEAD_DIM]
            for part in range(3)
        )
        start = 0
        for piece in (
            jnp.concatenate([query, key], axis=1),
            fold_half(value),
            where_to,
            fold_half(grads[:, first : first + HEAD_DIM]),
        ):
            send_ref[head, start : start + piece.shape[0]] = piece
            start += piece.shape[0]


def target_row(lines, token_cap, local_rows):
    lines = lines.astype(jnp.float32)
    shard = jnp.concatenate([lines[0:1], lines[1:2]], axis=1)[:, :token_cap]
    slot = jnp.concatenate([lines[2:3], lines[3:4]], axis=1)[:, :token_cap]
    return (shard * local_rows + slot).astype(jnp.int32)


def head_kernel(token_cap, came_ref, attended_ref, proj_ref, target_ref):
    devices, local_rows = came_ref.shape[0], 2 * attended_ref.shape[1]
    rows = devices * local_rows
    scaling = HEAD_DIM ** (-0.5)
    half_cap = token_cap // 2
    lines_at = token_cap + half_cap
    row_id = lax.broadcasted_iota(jnp.int32, (rows, token_cap), 0)
    total = jnp.zeros((rows, 3 * HEAD_DIM), jnp.float32)
    grads = []
    for sender in range(devices):
        target = target_row(came_ref[sender, lines_at : lines_at + 16], token_cap, local_rows)
        target_ref[sender : sender + 1, :] = target
        placer = one_hot(row_id == target)
        rows_in = jnp.concatenate(
            [
                came_ref[sender, :token_cap],
                unfold_half(came_ref[sender, token_cap:lines_at]),
            ],
            axis=1,
        )
        total = total + dot(placer, rows_in)
        grads.append(unfold_half(came_ref[sender, lines_at + 16 :]))
    projected = total.astype(jnp.bfloat16)
    query = projected[:, :HEAD_DIM]
    key = projected[:, HEAD_DIM : 2 * HEAD_DIM]
    value = projected[:, 2 * HEAD_DIM :]
    grad = jnp.concatenate(grads, axis=0)
    scores = dot(key, query, NT) * scaling
    weights = jnp.exp(scores - jnp.max(scores, axis=0, keepdims=True))
    row_total = jnp.sum(weights, axis=0, keepdims=True)
    attended = (dot(value, weights.astype(jnp.bfloat16), TN) / row_total).astype(jnp.bfloat16)
    attended = attended.astype(jnp.float32)
    grad_dot = jnp.sum(grad.astype(jnp.float32).T * attended, axis=0, keepdims=True)
    probability = weights * (1.0 / row_total)
    score_grad = (probability * (dot(value, grad, NT) - grad_dot)).astype(jnp.bfloat16)
    value_grad = dot(probability.astype(jnp.bfloat16), grad)
    key_grad = dot(score_grad, query) * scaling
    query_grad = (dot(key, score_grad, TN) * scaling).T
    attended = attended.T.astype(jnp.bfloat16)
    for place in range(devices):
        attended_ref[place] = fold_half(attended[place * local_rows : (place + 1) * local_rows])
    proj_ref[:rows] = jnp.concatenate([query_grad, key_grad], axis=1).astype(jnp.bfloat16)
    proj_ref[rows:] = fold_half(value_grad.astype(jnp.bfloat16))


def block_kernel(came_ref, target_ref, placed_ref):
    devices, token_cap, width = came_ref.shape
    rows = placed_ref.shape[1]
    row_id = lax.broadcasted_iota(jnp.int32, (rows, token_cap), 0)
    total = jnp.zeros((rows, width), jnp.float32)
    for sender in range(devices):
        total = total + dot(one_hot(row_id == target_ref[sender : sender + 1, :]), came_ref[sender])
    placed_ref[...] = total.T.astype(jnp.bfloat16)


def by_column(left, pieces, held_ref):
    rows = left.shape[1]
    half = rows // 2
    me = lax.axis_index("seq")
    for flip, piece in enumerate(pieces):
        both = dot(left, piece[:rows])
        low = dot(left[:, :half], piece[rows:])
        high = dot(left[:, half:], piece[rows:])
        value = low[:, :HEAD_DIM] + high[:, HEAD_DIM:]
        held_ref[jnp.bitwise_xor(me, flip)] = jnp.concatenate([both, value], axis=1)
    return jnp.concatenate(
        [
            held_ref[head, :, part * HEAD_DIM : (part + 1) * HEAD_DIM]
            for part in range(3)
            for head in range(len(pieces))
        ],
        axis=1,
    )


def weight_kernel(placed_ref, *refs):
    pieces, outs, (held_ref, block_ref) = refs[:HEADS], refs[HEADS:-2], refs[-2:]
    columns = by_column(placed_ref[...], pieces, held_ref).astype(jnp.bfloat16)
    width = columns.shape[1] // len(outs)
    me = lax.axis_index("clip")
    for index in range(len(outs)):
        block_ref[index] = columns[:, index * width : (index + 1) * width]
    for flip, out in enumerate(outs):
        out[...] = block_ref[jnp.bitwise_xor(me, flip)]


def patch_kernel(segment_ref, shard_ref, slot_ref, w_ref, came_ref, *refs):
    pieces, (patch_ref, attended_ref, held_ref) = refs[:HEADS], refs[HEADS:]
    token_cap = shard_ref.shape[1]
    local_rows = attended_ref.shape[0]
    rows = came_ref.shape[0] * local_rows
    shard = shard_ref[...]
    target = jnp.where(shard >= 0, shard * local_rows + slot_ref[...], -1)
    row_id = lax.broadcasted_iota(jnp.int32, (rows, token_cap), 0)
    chooser = jnp.where(row_id == target, 1.0, 0.0).T.astype(jnp.bfloat16)
    proj_grad = by_column(chooser, pieces, held_ref).astype(jnp.bfloat16)
    token_grad = dot(proj_grad, w_ref[...], NT).astype(jnp.bfloat16).astype(jnp.float32)
    member = (
        lax.broadcasted_iota(jnp.int32, (token_cap, segment_ref.shape[1]), 0) == segment_ref[...]
    )
    counts = jnp.sum(jnp.where(member, 1.0, 0.0), axis=1, keepdims=True)
    shared = (token_grad / jnp.maximum(counts, 1.0)).astype(jnp.bfloat16)
    patch_ref[...] = dot(one_hot(member), shared, TN).astype(jnp.bfloat16)
    attended_ref[...] = jnp.concatenate(
        [unfold_half(came_ref[head]) for head in range(came_ref.shape[0])], axis=1
    )


def sum_kernel(*refs):
    total = refs[0][...].astype(jnp.float32)
    for ref in refs[1:-1]:
        total = total + ref[...].astype(jnp.float32)
    refs[-1][...] = total


def exchange(rows, axis, flip):
    count = lax.axis_size(axis)
    return lax.ppermute(rows, axis, [(index, index ^ flip) for index in range(count)])


def all_to_all(rows):
    return lax.all_to_all(rows, "seq", split_axis=0, concat_axis=0, tiled=True)


def shape(*sizes, dtype=jnp.bfloat16):
    return jax.ShapeDtypeStruct(sizes, dtype)


def heads_plan(patches, segment, dest_shard, dest_slot, w_qkv, out_grad):
    devices = lax.axis_size("seq")
    clips = lax.axis_size("clip")
    token_cap = dest_shard.shape[1]
    local_rows, inner = out_grad.shape[1:]
    rows = devices * local_rows
    model = patches.shape[2]
    width = model // devices
    sent = token_cap + token_cap // 2 + 16 + local_rows // 2
    send, blocks = call(
        token_kernel,
        [shape(devices, sent, 2 * HEAD_DIM), shape(devices, token_cap, width)],
        patches[0],
        segment,
        dest_shard,
        dest_slot,
        w_qkv,
        out_grad[0],
    )
    came = all_to_all(send)
    came_blocks = all_to_all(blocks)
    attended_send, proj, target = call(
        lambda *refs: head_kernel(token_cap, *refs),
        [
            shape(devices, local_rows // 2, 2 * HEAD_DIM),
            shape(rows + rows // 2, 2 * HEAD_DIM),
            shape(devices, token_cap, dtype=jnp.int32),
        ],
        came,
    )
    placed = call(block_kernel, shape(width, rows), came_blocks, target)
    even = [proj] + [exchange(proj, "seq", flip) for flip in range(2, devices, 2)]
    odd = [exchange(piece, "seq", 1) for piece in even]
    pieces = [piece for pair in zip(even, odd) for piece in pair]
    weights = call(
        weight_kernel,
        [shape(width, 3 * inner // clips)] * clips,
        placed,
        *pieces,
        scratch=[
            pltpu.VMEM((devices, width, 3 * HEAD_DIM), jnp.float32),
            pltpu.VMEM((clips, width, 3 * inner // clips), jnp.bfloat16),
        ],
    )
    weights = [weights[0]] + [exchange(weights[flip], "clip", flip) for flip in range(1, clips)]
    patch_grad, attended = call(
        patch_kernel,
        [shape(patches.shape[1], model), shape(local_rows, inner)],
        segment,
        dest_shard,
        dest_slot,
        w_qkv,
        all_to_all(attended_send),
        *pieces,
        scratch=[pltpu.VMEM((devices, token_cap, 3 * HEAD_DIM), jnp.float32)],
    )
    weight_grad = call(
        sum_kernel, shape(width, 3 * inner // clips, dtype=jnp.float32), *weights
    )
    return attended[None], patch_grad[None], weight_grad


def solution(mesh):
    devices, clips = mesh.shape["seq"], mesh.shape["clip"]
    one_head_each = devices == HEADS and clips in (1, 2, 4, 8)
    return jax.shard_map(
        heads_plan if one_head_each else rows_plan,
        mesh=mesh,
        in_specs=(
            P("clip", "seq", None),
            P("clip", "seq"),
            P("clip", "seq"),
            P("clip", "seq"),
            P(),
            P("clip", "seq", None),
        ),
        out_specs=(P("clip", "seq", None), P("clip", "seq", None), P("seq", "clip")),
        check_vma=False,
    )
```

```python
import jax
import jax.numpy as jnp
from jax import lax
from jax.experimental import pallas as pl
from jax.experimental.pallas import tpu as pltpu
from jax.sharding import PartitionSpec as P

HEADS = 8
HEAD_DIM = 64


neg_large = -1e30


def split_heads(rows_in):
    return rows_in.reshape(rows_in.shape[0], HEADS, HEAD_DIM)


def forward_fold(query_heads, running, pieces):
    scaling = HEAD_DIM ** (-0.5)
    row_max, row_total, weighted = running
    key_heads = split_heads(pieces[0])
    value_heads = split_heads(pieces[1])
    scores = (
        jnp.einsum("rhd,khd->hrk", query_heads, key_heads, preferred_element_type=jnp.float32)
        * scaling
    )
    new_max = jnp.maximum(row_max, jnp.max(scores, axis=2))
    weights = jnp.exp(scores - new_max[:, :, None])
    row_total = jnp.sum(weights, axis=2)
    weighted = jnp.einsum(
        "hrk,khd->hrd",
        weights.astype(jnp.bfloat16),
        value_heads,
        preferred_element_type=jnp.float32,
    )
    return (new_max, row_total, weighted)


def query_fold(query_heads, grad_heads, log_total, grad_dot):
    scaling = HEAD_DIM ** (-0.5)

    def combine_piece(running, pieces, offset):
        key_heads = split_heads(pieces[0])
        value_heads = split_heads(pieces[1])
        scores = (
            jnp.einsum("rhd,khd->hrk", query_heads, key_heads, preferred_element_type=jnp.float32)
            * scaling
        )
        probability = jnp.exp(scores - log_total[:, :, None])
        prob_grad = jnp.einsum(
            "rhd,khd->hrk", grad_heads, value_heads, preferred_element_type=jnp.float32
        )
        score_grad = (probability * (prob_grad - grad_dot[:, :, None])).astype(jnp.bfloat16)
        return (
            jnp.einsum("hrk,khd->hrd", score_grad, key_heads, preferred_element_type=jnp.float32)
            * scaling
        )

    return combine_piece


def key_fold(key_heads, value_heads, all_log, all_dot, pieces):
    scaling = HEAD_DIM ** (-0.5)
    piece_query = split_heads(pieces[0])
    piece_grad = split_heads(pieces[1])
    piece_log = all_log.T
    piece_dot = all_dot.T
    scores = (
        jnp.einsum("qhd,khd->hqk", piece_query, key_heads, preferred_element_type=jnp.float32)
        * scaling
    )
    probability = jnp.exp(scores - piece_log[:, :, None])
    value_grad = jnp.einsum(
        "hqk,qhd->hkd",
        probability.astype(jnp.bfloat16),
        piece_grad,
        preferred_element_type=jnp.float32,
    )
    prob_grad = jnp.einsum(
        "qhd,khd->hqk", piece_grad, value_heads, preferred_element_type=jnp.float32
    )
    score_grad = (probability * (prob_grad - piece_dot[:, :, None])).astype(jnp.bfloat16)
    key_grad = (
        jnp.einsum("hqk,qhd->hkd", score_grad, piece_query, preferred_element_type=jnp.float32)
        * scaling
    )
    return (key_grad, value_grad)


def head_rows(matrix):
    return matrix.transpose(1, 0, 2).reshape(matrix.shape[1], HEADS * HEAD_DIM)


def rows_plan(patches, segment, dest_shard, dest_slot, w_qkv, out_grad):
    shard_count = lax.axis_size("seq")
    patch_rows = patches[0]
    patch_token = segment[0]
    targets = dest_shard[0]
    slot_ids = dest_slot[0]
    token_cap = targets.shape[0]
    pair_cap = token_cap // shard_count
    local_rows = out_grad.shape[1]
    inner_width = HEADS * HEAD_DIM
    member = (
        lax.broadcasted_iota(jnp.int32, (token_cap, patch_token.shape[0]), 0)
        == patch_token[None, :]
    )
    member_half = member.astype(jnp.bfloat16)
    counts = jnp.sum(member.astype(jnp.float32), axis=1)
    token_sums = jnp.dot(member_half, patch_rows, preferred_element_type=jnp.float32)
    tokens = (token_sums / jnp.maximum(counts, 1.0)[:, None]).astype(jnp.bfloat16)
    to_shard = (
        targets[:, None] == lax.broadcasted_iota(jnp.int32, (token_cap, shard_count), 1)
    ).astype(jnp.int32)
    ranking = jnp.sum((jnp.cumsum(to_shard, axis=0) - 1) * to_shard, axis=1)
    position = jnp.where(targets >= 0, targets * pair_cap + ranking, -1)
    chooser = position[None, :] == lax.broadcasted_iota(
        jnp.int32, (shard_count * pair_cap, token_cap), 0
    )
    chooser_half = chooser.astype(jnp.bfloat16)
    send_rows = jnp.dot(chooser_half, tokens, preferred_element_type=jnp.float32).astype(
        jnp.bfloat16
    )
    send_slot = jnp.sum(chooser.astype(jnp.int32) * (slot_ids + 1)[None, :], axis=1) - 1
    came_rows, came_slot = (
        lax.all_to_all(
            send_rows.reshape(shard_count, pair_cap, -1),
            "seq",
            split_axis=0,
            concat_axis=0,
            tiled=True,
        ),
        lax.all_to_all(
            send_slot.reshape(shard_count, pair_cap), "seq", split_axis=0, concat_axis=0, tiled=True
        ),
    )
    came_slot = came_slot.reshape(-1)
    placer = (
        came_slot[None, :]
        == lax.broadcasted_iota(jnp.int32, (local_rows, shard_count * pair_cap), 0)
    ).astype(jnp.bfloat16)
    placed = jnp.dot(
        placer, came_rows.reshape(shard_count * pair_cap, -1), preferred_element_type=jnp.float32
    ).astype(jnp.bfloat16)
    projected = jnp.dot(placed, w_qkv, preferred_element_type=jnp.float32).astype(jnp.bfloat16)
    query_rows = projected[:, :inner_width]
    key_rows = projected[:, inner_width : 2 * inner_width]
    value_rows = projected[:, 2 * inner_width :]
    query_heads = split_heads(query_rows)
    initial = (
        jnp.full((HEADS, local_rows), neg_large, jnp.float32),
        jnp.zeros((HEADS, local_rows), jnp.float32),
        jnp.zeros((HEADS, local_rows, HEAD_DIM), jnp.float32),
    )
    row_max, row_total, weighted = forward_fold(
        query_heads,
        initial,
        (
            lax.all_gather(key_rows, "seq", axis=0, tiled=True),
            lax.all_gather(value_rows, "seq", axis=0, tiled=True),
        ),
    )
    attended_rows = head_rows((weighted / row_total[:, :, None]).astype(jnp.bfloat16))
    grad_rows = out_grad[0]
    grad_heads = split_heads(grad_rows)
    log_total = row_max + jnp.log(row_total)
    grad_dot = jnp.sum(
        grad_heads.astype(jnp.float32) * split_heads(attended_rows).astype(jnp.float32), axis=2
    )
    blank = jnp.zeros((HEADS, local_rows, HEAD_DIM), jnp.float32)
    query_step = query_fold(query_heads, grad_heads, log_total, grad_dot.T)
    query_grad = query_step(
        blank,
        (
            lax.all_gather(key_rows, "seq", axis=0, tiled=True),
            lax.all_gather(value_rows, "seq", axis=0, tiled=True),
        ),
        jnp.int32(0),
    )
    all_log, all_dot = (
        lax.all_gather(log_total.T, "seq", axis=0, tiled=True),
        lax.all_gather(grad_dot, "seq", axis=0, tiled=True),
    )
    key_grad, value_grad = key_fold(
        split_heads(key_rows),
        split_heads(value_rows),
        all_log,
        all_dot,
        (
            lax.all_gather(query_rows, "seq", axis=0, tiled=True),
            lax.all_gather(grad_rows, "seq", axis=0, tiled=True),
        ),
    )
    proj_grad = jnp.concatenate(
        [head_rows(query_grad), head_rows(key_grad), head_rows(value_grad)], axis=1
    ).astype(jnp.bfloat16)
    placed_grad = jnp.einsum(
        "rc,dc->rd", proj_grad, w_qkv, preferred_element_type=jnp.float32
    ).astype(jnp.bfloat16)
    partial_value = jnp.einsum(
        "rd,rc->dc", placed, proj_grad, preferred_element_type=jnp.float32
    ).astype(jnp.bfloat16)
    across = lax.psum_scatter(partial_value, "seq", scatter_dimension=0, tiled=True).astype(
        jnp.float32
    )
    weight_grad = lax.psum_scatter(
        across.astype(jnp.bfloat16), "clip", scatter_dimension=1, tiled=True
    ).astype(jnp.float32)
    back_rows = jnp.einsum(
        "rj,rd->jd", placer, placed_grad, preferred_element_type=jnp.float32
    ).astype(jnp.bfloat16)
    returned = lax.all_to_all(
        back_rows.reshape(shard_count, pair_cap, -1), "seq", split_axis=0, concat_axis=0, tiled=True
    )
    token_grad = jnp.einsum(
        "jt,jd->td",
        chooser_half,
        returned.reshape(shard_count * pair_cap, -1),
        preferred_element_type=jnp.float32,
    ).astype(jnp.bfloat16)
    patch_sums = jnp.einsum(
        "tp,td->pd", member_half, token_grad, preferred_element_type=jnp.float32
    )
    patch_count = jnp.sum(member.astype(jnp.float32) * counts[:, None], axis=0)
    patch_grad = (patch_sums / patch_count[:, None]).astype(jnp.bfloat16)
    return (attended_rows[None], patch_grad[None], weight_grad)


VMEM_LIMIT = 40 * 1024 * 1024
NN = (((1,), (0,)), ((), ()))
NT = (((1,), (1,)), ((), ()))
TN = (((0,), (0,)), ((), ()))


def dot(left, right, dims=NN):
    return lax.dot_general(left, right, dims, preferred_element_type=jnp.float32)


def call(body, outs, *args, scratch=(), space=pltpu.VMEM, limit=VMEM_LIMIT):
    return pl.pallas_call(
        body,
        out_shape=outs,
        in_specs=[pl.BlockSpec(memory_space=space)] * len(args),
        scratch_shapes=scratch,
        compiler_params=pltpu.CompilerParams(vmem_limit_bytes=limit),
    )(*args)


def one_hot(condition):
    return jnp.where(condition, 1.0, 0.0).astype(jnp.bfloat16)


def fold_half(rows):
    half = rows.shape[0] // 2
    return jnp.concatenate([rows[:half], rows[half:]], axis=1)


def unfold_half(rows):
    width = rows.shape[1] // 2
    return jnp.concatenate([rows[:, :width], rows[:, width:]], axis=0)


def wide_row(row):
    short = 256 - row.shape[1]
    wide = row.astype(jnp.float32)
    wide = jnp.concatenate([wide, jnp.full((1, short), -1.0, jnp.float32)], axis=1)
    return wide[:, :128], wide[:, 128:]


def token_kernel(*refs):
    sources, refs = refs[:6], refs[6:]
    sends, refs = refs[:HEADS], refs[HEADS:]
    (target_ref, segment_out, held_ref), refs = refs[:3], refs[3:]
    copies = [
        pltpu.make_async_copy(source, held, refs[6].at[index])
        for index, (source, held) in enumerate(zip(sources, refs))
    ]
    for copy in copies:
        copy.start()
    segment_ref, patch_ref, shard_ref, slot_ref, grad_ref, w_ref = refs[:6]
    token_cap = shard_ref.shape[1]
    local_rows, inner = grad_ref.shape
    devices = len(sends)
    width = patch_ref.shape[1] // devices
    copies[0].wait()
    segment = segment_ref[...]
    segment_out[...] = segment
    member = lax.broadcasted_iota(jnp.int32, (token_cap, segment.shape[1]), 0) == segment
    counts = jnp.sum(jnp.where(member, 1.0, 0.0), axis=1, keepdims=True)
    copies[1].wait()
    token_sums = dot(one_hot(member), patch_ref[...])
    tokens = (token_sums / jnp.maximum(counts, 1.0)).astype(jnp.bfloat16)
    for copy in copies[2:5]:
        copy.wait()
    shard, slot = shard_ref[...], slot_ref[...]
    target_ref[...] = jnp.where(shard >= 0, shard * local_rows + slot, -1)
    shard_low, shard_high = wide_row(shard)
    slot_low, slot_high = wide_row(slot)
    line = lax.broadcasted_iota(jnp.int32, (16, 128), 0)
    where_to = jnp.where(
        line == 0,
        shard_low,
        jnp.where(line == 1, shard_high, jnp.where(line == 2, slot_low, slot_high)),
    ).astype(jnp.bfloat16)
    grads = grad_ref[...]
    copies[5].wait()
    projected = dot(tokens, w_ref[...]).astype(jnp.bfloat16)
    for head in range(devices):
        first = head * HEAD_DIM
        query, key, value = (
            projected[:, part * inner + first : part * inner + first + HEAD_DIM]
            for part in range(3)
        )
        start = 0
        for piece in (
            jnp.concatenate([query, key], axis=1),
            fold_half(value),
            where_to,
            fold_half(grads[:, first : first + HEAD_DIM]),
            tokens[:, head * width : (head + 1) * width],
        ):
            held_ref[head, start : start + piece.shape[0]] = piece
            start += piece.shape[0]
    me = lax.axis_index("seq")
    for flip, send in enumerate(sends):
        send[...] = held_ref[jnp.bitwise_xor(me, flip)]


def target_row(lines, token_cap, local_rows):
    lines = lines.astype(jnp.float32)
    shard = jnp.concatenate([lines[0:1], lines[1:2]], axis=1)[:, :token_cap]
    slot = jnp.concatenate([lines[2:3], lines[3:4]], axis=1)[:, :token_cap]
    return (shard * local_rows + slot).astype(jnp.int32)


def head_kernel(token_cap, *refs):
    pieces, refs = refs[:HEADS], refs[HEADS:]
    outs, (target_ref, grad_ref, attended_ref) = refs[: HEADS // 2], refs[HEADS // 2 :]
    devices, local_rows = len(pieces), grad_ref.shape[1]
    rows = devices * local_rows
    scaling = HEAD_DIM ** (-0.5)
    half_cap = token_cap // 2
    lines_at = token_cap + half_cap
    row_id = lax.broadcasted_iota(jnp.int32, (rows, token_cap), 0)
    total = jnp.zeros((rows, 3 * HEAD_DIM), jnp.float32)
    me = lax.axis_index("seq")
    for flip, piece in enumerate(pieces):
        sender = jnp.bitwise_xor(me, flip)
        target = target_row(piece[lines_at : lines_at + 16], token_cap, local_rows)
        target_ref[sender] = target
        rows_in = jnp.concatenate(
            [piece[:token_cap], unfold_half(piece[token_cap:lines_at])], axis=1
        )
        total = total + dot(one_hot(row_id == target), rows_in)
        grad_ref[sender] = unfold_half(piece[lines_at + 16 : lines_at + 16 + local_rows // 2])
    projected = total.astype(jnp.bfloat16)
    query = projected[:, :HEAD_DIM]
    key = projected[:, HEAD_DIM : 2 * HEAD_DIM]
    value = projected[:, 2 * HEAD_DIM :]
    grad = jnp.concatenate([grad_ref[place] for place in range(devices)], axis=0)
    scores = dot(key, query, NT) * scaling
    weights = jnp.exp(scores - jnp.max(scores, axis=0, keepdims=True))
    row_total = jnp.sum(weights, axis=0, keepdims=True)
    attended = (dot(value, weights.astype(jnp.bfloat16), TN) / row_total).astype(jnp.bfloat16)
    attended = attended.astype(jnp.float32)
    grad_dot = jnp.sum(grad.astype(jnp.float32).T * attended, axis=0, keepdims=True)
    probability = weights * (1.0 / row_total)
    score_grad = (probability * (dot(value, grad, NT) - grad_dot)).astype(jnp.bfloat16)
    value_grad = dot(probability.astype(jnp.bfloat16), grad)
    key_grad = dot(score_grad, query) * scaling
    query_grad = (dot(key, score_grad, TN) * scaling).T
    attended = attended.T.astype(jnp.bfloat16)
    for place in range(devices):
        attended_ref[place] = fold_half(attended[place * local_rows : (place + 1) * local_rows])
    proj_grad = jnp.concatenate([query_grad, key_grad], axis=1).astype(jnp.bfloat16)
    value_grad = fold_half(value_grad.astype(jnp.bfloat16))
    end = rows + rows // 2
    for chip, out in enumerate(outs):
        out[:rows] = proj_grad
        out[rows:end] = value_grad
        for core in range(2):
            first = end + core * local_rows // 2
            place = jnp.bitwise_xor(me, 2 * chip + core)
            out[first : first + local_rows // 2] = attended_ref[place]


def block_kernel(target_ref, *refs):
    pieces, placed_ref = refs[:-1], refs[-1]
    token_cap = target_ref.shape[2]
    width, rows = placed_ref.shape
    row_id = lax.broadcasted_iota(jnp.int32, (rows, token_cap), 0)
    total = jnp.zeros((rows, width), jnp.float32)
    me = lax.axis_index("seq")
    for flip, piece in enumerate(pieces):
        target = target_ref[jnp.bitwise_xor(me, flip)]
        total = total + dot(one_hot(row_id == target), piece[piece.shape[0] - token_cap :])
    placed_ref[...] = total.T.astype(jnp.bfloat16)


def by_column(left, pieces, held_ref):
    rows = left.shape[1]
    half, end = rows // 2, rows + rows // 2
    me = lax.axis_index("seq")
    for flip, piece in enumerate(pieces):
        both = dot(left, piece[:rows])
        low = dot(left[:, :half], piece[rows:end])
        high = dot(left[:, half:], piece[rows:end])
        value = low[:, :HEAD_DIM] + high[:, HEAD_DIM:]
        held_ref[jnp.bitwise_xor(me, flip)] = jnp.concatenate([both, value], axis=1)
    return jnp.concatenate(
        [
            held_ref[head, :, part * HEAD_DIM : (part + 1) * HEAD_DIM]
            for part in range(3)
            for head in range(len(pieces))
        ],
        axis=1,
    )


def weight_kernel(placed_ref, *refs):
    pieces, outs, (held_ref, block_ref) = refs[:HEADS], refs[HEADS:-2], refs[-2:]
    columns = by_column(placed_ref[...], pieces, held_ref).astype(jnp.bfloat16)
    width = columns.shape[1] // len(outs)
    me = lax.axis_index("clip")
    for index in range(len(outs)):
        block_ref[index] = columns[:, index * width : (index + 1) * width]
    for flip, out in enumerate(outs):
        out[...] = block_ref[jnp.bitwise_xor(me, flip)]


def patch_kernel(segment_ref, target_ref, w_ref, *refs):
    pieces, (patch_ref, attended_ref, held_ref, part_ref) = refs[:HEADS], refs[HEADS:]
    token_cap = target_ref.shape[1]
    local_rows = attended_ref.shape[0]
    rows = HEADS * local_rows
    me = lax.axis_index("seq")
    for flip, piece in enumerate(pieces):
        first = rows + rows // 2 + flip % 2 * local_rows // 2
        part_ref[jnp.bitwise_xor(me, flip)] = unfold_half(piece[first : first + local_rows // 2])
    attended_ref[...] = jnp.concatenate([part_ref[head] for head in range(HEADS)], axis=1)
    row_id = lax.broadcasted_iota(jnp.int32, (rows, token_cap), 0)
    chooser = jnp.where(row_id == target_ref[...], 1.0, 0.0).T.astype(jnp.bfloat16)
    proj_grad = by_column(chooser, pieces, held_ref).astype(jnp.bfloat16)
    token_grad = dot(proj_grad, w_ref[...], NT).astype(jnp.bfloat16).astype(jnp.float32)
    member = (
        lax.broadcasted_iota(jnp.int32, (token_cap, segment_ref.shape[1]), 0) == segment_ref[...]
    )
    counts = jnp.sum(jnp.where(member, 1.0, 0.0), axis=1, keepdims=True)
    shared = (token_grad / jnp.maximum(counts, 1.0)).astype(jnp.bfloat16)
    patch_ref[...] = dot(one_hot(member), shared, TN).astype(jnp.bfloat16)


def sum_kernel(*refs):
    total = refs[0][...].astype(jnp.float32)
    for ref in refs[1:-1]:
        total = total + ref[...].astype(jnp.float32)
    refs[-1][...] = total


def exchange(rows, axis, flip):
    count = lax.axis_size(axis)
    return lax.ppermute(rows, axis, [(index, index ^ flip) for index in range(count)])


def shape(*sizes, dtype=jnp.bfloat16):
    return jax.ShapeDtypeStruct(sizes, dtype)


def heads_plan(patches, segment, dest_shard, dest_slot, w_qkv, out_grad):
    devices = lax.axis_size("seq")
    clips = lax.axis_size("clip")
    token_cap = dest_shard.shape[1]
    local_rows, inner = out_grad.shape[1:]
    rows = devices * local_rows
    model = patches.shape[2]
    width = model // devices
    sent = token_cap + token_cap // 2 + 16 + local_rows // 2 + token_cap
    sources = (segment, patches[0], dest_shard, dest_slot, out_grad[0], w_qkv)
    outs = call(
        token_kernel,
        [shape(sent, 2 * HEAD_DIM)] * devices
        + [shape(1, token_cap, dtype=jnp.int32), shape(*segment.shape, dtype=jnp.int32)],
        *sources,
        scratch=[
            pltpu.VMEM((devices, sent, 2 * HEAD_DIM), jnp.bfloat16),
        ]
        + [pltpu.VMEM(source.shape, source.dtype) for source in sources]
        + [pltpu.SemaphoreType.DMA((len(sources),))],
        space=pltpu.HBM,
        limit=60 * 1024 * 1024,
    )
    sends, (target, segment) = outs[:devices], outs[devices:]
    far_first = sorted(range(1, devices), key=lambda flip: (-(flip // 2).bit_count(), flip))
    came = [sends[0]] + [None] * (devices - 1)
    for flip in far_first:
        came[flip] = exchange(sends[flip], "seq", flip)
    *proj, targets = call(
        lambda *refs: head_kernel(token_cap, *refs),
        [shape(rows + rows // 2 + local_rows, 2 * HEAD_DIM)] * (devices // 2)
        + [shape(devices, 1, token_cap, dtype=jnp.int32)],
        *came,
        scratch=[
            pltpu.VMEM((devices, local_rows, HEAD_DIM), jnp.bfloat16),
            pltpu.VMEM((devices, local_rows // 2, 2 * HEAD_DIM), jnp.bfloat16),
        ],
    )
    pieces = [proj[0]] + [None] * (devices - 1)
    for flip in far_first:
        if flip % 2 == 0:
            pieces[flip] = exchange(proj[flip // 2], "seq", flip)
    for flip in range(1, devices, 2):
        pieces[flip] = exchange(pieces[flip - 1], "seq", 1)
    placed = call(block_kernel, shape(width, rows), targets, *came)
    weights = call(
        weight_kernel,
        [shape(width, 3 * inner // clips)] * clips,
        placed,
        *pieces,
        scratch=[
            pltpu.VMEM((devices, width, 3 * HEAD_DIM), jnp.float32),
            pltpu.VMEM((clips, width, 3 * inner // clips), jnp.bfloat16),
        ],
    )
    weights = [weights[0]] + [exchange(weights[flip], "clip", flip) for flip in range(1, clips)]
    patch_grad, attended = call(
        patch_kernel,
        [shape(patches.shape[1], model), shape(local_rows, inner)],
        segment,
        target,
        w_qkv,
        *pieces,
        scratch=[
            pltpu.VMEM((devices, token_cap, 3 * HEAD_DIM), jnp.float32),
            pltpu.VMEM((devices, local_rows, HEAD_DIM), jnp.bfloat16),
        ],
    )
    weight_grad = call(
        sum_kernel, shape(width, 3 * inner // clips, dtype=jnp.float32), *weights
    )
    return attended[None], patch_grad[None], weight_grad


def solution(mesh):
    devices, clips = mesh.shape["seq"], mesh.shape["clip"]
    one_head_each = devices == HEADS and clips in (1, 2, 4, 8)
    return jax.shard_map(
        heads_plan if one_head_each else rows_plan,
        mesh=mesh,
        in_specs=(
            P("clip", "seq", None),
            P("clip", "seq"),
            P("clip", "seq"),
            P("clip", "seq"),
            P(),
            P("clip", "seq", None),
        ),
        out_specs=(P("clip", "seq", None), P("clip", "seq", None), P("seq", "clip")),
        check_vma=False,
    )
```

```python
import functools

import jax
import jax.numpy as jnp
from jax import lax
from jax.experimental import pallas as pl
from jax.experimental.pallas import tpu as pltpu
from jax.sharding import PartitionSpec as P

HEADS = 8
HEAD_DIM = 64


neg_large = -1e30


def split_heads(rows_in):
    return rows_in.reshape(rows_in.shape[0], HEADS, HEAD_DIM)


def forward_fold(query_heads, running, pieces):
    scaling = HEAD_DIM ** (-0.5)
    row_max, row_total, weighted = running
    key_heads = split_heads(pieces[0])
    value_heads = split_heads(pieces[1])
    scores = (
        jnp.einsum("rhd,khd->hrk", query_heads, key_heads, preferred_element_type=jnp.float32)
        * scaling
    )
    new_max = jnp.maximum(row_max, jnp.max(scores, axis=2))
    weights = jnp.exp(scores - new_max[:, :, None])
    row_total = jnp.sum(weights, axis=2)
    weighted = jnp.einsum(
        "hrk,khd->hrd",
        weights.astype(jnp.bfloat16),
        value_heads,
        preferred_element_type=jnp.float32,
    )
    return (new_max, row_total, weighted)


def query_fold(query_heads, grad_heads, log_total, grad_dot):
    scaling = HEAD_DIM ** (-0.5)

    def combine_piece(running, pieces, offset):
        key_heads = split_heads(pieces[0])
        value_heads = split_heads(pieces[1])
        scores = (
            jnp.einsum("rhd,khd->hrk", query_heads, key_heads, preferred_element_type=jnp.float32)
            * scaling
        )
        probability = jnp.exp(scores - log_total[:, :, None])
        prob_grad = jnp.einsum(
            "rhd,khd->hrk", grad_heads, value_heads, preferred_element_type=jnp.float32
        )
        score_grad = (probability * (prob_grad - grad_dot[:, :, None])).astype(jnp.bfloat16)
        return (
            jnp.einsum("hrk,khd->hrd", score_grad, key_heads, preferred_element_type=jnp.float32)
            * scaling
        )

    return combine_piece


def key_fold(key_heads, value_heads, all_log, all_dot, pieces):
    scaling = HEAD_DIM ** (-0.5)
    piece_query = split_heads(pieces[0])
    piece_grad = split_heads(pieces[1])
    piece_log = all_log.T
    piece_dot = all_dot.T
    scores = (
        jnp.einsum("qhd,khd->hqk", piece_query, key_heads, preferred_element_type=jnp.float32)
        * scaling
    )
    probability = jnp.exp(scores - piece_log[:, :, None])
    value_grad = jnp.einsum(
        "hqk,qhd->hkd",
        probability.astype(jnp.bfloat16),
        piece_grad,
        preferred_element_type=jnp.float32,
    )
    prob_grad = jnp.einsum(
        "qhd,khd->hqk", piece_grad, value_heads, preferred_element_type=jnp.float32
    )
    score_grad = (probability * (prob_grad - piece_dot[:, :, None])).astype(jnp.bfloat16)
    key_grad = (
        jnp.einsum("hqk,qhd->hkd", score_grad, piece_query, preferred_element_type=jnp.float32)
        * scaling
    )
    return (key_grad, value_grad)


def head_rows(matrix):
    return matrix.transpose(1, 0, 2).reshape(matrix.shape[1], HEADS * HEAD_DIM)


def rows_plan(patches, segment, dest_shard, dest_slot, w_qkv, out_grad):
    shard_count = lax.axis_size("seq")
    patch_rows = patches[0]
    patch_token = segment[0]
    targets = dest_shard[0]
    slot_ids = dest_slot[0]
    token_cap = targets.shape[0]
    pair_cap = token_cap // shard_count
    local_rows = out_grad.shape[1]
    inner_width = HEADS * HEAD_DIM
    member = (
        lax.broadcasted_iota(jnp.int32, (token_cap, patch_token.shape[0]), 0)
        == patch_token[None, :]
    )
    member_half = member.astype(jnp.bfloat16)
    counts = jnp.sum(member.astype(jnp.float32), axis=1)
    token_sums = jnp.dot(member_half, patch_rows, preferred_element_type=jnp.float32)
    tokens = (token_sums / jnp.maximum(counts, 1.0)[:, None]).astype(jnp.bfloat16)
    to_shard = (
        targets[:, None] == lax.broadcasted_iota(jnp.int32, (token_cap, shard_count), 1)
    ).astype(jnp.int32)
    ranking = jnp.sum((jnp.cumsum(to_shard, axis=0) - 1) * to_shard, axis=1)
    position = jnp.where(targets >= 0, targets * pair_cap + ranking, -1)
    chooser = position[None, :] == lax.broadcasted_iota(
        jnp.int32, (shard_count * pair_cap, token_cap), 0
    )
    chooser_half = chooser.astype(jnp.bfloat16)
    send_rows = jnp.dot(chooser_half, tokens, preferred_element_type=jnp.float32).astype(
        jnp.bfloat16
    )
    send_slot = jnp.sum(chooser.astype(jnp.int32) * (slot_ids + 1)[None, :], axis=1) - 1
    came_rows, came_slot = (
        lax.all_to_all(
            send_rows.reshape(shard_count, pair_cap, -1),
            "seq",
            split_axis=0,
            concat_axis=0,
            tiled=True,
        ),
        lax.all_to_all(
            send_slot.reshape(shard_count, pair_cap), "seq", split_axis=0, concat_axis=0, tiled=True
        ),
    )
    came_slot = came_slot.reshape(-1)
    placer = (
        came_slot[None, :]
        == lax.broadcasted_iota(jnp.int32, (local_rows, shard_count * pair_cap), 0)
    ).astype(jnp.bfloat16)
    placed = jnp.dot(
        placer, came_rows.reshape(shard_count * pair_cap, -1), preferred_element_type=jnp.float32
    ).astype(jnp.bfloat16)
    projected = jnp.dot(placed, w_qkv, preferred_element_type=jnp.float32).astype(jnp.bfloat16)
    query_rows = projected[:, :inner_width]
    key_rows = projected[:, inner_width : 2 * inner_width]
    value_rows = projected[:, 2 * inner_width :]
    query_heads = split_heads(query_rows)
    initial = (
        jnp.full((HEADS, local_rows), neg_large, jnp.float32),
        jnp.zeros((HEADS, local_rows), jnp.float32),
        jnp.zeros((HEADS, local_rows, HEAD_DIM), jnp.float32),
    )
    row_max, row_total, weighted = forward_fold(
        query_heads,
        initial,
        (
            lax.all_gather(key_rows, "seq", axis=0, tiled=True),
            lax.all_gather(value_rows, "seq", axis=0, tiled=True),
        ),
    )
    attended_rows = head_rows((weighted / row_total[:, :, None]).astype(jnp.bfloat16))
    grad_rows = out_grad[0]
    grad_heads = split_heads(grad_rows)
    log_total = row_max + jnp.log(row_total)
    grad_dot = jnp.sum(
        grad_heads.astype(jnp.float32) * split_heads(attended_rows).astype(jnp.float32), axis=2
    )
    blank = jnp.zeros((HEADS, local_rows, HEAD_DIM), jnp.float32)
    query_step = query_fold(query_heads, grad_heads, log_total, grad_dot.T)
    query_grad = query_step(
        blank,
        (
            lax.all_gather(key_rows, "seq", axis=0, tiled=True),
            lax.all_gather(value_rows, "seq", axis=0, tiled=True),
        ),
        jnp.int32(0),
    )
    all_log, all_dot = (
        lax.all_gather(log_total.T, "seq", axis=0, tiled=True),
        lax.all_gather(grad_dot, "seq", axis=0, tiled=True),
    )
    key_grad, value_grad = key_fold(
        split_heads(key_rows),
        split_heads(value_rows),
        all_log,
        all_dot,
        (
            lax.all_gather(query_rows, "seq", axis=0, tiled=True),
            lax.all_gather(grad_rows, "seq", axis=0, tiled=True),
        ),
    )
    proj_grad = jnp.concatenate(
        [head_rows(query_grad), head_rows(key_grad), head_rows(value_grad)], axis=1
    ).astype(jnp.bfloat16)
    placed_grad = jnp.einsum(
        "rc,dc->rd", proj_grad, w_qkv, preferred_element_type=jnp.float32
    ).astype(jnp.bfloat16)
    partial_value = jnp.einsum(
        "rd,rc->dc", placed, proj_grad, preferred_element_type=jnp.float32
    ).astype(jnp.bfloat16)
    across = lax.psum_scatter(partial_value, "seq", scatter_dimension=0, tiled=True).astype(
        jnp.float32
    )
    weight_grad = lax.psum_scatter(
        across.astype(jnp.bfloat16), "clip", scatter_dimension=1, tiled=True
    ).astype(jnp.float32)
    back_rows = jnp.einsum(
        "rj,rd->jd", placer, placed_grad, preferred_element_type=jnp.float32
    ).astype(jnp.bfloat16)
    returned = lax.all_to_all(
        back_rows.reshape(shard_count, pair_cap, -1), "seq", split_axis=0, concat_axis=0, tiled=True
    )
    token_grad = jnp.einsum(
        "jt,jd->td",
        chooser_half,
        returned.reshape(shard_count * pair_cap, -1),
        preferred_element_type=jnp.float32,
    ).astype(jnp.bfloat16)
    patch_sums = jnp.einsum(
        "tp,td->pd", member_half, token_grad, preferred_element_type=jnp.float32
    )
    patch_count = jnp.sum(member.astype(jnp.float32) * counts[:, None], axis=0)
    patch_grad = (patch_sums / patch_count[:, None]).astype(jnp.bfloat16)
    return (attended_rows[None], patch_grad[None], weight_grad)


VMEM_LIMIT = 40 * 1024 * 1024
NN = (((1,), (0,)), ((), ()))
NT = (((1,), (1,)), ((), ()))
TN = (((0,), (0,)), ((), ()))


def dot(left, right, dims=NN):
    return lax.dot_general(left, right, dims, preferred_element_type=jnp.float32)


def call(body, outs, *args, scratch=(), space=None, limit=VMEM_LIMIT):
    space = space or [pltpu.VMEM] * len(args)
    return pl.pallas_call(
        body,
        out_shape=outs,
        in_specs=[pl.BlockSpec(memory_space=each) for each in space],
        scratch_shapes=scratch,
        compiler_params=pltpu.CompilerParams(vmem_limit_bytes=limit),
    )(*args)


def one_hot(condition):
    return jnp.where(condition, 1.0, 0.0).astype(jnp.bfloat16)


def fold_half(rows):
    half = rows.shape[0] // 2
    return jnp.concatenate([rows[:half], rows[half:]], axis=1)


def unfold_half(rows):
    width = rows.shape[1] // 2
    return jnp.concatenate([rows[:, :width], rows[:, width:]], axis=0)


def wide_row(row):
    short = 256 - row.shape[1]
    wide = row.astype(jnp.float32)
    wide = jnp.concatenate([wide, jnp.full((1, short), -1.0, jnp.float32)], axis=1)
    return wide[:, :128], wide[:, 128:]


def token_kernel(*refs):
    sources, refs = refs[:6], refs[6:]
    sends, refs = refs[:HEADS], refs[HEADS:]
    (target_ref, segment_out, held_ref), refs = refs[:3], refs[3:]
    segment_ref, patch_ref, shard_ref, slot_ref, grad_ref, w_ref, done = refs
    pairs = list(zip(sources, refs))[:-1]
    for part in range(3):
        columns = pl.ds(part * grad_ref.shape[1], grad_ref.shape[1])
        pairs.append((sources[5].at[:, columns], w_ref.at[part]))
    copies = [
        pltpu.make_async_copy(source, held, done.at[index])
        for index, (source, held) in enumerate(pairs)
    ]
    for copy in copies:
        copy.start()
    token_cap = shard_ref.shape[1]
    local_rows, inner = grad_ref.shape
    devices = len(sends)
    width = patch_ref.shape[1] // devices
    copies[0].wait()
    segment = segment_ref[...]
    segment_out[...] = segment
    member = lax.broadcasted_iota(jnp.int32, (token_cap, segment.shape[1]), 0) == segment
    counts = jnp.sum(jnp.where(member, 1.0, 0.0), axis=1, keepdims=True)
    copies[1].wait()
    token_sums = dot(one_hot(member), patch_ref[...])
    tokens = (token_sums / jnp.maximum(counts, 1.0)).astype(jnp.bfloat16)
    for copy in copies[2:5]:
        copy.wait()
    shard, slot = shard_ref[...], slot_ref[...]
    target_ref[...] = jnp.where(shard >= 0, shard * local_rows + slot, -1)
    shard_low, shard_high = wide_row(shard)
    slot_low, slot_high = wide_row(slot)
    line = lax.broadcasted_iota(jnp.int32, (16, 128), 0)
    where_to = jnp.where(
        line == 0,
        shard_low,
        jnp.where(line == 1, shard_high, jnp.where(line == 2, slot_low, slot_high)),
    ).astype(jnp.bfloat16)
    grads = grad_ref[...]
    half = token_cap + token_cap // 2
    for head in range(devices):
        first = head * HEAD_DIM
        start = half
        for piece in (
            where_to,
            fold_half(grads[:, first : first + HEAD_DIM]),
            tokens[:, head * width : (head + 1) * width],
        ):
            held_ref[head, start : start + piece.shape[0]] = piece
            start += piece.shape[0]
    for part, copy in enumerate(copies[5:]):
        copy.wait()
        projected = dot(tokens, w_ref[part]).astype(jnp.bfloat16)
        for head in range(devices):
            rows = projected[:, head * HEAD_DIM : (head + 1) * HEAD_DIM]
            if part < 2:
                held_ref[head, :token_cap, part * HEAD_DIM : (part + 1) * HEAD_DIM] = rows
            else:
                held_ref[head, token_cap:half] = fold_half(rows)
    me = lax.axis_index("seq")
    for flip, send in enumerate(sends):
        send[...] = held_ref[jnp.bitwise_xor(me, flip)]


def target_row(lines, token_cap, local_rows):
    lines = lines.astype(jnp.float32)
    shard = jnp.concatenate([lines[0:1], lines[1:2]], axis=1)[:, :token_cap]
    slot = jnp.concatenate([lines[2:3], lines[3:4]], axis=1)[:, :token_cap]
    return (shard * local_rows + slot).astype(jnp.int32)


def head_kernel(token_cap, flips, *refs):
    pieces, refs = refs[:HEADS], refs[HEADS:]
    outs, (target_ref, grad_ref, attended_ref) = refs[: HEADS // 2], refs[HEADS // 2 :]
    devices, local_rows = len(pieces), grad_ref.shape[1]
    rows = devices * local_rows
    scaling = HEAD_DIM ** (-0.5)
    half_cap = token_cap // 2
    lines_at = token_cap + half_cap
    row_id = lax.broadcasted_iota(jnp.int32, (rows, token_cap), 0)
    total = jnp.zeros((rows, 3 * HEAD_DIM), jnp.float32)
    me = lax.axis_index("seq")
    for flip, piece in zip(flips, pieces):
        sender = jnp.bitwise_xor(me, flip)
        target = target_row(piece[lines_at : lines_at + 16], token_cap, local_rows)
        target_ref[sender] = target
        rows_in = jnp.concatenate(
            [piece[:token_cap], unfold_half(piece[token_cap:lines_at])], axis=1
        )
        total = total + dot(one_hot(row_id == target), rows_in)
        grad_ref[sender] = unfold_half(piece[lines_at + 16 : lines_at + 16 + local_rows // 2])
    projected = total.astype(jnp.bfloat16)
    query = projected[:, :HEAD_DIM]
    key = projected[:, HEAD_DIM : 2 * HEAD_DIM]
    value = projected[:, 2 * HEAD_DIM :]
    grad = jnp.concatenate([grad_ref[place] for place in range(devices)], axis=0)
    scores = dot(key, query, NT) * scaling
    weights = jnp.exp(scores - jnp.max(scores, axis=0, keepdims=True))
    row_total = jnp.sum(weights, axis=0, keepdims=True)
    attended = (dot(value, weights.astype(jnp.bfloat16), TN) / row_total).astype(jnp.bfloat16)
    attended = attended.astype(jnp.float32)
    grad_dot = jnp.sum(grad.astype(jnp.float32).T * attended, axis=0, keepdims=True)
    probability = weights * (1.0 / row_total)
    score_grad = (probability * (dot(value, grad, NT) - grad_dot)).astype(jnp.bfloat16)
    value_grad = dot(probability.astype(jnp.bfloat16), grad)
    key_grad = dot(score_grad, query) * scaling
    query_grad = (dot(key, score_grad, TN) * scaling).T
    attended = attended.T.astype(jnp.bfloat16)
    for place in range(devices):
        attended_ref[place] = fold_half(attended[place * local_rows : (place + 1) * local_rows])
    proj_grad = jnp.concatenate([query_grad, key_grad], axis=1).astype(jnp.bfloat16)
    value_grad = fold_half(value_grad.astype(jnp.bfloat16))
    end = rows + rows // 2
    for chip, out in enumerate(outs):
        out[:rows] = proj_grad
        out[rows:end] = value_grad
        for core in range(2):
            first = end + core * local_rows // 2
            place = jnp.bitwise_xor(me, 2 * chip + core)
            out[first : first + local_rows // 2] = attended_ref[place]


def block_kernel(flips, target_ref, *refs):
    pieces, placed_ref = refs[:-1], refs[-1]
    token_cap = target_ref.shape[2]
    width, rows = placed_ref.shape
    row_id = lax.broadcasted_iota(jnp.int32, (rows, token_cap), 0)
    total = jnp.zeros((rows, width), jnp.float32)
    me = lax.axis_index("seq")
    for flip, piece in zip(flips, pieces):
        target = target_ref[jnp.bitwise_xor(me, flip)]
        total = total + dot(one_hot(row_id == target), piece[piece.shape[0] - token_cap :])
    placed_ref[...] = total.T.astype(jnp.bfloat16)


def by_column(left, flips, pieces, held_ref):
    rows = left.shape[1]
    half, end = rows // 2, rows + rows // 2
    me = lax.axis_index("seq")
    for flip, piece in zip(flips, pieces):
        both = dot(left, piece[:rows])
        low = dot(left[:, :half], piece[rows:end])
        high = dot(left[:, half:], piece[rows:end])
        value = low[:, :HEAD_DIM] + high[:, HEAD_DIM:]
        held_ref[jnp.bitwise_xor(me, flip)] = jnp.concatenate([both, value], axis=1)
    return jnp.concatenate(
        [
            held_ref[head, :, part * HEAD_DIM : (part + 1) * HEAD_DIM]
            for part in range(3)
            for head in range(len(pieces))
        ],
        axis=1,
    )


def weight_kernel(flips, placed_ref, *refs):
    pieces, outs, (held_ref, block_ref) = refs[:HEADS], refs[HEADS:-2], refs[-2:]
    columns = by_column(placed_ref[...], flips, pieces, held_ref).astype(jnp.bfloat16)
    width = columns.shape[1] // len(outs)
    me = lax.axis_index("clip")
    for index in range(len(outs)):
        block_ref[index] = columns[:, index * width : (index + 1) * width]
    for flip, out in enumerate(outs):
        out[...] = block_ref[jnp.bitwise_xor(me, flip)]


def patch_kernel(flips, segment_ref, target_ref, w_hbm, *refs):
    pieces, (patch_ref, attended_ref, held_ref, part_ref, w_ref, done) = refs[:HEADS], refs[HEADS:]
    copy = pltpu.make_async_copy(w_hbm, w_ref, done)
    copy.start()
    token_cap = target_ref.shape[1]
    local_rows = attended_ref.shape[0]
    rows = HEADS * local_rows
    me = lax.axis_index("seq")
    for flip, piece in zip(flips, pieces):
        first = rows + rows // 2 + flip % 2 * local_rows // 2
        part_ref[jnp.bitwise_xor(me, flip)] = unfold_half(piece[first : first + local_rows // 2])
    attended_ref[...] = jnp.concatenate([part_ref[head] for head in range(HEADS)], axis=1)
    row_id = lax.broadcasted_iota(jnp.int32, (rows, token_cap), 0)
    chooser = jnp.where(row_id == target_ref[...], 1.0, 0.0).T.astype(jnp.bfloat16)
    proj_grad = by_column(chooser, flips, pieces, held_ref).astype(jnp.bfloat16)
    copy.wait()
    token_grad = dot(proj_grad, w_ref[...], NT).astype(jnp.bfloat16).astype(jnp.float32)
    member = (
        lax.broadcasted_iota(jnp.int32, (token_cap, segment_ref.shape[1]), 0) == segment_ref[...]
    )
    counts = jnp.sum(jnp.where(member, 1.0, 0.0), axis=1, keepdims=True)
    shared = (token_grad / jnp.maximum(counts, 1.0)).astype(jnp.bfloat16)
    patch_ref[...] = dot(one_hot(member), shared, TN).astype(jnp.bfloat16)


def copy_kernel(source_ref, target_ref):
    target_ref[...] = source_ref[...]


def sum_kernel(*refs):
    total = refs[0][...].astype(jnp.float32)
    for ref in refs[1:-1]:
        total = total + ref[...].astype(jnp.float32)
    refs[-1][...] = total


def exchange(rows, axis, flip):
    count = lax.axis_size(axis)
    return lax.ppermute(rows, axis, [(index, index ^ flip) for index in range(count)])


def shape(*sizes, dtype=jnp.bfloat16):
    return jax.ShapeDtypeStruct(sizes, dtype)


def heads_plan(patches, segment, dest_shard, dest_slot, w_qkv, out_grad):
    devices = lax.axis_size("seq")
    clips = lax.axis_size("clip")
    token_cap = dest_shard.shape[1]
    local_rows, inner = out_grad.shape[1:]
    rows = devices * local_rows
    model = patches.shape[2]
    width = model // devices
    sent = token_cap + token_cap // 2 + 16 + local_rows // 2 + token_cap
    sources = (segment, patches[0], dest_shard, dest_slot, out_grad[0], w_qkv)
    outs = call(
        token_kernel,
        [shape(sent, 2 * HEAD_DIM)] * devices
        + [shape(1, token_cap, dtype=jnp.int32), shape(*segment.shape, dtype=jnp.int32)],
        *sources,
        scratch=[
            pltpu.VMEM((devices, sent, 2 * HEAD_DIM), jnp.bfloat16),
        ]
        + [pltpu.VMEM(source.shape, source.dtype) for source in sources[:-1]]
        + [
            pltpu.VMEM((3, model, inner), w_qkv.dtype),
            pltpu.SemaphoreType.DMA((len(sources) + 2,)),
        ],
        space=[pltpu.HBM] * len(sources),
        limit=62 * 1024 * 1024,
    )
    sends, (target, segment) = list(outs[:devices]), outs[devices:]
    order = [0] + sorted(range(1, devices), key=lambda flip: (-(flip // 2).bit_count(), flip))
    sends[0] = call(copy_kernel, shape(sent, 2 * HEAD_DIM), sends[0])
    came = {0: sends[0]}
    for flip in order[1:]:
        came[flip] = exchange(sends[flip], "seq", flip)
    came = [came[flip] for flip in order]
    *proj, targets = call(
        functools.partial(head_kernel, token_cap, order),
        [shape(rows + rows // 2 + local_rows, 2 * HEAD_DIM)] * (devices // 2)
        + [shape(devices, 1, token_cap, dtype=jnp.int32)],
        *came,
        scratch=[
            pltpu.VMEM((devices, local_rows, HEAD_DIM), jnp.bfloat16),
            pltpu.VMEM((devices, local_rows // 2, 2 * HEAD_DIM), jnp.bfloat16),
        ],
    )
    pieces = {0: proj[0]}
    for flip in order[1:]:
        if flip % 2 == 0:
            pieces[flip] = exchange(proj[flip // 2], "seq", flip)
    for flip in list(pieces):
        pieces[flip + 1] = exchange(pieces[flip], "seq", 1)
    flips = order
    pieces = [pieces[flip] for flip in flips]
    placed = call(
        functools.partial(block_kernel, order), shape(width, rows), targets, *came
    )
    weights = call(
        functools.partial(weight_kernel, flips),
        [shape(width, 3 * inner // clips)] * clips,
        placed,
        *pieces,
        scratch=[
            pltpu.VMEM((devices, width, 3 * HEAD_DIM), jnp.float32),
            pltpu.VMEM((clips, width, 3 * inner // clips), jnp.bfloat16),
        ],
    )
    weights = [weights[0]] + [exchange(weights[flip], "clip", flip) for flip in range(clips - 1, 0, -1)]
    patch_grad, attended = call(
        functools.partial(patch_kernel, flips),
        [shape(patches.shape[1], model), shape(local_rows, inner)],
        segment,
        target,
        w_qkv,
        *pieces,
        scratch=[
            pltpu.VMEM((devices, token_cap, 3 * HEAD_DIM), jnp.float32),
            pltpu.VMEM((devices, local_rows, HEAD_DIM), jnp.bfloat16),
            pltpu.VMEM(w_qkv.shape, w_qkv.dtype),
            pltpu.SemaphoreType.DMA(()),
        ],
        space=[pltpu.VMEM] * 2 + [pltpu.HBM] + [pltpu.VMEM] * devices,
    )
    weight_grad = call(
        sum_kernel, shape(width, 3 * inner // clips, dtype=jnp.float32), *weights
    )
    return attended[None], patch_grad[None], weight_grad


def solution(mesh):
    devices, clips = mesh.shape["seq"], mesh.shape["clip"]
    one_head_each = devices == HEADS and clips in (1, 2, 4, 8)
    return jax.shard_map(
        heads_plan if one_head_each else rows_plan,
        mesh=mesh,
        in_specs=(
            P("clip", "seq", None),
            P("clip", "seq"),
            P("clip", "seq"),
            P("clip", "seq"),
            P(),
            P("clip", "seq", None),
        ),
        out_specs=(P("clip", "seq", None), P("clip", "seq", None), P("seq", "clip")),
        check_vma=False,
    )
```

```python
import functools

import jax
import jax.numpy as jnp
from jax import lax
from jax.experimental import pallas as pl
from jax.experimental.pallas import tpu as pltpu
from jax.sharding import PartitionSpec as P

HEADS = 8
HEAD_DIM = 64


neg_large = -1e30


def split_heads(rows_in):
    return rows_in.reshape(rows_in.shape[0], HEADS, HEAD_DIM)


def forward_fold(query_heads, running, pieces):
    scaling = HEAD_DIM ** (-0.5)
    row_max, row_total, weighted = running
    key_heads = split_heads(pieces[0])
    value_heads = split_heads(pieces[1])
    scores = (
        jnp.einsum("rhd,khd->hrk", query_heads, key_heads, preferred_element_type=jnp.float32)
        * scaling
    )
    new_max = jnp.maximum(row_max, jnp.max(scores, axis=2))
    weights = jnp.exp(scores - new_max[:, :, None])
    row_total = jnp.sum(weights, axis=2)
    weighted = jnp.einsum(
        "hrk,khd->hrd",
        weights.astype(jnp.bfloat16),
        value_heads,
        preferred_element_type=jnp.float32,
    )
    return (new_max, row_total, weighted)


def query_fold(query_heads, grad_heads, log_total, grad_dot):
    scaling = HEAD_DIM ** (-0.5)

    def combine_piece(running, pieces, offset):
        key_heads = split_heads(pieces[0])
        value_heads = split_heads(pieces[1])
        scores = (
            jnp.einsum("rhd,khd->hrk", query_heads, key_heads, preferred_element_type=jnp.float32)
            * scaling
        )
        probability = jnp.exp(scores - log_total[:, :, None])
        prob_grad = jnp.einsum(
            "rhd,khd->hrk", grad_heads, value_heads, preferred_element_type=jnp.float32
        )
        score_grad = (probability * (prob_grad - grad_dot[:, :, None])).astype(jnp.bfloat16)
        return (
            jnp.einsum("hrk,khd->hrd", score_grad, key_heads, preferred_element_type=jnp.float32)
            * scaling
        )

    return combine_piece


def key_fold(key_heads, value_heads, all_log, all_dot, pieces):
    scaling = HEAD_DIM ** (-0.5)
    piece_query = split_heads(pieces[0])
    piece_grad = split_heads(pieces[1])
    piece_log = all_log.T
    piece_dot = all_dot.T
    scores = (
        jnp.einsum("qhd,khd->hqk", piece_query, key_heads, preferred_element_type=jnp.float32)
        * scaling
    )
    probability = jnp.exp(scores - piece_log[:, :, None])
    value_grad = jnp.einsum(
        "hqk,qhd->hkd",
        probability.astype(jnp.bfloat16),
        piece_grad,
        preferred_element_type=jnp.float32,
    )
    prob_grad = jnp.einsum(
        "qhd,khd->hqk", piece_grad, value_heads, preferred_element_type=jnp.float32
    )
    score_grad = (probability * (prob_grad - piece_dot[:, :, None])).astype(jnp.bfloat16)
    key_grad = (
        jnp.einsum("hqk,qhd->hkd", score_grad, piece_query, preferred_element_type=jnp.float32)
        * scaling
    )
    return (key_grad, value_grad)


def head_rows(matrix):
    return matrix.transpose(1, 0, 2).reshape(matrix.shape[1], HEADS * HEAD_DIM)


def rows_plan(patches, segment, dest_shard, dest_slot, w_qkv, out_grad):
    shard_count = lax.axis_size("seq")
    patch_rows = patches[0]
    patch_token = segment[0]
    targets = dest_shard[0]
    slot_ids = dest_slot[0]
    token_cap = targets.shape[0]
    pair_cap = token_cap // shard_count
    local_rows = out_grad.shape[1]
    inner_width = HEADS * HEAD_DIM
    member = (
        lax.broadcasted_iota(jnp.int32, (token_cap, patch_token.shape[0]), 0)
        == patch_token[None, :]
    )
    member_half = member.astype(jnp.bfloat16)
    counts = jnp.sum(member.astype(jnp.float32), axis=1)
    token_sums = jnp.dot(member_half, patch_rows, preferred_element_type=jnp.float32)
    tokens = (token_sums / jnp.maximum(counts, 1.0)[:, None]).astype(jnp.bfloat16)
    to_shard = (
        targets[:, None] == lax.broadcasted_iota(jnp.int32, (token_cap, shard_count), 1)
    ).astype(jnp.int32)
    ranking = jnp.sum((jnp.cumsum(to_shard, axis=0) - 1) * to_shard, axis=1)
    position = jnp.where(targets >= 0, targets * pair_cap + ranking, -1)
    chooser = position[None, :] == lax.broadcasted_iota(
        jnp.int32, (shard_count * pair_cap, token_cap), 0
    )
    chooser_half = chooser.astype(jnp.bfloat16)
    send_rows = jnp.dot(chooser_half, tokens, preferred_element_type=jnp.float32).astype(
        jnp.bfloat16
    )
    send_slot = jnp.sum(chooser.astype(jnp.int32) * (slot_ids + 1)[None, :], axis=1) - 1
    came_rows, came_slot = (
        lax.all_to_all(
            send_rows.reshape(shard_count, pair_cap, -1),
            "seq",
            split_axis=0,
            concat_axis=0,
            tiled=True,
        ),
        lax.all_to_all(
            send_slot.reshape(shard_count, pair_cap), "seq", split_axis=0, concat_axis=0, tiled=True
        ),
    )
    came_slot = came_slot.reshape(-1)
    placer = (
        came_slot[None, :]
        == lax.broadcasted_iota(jnp.int32, (local_rows, shard_count * pair_cap), 0)
    ).astype(jnp.bfloat16)
    placed = jnp.dot(
        placer, came_rows.reshape(shard_count * pair_cap, -1), preferred_element_type=jnp.float32
    ).astype(jnp.bfloat16)
    projected = jnp.dot(placed, w_qkv, preferred_element_type=jnp.float32).astype(jnp.bfloat16)
    query_rows = projected[:, :inner_width]
    key_rows = projected[:, inner_width : 2 * inner_width]
    value_rows = projected[:, 2 * inner_width :]
    query_heads = split_heads(query_rows)
    initial = (
        jnp.full((HEADS, local_rows), neg_large, jnp.float32),
        jnp.zeros((HEADS, local_rows), jnp.float32),
        jnp.zeros((HEADS, local_rows, HEAD_DIM), jnp.float32),
    )
    row_max, row_total, weighted = forward_fold(
        query_heads,
        initial,
        (
            lax.all_gather(key_rows, "seq", axis=0, tiled=True),
            lax.all_gather(value_rows, "seq", axis=0, tiled=True),
        ),
    )
    attended_rows = head_rows((weighted / row_total[:, :, None]).astype(jnp.bfloat16))
    grad_rows = out_grad[0]
    grad_heads = split_heads(grad_rows)
    log_total = row_max + jnp.log(row_total)
    grad_dot = jnp.sum(
        grad_heads.astype(jnp.float32) * split_heads(attended_rows).astype(jnp.float32), axis=2
    )
    blank = jnp.zeros((HEADS, local_rows, HEAD_DIM), jnp.float32)
    query_step = query_fold(query_heads, grad_heads, log_total, grad_dot.T)
    query_grad = query_step(
        blank,
        (
            lax.all_gather(key_rows, "seq", axis=0, tiled=True),
            lax.all_gather(value_rows, "seq", axis=0, tiled=True),
        ),
        jnp.int32(0),
    )
    all_log, all_dot = (
        lax.all_gather(log_total.T, "seq", axis=0, tiled=True),
        lax.all_gather(grad_dot, "seq", axis=0, tiled=True),
    )
    key_grad, value_grad = key_fold(
        split_heads(key_rows),
        split_heads(value_rows),
        all_log,
        all_dot,
        (
            lax.all_gather(query_rows, "seq", axis=0, tiled=True),
            lax.all_gather(grad_rows, "seq", axis=0, tiled=True),
        ),
    )
    proj_grad = jnp.concatenate(
        [head_rows(query_grad), head_rows(key_grad), head_rows(value_grad)], axis=1
    ).astype(jnp.bfloat16)
    placed_grad = jnp.einsum(
        "rc,dc->rd", proj_grad, w_qkv, preferred_element_type=jnp.float32
    ).astype(jnp.bfloat16)
    partial_value = jnp.einsum(
        "rd,rc->dc", placed, proj_grad, preferred_element_type=jnp.float32
    ).astype(jnp.bfloat16)
    across = lax.psum_scatter(partial_value, "seq", scatter_dimension=0, tiled=True).astype(
        jnp.float32
    )
    weight_grad = lax.psum_scatter(
        across.astype(jnp.bfloat16), "clip", scatter_dimension=1, tiled=True
    ).astype(jnp.float32)
    back_rows = jnp.einsum(
        "rj,rd->jd", placer, placed_grad, preferred_element_type=jnp.float32
    ).astype(jnp.bfloat16)
    returned = lax.all_to_all(
        back_rows.reshape(shard_count, pair_cap, -1), "seq", split_axis=0, concat_axis=0, tiled=True
    )
    token_grad = jnp.einsum(
        "jt,jd->td",
        chooser_half,
        returned.reshape(shard_count * pair_cap, -1),
        preferred_element_type=jnp.float32,
    ).astype(jnp.bfloat16)
    patch_sums = jnp.einsum(
        "tp,td->pd", member_half, token_grad, preferred_element_type=jnp.float32
    )
    patch_count = jnp.sum(member.astype(jnp.float32) * counts[:, None], axis=0)
    patch_grad = (patch_sums / patch_count[:, None]).astype(jnp.bfloat16)
    return (attended_rows[None], patch_grad[None], weight_grad)


VMEM_LIMIT = 40 * 1024 * 1024
NN = (((1,), (0,)), ((), ()))
NT = (((1,), (1,)), ((), ()))
TN = (((0,), (0,)), ((), ()))


def dot(left, right, dims=NN):
    return lax.dot_general(left, right, dims, preferred_element_type=jnp.float32)


def call(body, outs, *args, scratch=(), space=None, limit=VMEM_LIMIT):
    space = space or [pltpu.VMEM] * len(args)
    return pl.pallas_call(
        body,
        out_shape=outs,
        in_specs=[pl.BlockSpec(memory_space=each) for each in space],
        scratch_shapes=scratch,
        compiler_params=pltpu.CompilerParams(vmem_limit_bytes=limit),
    )(*args)


def one_hot(condition):
    return jnp.where(condition, 1.0, 0.0).astype(jnp.bfloat16)


def fold_half(rows):
    half = rows.shape[0] // 2
    return jnp.concatenate([rows[:half], rows[half:]], axis=1)


def unfold_half(rows):
    width = rows.shape[1] // 2
    return jnp.concatenate([rows[:, :width], rows[:, width:]], axis=0)


def wide_row(row):
    short = 256 - row.shape[1]
    wide = row.astype(jnp.float32)
    wide = jnp.concatenate([wide, jnp.full((1, short), -1.0, jnp.float32)], axis=1)
    return wide[:, :128], wide[:, 128:]


def token_kernel(*refs):
    sources, refs = refs[:6], refs[6:]
    sends, refs = refs[:HEADS], refs[HEADS:]
    (target_ref, segment_out, held_ref), refs = refs[:3], refs[3:]
    segment_ref, patch_ref, shard_ref, slot_ref, grad_ref, w_ref, done = refs
    pairs = list(zip(sources, refs))[:-1]
    for part in range(3):
        columns = pl.ds(part * grad_ref.shape[1], grad_ref.shape[1])
        pairs.append((sources[5].at[:, columns], w_ref.at[part]))
    copies = [
        pltpu.make_async_copy(source, held, done.at[index])
        for index, (source, held) in enumerate(pairs)
    ]
    for copy in copies:
        copy.start()
    token_cap = shard_ref.shape[1]
    local_rows, inner = grad_ref.shape
    devices = len(sends)
    width = patch_ref.shape[1] // devices
    copies[0].wait()
    segment = segment_ref[...]
    segment_out[...] = segment
    member = lax.broadcasted_iota(jnp.int32, (token_cap, segment.shape[1]), 0) == segment
    counts = jnp.sum(jnp.where(member, 1.0, 0.0), axis=1, keepdims=True)
    copies[1].wait()
    token_sums = dot(one_hot(member), patch_ref[...])
    tokens = (token_sums / jnp.maximum(counts, 1.0)).astype(jnp.bfloat16)
    for copy in copies[2:5]:
        copy.wait()
    shard, slot = shard_ref[...], slot_ref[...]
    target_ref[...] = jnp.where(shard >= 0, shard * local_rows + slot, -1)
    shard_low, shard_high = wide_row(shard)
    slot_low, slot_high = wide_row(slot)
    line = lax.broadcasted_iota(jnp.int32, (16, 128), 0)
    where_to = jnp.where(
        line == 0,
        shard_low,
        jnp.where(line == 1, shard_high, jnp.where(line == 2, slot_low, slot_high)),
    ).astype(jnp.bfloat16)
    grads = grad_ref[...]
    half = token_cap + token_cap // 2
    for head in range(devices):
        first = head * HEAD_DIM
        start = half
        for piece in (
            where_to,
            fold_half(grads[:, first : first + HEAD_DIM]),
            tokens[:, head * width : (head + 1) * width],
        ):
            held_ref[head, start : start + piece.shape[0]] = piece
            start += piece.shape[0]
    for part, copy in enumerate(copies[5:]):
        copy.wait()
        projected = dot(tokens, w_ref[part]).astype(jnp.bfloat16)
        for head in range(devices):
            rows = projected[:, head * HEAD_DIM : (head + 1) * HEAD_DIM]
            if part < 2:
                held_ref[head, :token_cap, part * HEAD_DIM : (part + 1) * HEAD_DIM] = rows
            else:
                held_ref[head, token_cap:half] = fold_half(rows)
    me = lax.axis_index("seq")
    for flip, send in enumerate(sends):
        send[...] = held_ref[jnp.bitwise_xor(me, flip)]


def target_row(lines, token_cap, local_rows):
    lines = lines.astype(jnp.float32)
    shard = jnp.concatenate([lines[0:1], lines[1:2]], axis=1)[:, :token_cap]
    slot = jnp.concatenate([lines[2:3], lines[3:4]], axis=1)[:, :token_cap]
    return (shard * local_rows + slot).astype(jnp.int32)


def head_kernel(token_cap, flips, *refs):
    pieces, refs = refs[:HEADS], refs[HEADS:]
    outs, (target_ref, grad_ref, attended_ref) = refs[: HEADS // 2], refs[HEADS // 2 :]
    devices, local_rows = len(pieces), grad_ref.shape[1]
    rows = devices * local_rows
    scaling = HEAD_DIM ** (-0.5)
    half_cap = token_cap // 2
    lines_at = token_cap + half_cap
    me = lax.axis_index("seq")
    targets, rows_in = [], []
    for flip, piece in zip(flips, pieces):
        sender = jnp.bitwise_xor(me, flip)
        target = target_row(piece[lines_at : lines_at + 16], token_cap, local_rows)
        target_ref[sender] = target
        targets.append(target)
        value = unfold_half(piece[token_cap:lines_at])
        rows_in.append(jnp.concatenate([piece[:token_cap], value], axis=1))
        grad_ref[sender] = unfold_half(piece[lines_at + 16 : lines_at + 16 + local_rows // 2])
    row_id = lax.broadcasted_iota(jnp.int32, (rows, devices * token_cap), 0)
    placer = one_hot(row_id == jnp.concatenate(targets, axis=1))
    total = dot(placer, jnp.concatenate(rows_in, axis=0))
    projected = total.astype(jnp.bfloat16)
    query = projected[:, :HEAD_DIM]
    key = projected[:, HEAD_DIM : 2 * HEAD_DIM]
    value = projected[:, 2 * HEAD_DIM :]
    grad = jnp.concatenate([grad_ref[place] for place in range(devices)], axis=0)
    scores = dot(key, query, NT) * scaling
    weights = jnp.exp(scores - jnp.max(scores, axis=0, keepdims=True))
    row_total = jnp.sum(weights, axis=0, keepdims=True)
    attended = (dot(value, weights.astype(jnp.bfloat16), TN) / row_total).astype(jnp.bfloat16)
    attended = attended.astype(jnp.float32)
    grad_dot = jnp.sum(grad.astype(jnp.float32).T * attended, axis=0, keepdims=True)
    probability = weights * (1.0 / row_total)
    score_grad = (probability * (dot(value, grad, NT) - grad_dot)).astype(jnp.bfloat16)
    value_grad = dot(probability.astype(jnp.bfloat16), grad)
    key_grad = dot(score_grad, query) * scaling
    query_grad = (dot(key, score_grad, TN) * scaling).T
    attended = attended.T.astype(jnp.bfloat16)
    for place in range(devices):
        attended_ref[place] = fold_half(attended[place * local_rows : (place + 1) * local_rows])
    proj_grad = jnp.concatenate([query_grad, key_grad], axis=1).astype(jnp.bfloat16)
    value_grad = fold_half(value_grad.astype(jnp.bfloat16))
    end = rows + rows // 2
    for chip, out in enumerate(outs):
        out[:rows] = proj_grad
        out[rows:end] = value_grad
        for core in range(2):
            first = end + core * local_rows // 2
            place = jnp.bitwise_xor(me, 2 * chip + core)
            out[first : first + local_rows // 2] = attended_ref[place]


def block_kernel(flips, target_ref, *refs):
    pieces, placed_ref = refs[:-1], refs[-1]
    token_cap = target_ref.shape[2]
    width, rows = placed_ref.shape
    row_id = lax.broadcasted_iota(jnp.int32, (rows, token_cap), 0)
    total = jnp.zeros((rows, width), jnp.float32)
    me = lax.axis_index("seq")
    for flip, piece in zip(flips, pieces):
        target = target_ref[jnp.bitwise_xor(me, flip)]
        total = total + dot(one_hot(row_id == target), piece[piece.shape[0] - token_cap :])
    placed_ref[...] = total.T.astype(jnp.bfloat16)


def by_column(left, flips, pieces, held_ref):
    rows = left.shape[1]
    half, end = rows // 2, rows + rows // 2
    me = lax.axis_index("seq")
    for flip, piece in zip(flips, pieces):
        both = dot(left, piece[:rows])
        low = dot(left[:, :half], piece[rows:end])
        high = dot(left[:, half:], piece[rows:end])
        value = low[:, :HEAD_DIM] + high[:, HEAD_DIM:]
        held_ref[jnp.bitwise_xor(me, flip)] = jnp.concatenate([both, value], axis=1)
    return jnp.concatenate(
        [
            held_ref[head, :, part * HEAD_DIM : (part + 1) * HEAD_DIM]
            for part in range(3)
            for head in range(len(pieces))
        ],
        axis=1,
    )


def weight_kernel(flips, placed_ref, *refs):
    pieces, outs, (held_ref, block_ref) = refs[:HEADS], refs[HEADS:-2], refs[-2:]
    columns = by_column(placed_ref[...], flips, pieces, held_ref).astype(jnp.bfloat16)
    width = columns.shape[1] // len(outs)
    me = lax.axis_index("clip")
    for index in range(len(outs)):
        block_ref[index] = columns[:, index * width : (index + 1) * width]
    for flip, out in enumerate(outs):
        out[...] = block_ref[jnp.bitwise_xor(me, flip)]


def patch_kernel(flips, segment_ref, target_ref, w_hbm, *refs):
    pieces, (patch_ref, attended_ref, held_ref, part_ref, w_ref, done) = refs[:HEADS], refs[HEADS:]
    copy = pltpu.make_async_copy(w_hbm, w_ref, done)
    copy.start()
    token_cap = target_ref.shape[1]
    local_rows = attended_ref.shape[0]
    rows = HEADS * local_rows
    me = lax.axis_index("seq")
    for flip, piece in zip(flips, pieces):
        first = rows + rows // 2 + flip % 2 * local_rows // 2
        part_ref[jnp.bitwise_xor(me, flip)] = unfold_half(piece[first : first + local_rows // 2])
    attended_ref[...] = jnp.concatenate([part_ref[head] for head in range(HEADS)], axis=1)
    row_id = lax.broadcasted_iota(jnp.int32, (rows, token_cap), 0)
    chooser = jnp.where(row_id == target_ref[...], 1.0, 0.0).T.astype(jnp.bfloat16)
    proj_grad = by_column(chooser, flips, pieces, held_ref).astype(jnp.bfloat16)
    copy.wait()
    token_grad = dot(proj_grad, w_ref[...], NT).astype(jnp.bfloat16).astype(jnp.float32)
    member = (
        lax.broadcasted_iota(jnp.int32, (token_cap, segment_ref.shape[1]), 0) == segment_ref[...]
    )
    counts = jnp.sum(jnp.where(member, 1.0, 0.0), axis=1, keepdims=True)
    shared = (token_grad / jnp.maximum(counts, 1.0)).astype(jnp.bfloat16)
    patch_ref[...] = dot(one_hot(member), shared, TN).astype(jnp.bfloat16)


def copy_kernel(source_ref, target_ref):
    target_ref[...] = source_ref[...]


def sum_kernel(*refs):
    total = refs[0][...].astype(jnp.float32)
    for ref in refs[1:-1]:
        total = total + ref[...].astype(jnp.float32)
    refs[-1][...] = total


def exchange(rows, axis, flip):
    count = lax.axis_size(axis)
    return lax.ppermute(rows, axis, [(index, index ^ flip) for index in range(count)])


def shape(*sizes, dtype=jnp.bfloat16):
    return jax.ShapeDtypeStruct(sizes, dtype)


def start_order(flip):
    steps = (flip // 2).bit_count()
    return flip > 0, -steps, flip % 2, -flip


def heads_plan(patches, segment, dest_shard, dest_slot, w_qkv, out_grad):
    devices = lax.axis_size("seq")
    clips = lax.axis_size("clip")
    token_cap = dest_shard.shape[1]
    local_rows, inner = out_grad.shape[1:]
    rows = devices * local_rows
    model = patches.shape[2]
    width = model // devices
    sent = token_cap + token_cap // 2 + 16 + local_rows // 2 + token_cap
    sources = (segment, patches[0], dest_shard, dest_slot, out_grad[0], w_qkv)
    outs = call(
        token_kernel,
        [shape(sent, 2 * HEAD_DIM)] * devices
        + [shape(1, token_cap, dtype=jnp.int32), shape(*segment.shape, dtype=jnp.int32)],
        *sources,
        scratch=[
            pltpu.VMEM((devices, sent, 2 * HEAD_DIM), jnp.bfloat16),
        ]
        + [pltpu.VMEM(source.shape, source.dtype) for source in sources[:-1]]
        + [
            pltpu.VMEM((3, model, inner), w_qkv.dtype),
            pltpu.SemaphoreType.DMA((len(sources) + 2,)),
        ],
        space=[pltpu.HBM] * len(sources),
        limit=62 * 1024 * 1024,
    )
    sends, (target, segment) = list(outs[:devices]), outs[devices:]
    order = sorted(range(devices), key=start_order)
    sends[0] = call(copy_kernel, shape(sent, 2 * HEAD_DIM), sends[0])
    came = {0: sends[0]}
    for flip in order[1:]:
        came[flip] = exchange(sends[flip], "seq", flip)
    came = [came[flip] for flip in order]
    *proj, targets = call(
        functools.partial(head_kernel, token_cap, order),
        [shape(rows + rows // 2 + local_rows, 2 * HEAD_DIM)] * (devices // 2)
        + [shape(devices, 1, token_cap, dtype=jnp.int32)],
        *came,
        scratch=[
            pltpu.VMEM((devices, local_rows, HEAD_DIM), jnp.bfloat16),
            pltpu.VMEM((devices, local_rows // 2, 2 * HEAD_DIM), jnp.bfloat16),
        ],
    )
    pieces = {0: proj[0]}
    for flip in order[1:]:
        if flip % 2 == 0:
            pieces[flip] = exchange(proj[flip // 2], "seq", flip)
    for flip in list(pieces):
        pieces[flip + 1] = exchange(pieces[flip], "seq", 1)
    flips = order
    pieces = [pieces[flip] for flip in flips]
    placed = call(
        functools.partial(block_kernel, order), shape(width, rows), targets, *came
    )
    weights = call(
        functools.partial(weight_kernel, flips),
        [shape(width, 3 * inner // clips)] * clips,
        placed,
        *pieces,
        scratch=[
            pltpu.VMEM((devices, width, 3 * HEAD_DIM), jnp.float32),
            pltpu.VMEM((clips, width, 3 * inner // clips), jnp.bfloat16),
        ],
    )
    clip_flips = sorted(range(1, clips), key=lambda flip: (flip < clips // 2, flip))
    weights = [weights[0]] + [exchange(weights[flip], "clip", flip) for flip in clip_flips]
    patch_grad, attended = call(
        functools.partial(patch_kernel, flips),
        [shape(patches.shape[1], model), shape(local_rows, inner)],
        segment,
        target,
        w_qkv,
        *pieces,
        scratch=[
            pltpu.VMEM((devices, token_cap, 3 * HEAD_DIM), jnp.float32),
            pltpu.VMEM((devices, local_rows, HEAD_DIM), jnp.bfloat16),
            pltpu.VMEM(w_qkv.shape, w_qkv.dtype),
            pltpu.SemaphoreType.DMA(()),
        ],
        space=[pltpu.VMEM] * 2 + [pltpu.HBM] + [pltpu.VMEM] * devices,
    )
    weight_grad = call(
        sum_kernel, shape(width, 3 * inner // clips, dtype=jnp.float32), *weights
    )
    return attended[None], patch_grad[None], weight_grad


def solution(mesh):
    devices, clips = mesh.shape["seq"], mesh.shape["clip"]
    one_head_each = devices == HEADS and clips in (1, 2, 4, 8)
    return jax.shard_map(
        heads_plan if one_head_each else rows_plan,
        mesh=mesh,
        in_specs=(
            P("clip", "seq", None),
            P("clip", "seq"),
            P("clip", "seq"),
            P("clip", "seq"),
            P(),
            P("clip", "seq", None),
        ),
        out_specs=(P("clip", "seq", None), P("clip", "seq", None), P("seq", "clip")),
        check_vma=False,
    )
```

```python
import functools

import jax
import jax.numpy as jnp
from jax import lax
from jax.experimental import pallas as pl
from jax.experimental.pallas import tpu as pltpu
from jax.sharding import PartitionSpec as P

HEADS = 8
HEAD_DIM = 64


neg_large = -1e30


def split_heads(rows_in):
    return rows_in.reshape(rows_in.shape[0], HEADS, HEAD_DIM)


def forward_fold(query_heads, running, pieces):
    scaling = HEAD_DIM ** (-0.5)
    row_max, row_total, weighted = running
    key_heads = split_heads(pieces[0])
    value_heads = split_heads(pieces[1])
    scores = (
        jnp.einsum("rhd,khd->hrk", query_heads, key_heads, preferred_element_type=jnp.float32)
        * scaling
    )
    new_max = jnp.maximum(row_max, jnp.max(scores, axis=2))
    weights = jnp.exp(scores - new_max[:, :, None])
    row_total = jnp.sum(weights, axis=2)
    weighted = jnp.einsum(
        "hrk,khd->hrd",
        weights.astype(jnp.bfloat16),
        value_heads,
        preferred_element_type=jnp.float32,
    )
    return (new_max, row_total, weighted)


def query_fold(query_heads, grad_heads, log_total, grad_dot):
    scaling = HEAD_DIM ** (-0.5)

    def combine_piece(running, pieces, offset):
        key_heads = split_heads(pieces[0])
        value_heads = split_heads(pieces[1])
        scores = (
            jnp.einsum("rhd,khd->hrk", query_heads, key_heads, preferred_element_type=jnp.float32)
            * scaling
        )
        probability = jnp.exp(scores - log_total[:, :, None])
        prob_grad = jnp.einsum(
            "rhd,khd->hrk", grad_heads, value_heads, preferred_element_type=jnp.float32
        )
        score_grad = (probability * (prob_grad - grad_dot[:, :, None])).astype(jnp.bfloat16)
        return (
            jnp.einsum("hrk,khd->hrd", score_grad, key_heads, preferred_element_type=jnp.float32)
            * scaling
        )

    return combine_piece


def key_fold(key_heads, value_heads, all_log, all_dot, pieces):
    scaling = HEAD_DIM ** (-0.5)
    piece_query = split_heads(pieces[0])
    piece_grad = split_heads(pieces[1])
    piece_log = all_log.T
    piece_dot = all_dot.T
    scores = (
        jnp.einsum("qhd,khd->hqk", piece_query, key_heads, preferred_element_type=jnp.float32)
        * scaling
    )
    probability = jnp.exp(scores - piece_log[:, :, None])
    value_grad = jnp.einsum(
        "hqk,qhd->hkd",
        probability.astype(jnp.bfloat16),
        piece_grad,
        preferred_element_type=jnp.float32,
    )
    prob_grad = jnp.einsum(
        "qhd,khd->hqk", piece_grad, value_heads, preferred_element_type=jnp.float32
    )
    score_grad = (probability * (prob_grad - piece_dot[:, :, None])).astype(jnp.bfloat16)
    key_grad = (
        jnp.einsum("hqk,qhd->hkd", score_grad, piece_query, preferred_element_type=jnp.float32)
        * scaling
    )
    return (key_grad, value_grad)


def head_rows(matrix):
    return matrix.transpose(1, 0, 2).reshape(matrix.shape[1], HEADS * HEAD_DIM)


def rows_plan(patches, segment, dest_shard, dest_slot, w_qkv, out_grad):
    shard_count = lax.axis_size("seq")
    patch_rows = patches[0]
    patch_token = segment[0]
    targets = dest_shard[0]
    slot_ids = dest_slot[0]
    token_cap = targets.shape[0]
    pair_cap = token_cap // shard_count
    local_rows = out_grad.shape[1]
    inner_width = HEADS * HEAD_DIM
    member = (
        lax.broadcasted_iota(jnp.int32, (token_cap, patch_token.shape[0]), 0)
        == patch_token[None, :]
    )
    member_half = member.astype(jnp.bfloat16)
    counts = jnp.sum(member.astype(jnp.float32), axis=1)
    token_sums = jnp.dot(member_half, patch_rows, preferred_element_type=jnp.float32)
    tokens = (token_sums / jnp.maximum(counts, 1.0)[:, None]).astype(jnp.bfloat16)
    to_shard = (
        targets[:, None] == lax.broadcasted_iota(jnp.int32, (token_cap, shard_count), 1)
    ).astype(jnp.int32)
    ranking = jnp.sum((jnp.cumsum(to_shard, axis=0) - 1) * to_shard, axis=1)
    position = jnp.where(targets >= 0, targets * pair_cap + ranking, -1)
    chooser = position[None, :] == lax.broadcasted_iota(
        jnp.int32, (shard_count * pair_cap, token_cap), 0
    )
    chooser_half = chooser.astype(jnp.bfloat16)
    send_rows = jnp.dot(chooser_half, tokens, preferred_element_type=jnp.float32).astype(
        jnp.bfloat16
    )
    send_slot = jnp.sum(chooser.astype(jnp.int32) * (slot_ids + 1)[None, :], axis=1) - 1
    came_rows, came_slot = (
        lax.all_to_all(
            send_rows.reshape(shard_count, pair_cap, -1),
            "seq",
            split_axis=0,
            concat_axis=0,
            tiled=True,
        ),
        lax.all_to_all(
            send_slot.reshape(shard_count, pair_cap), "seq", split_axis=0, concat_axis=0, tiled=True
        ),
    )
    came_slot = came_slot.reshape(-1)
    placer = (
        came_slot[None, :]
        == lax.broadcasted_iota(jnp.int32, (local_rows, shard_count * pair_cap), 0)
    ).astype(jnp.bfloat16)
    placed = jnp.dot(
        placer, came_rows.reshape(shard_count * pair_cap, -1), preferred_element_type=jnp.float32
    ).astype(jnp.bfloat16)
    projected = jnp.dot(placed, w_qkv, preferred_element_type=jnp.float32).astype(jnp.bfloat16)
    query_rows = projected[:, :inner_width]
    key_rows = projected[:, inner_width : 2 * inner_width]
    value_rows = projected[:, 2 * inner_width :]
    query_heads = split_heads(query_rows)
    initial = (
        jnp.full((HEADS, local_rows), neg_large, jnp.float32),
        jnp.zeros((HEADS, local_rows), jnp.float32),
        jnp.zeros((HEADS, local_rows, HEAD_DIM), jnp.float32),
    )
    row_max, row_total, weighted = forward_fold(
        query_heads,
        initial,
        (
            lax.all_gather(key_rows, "seq", axis=0, tiled=True),
            lax.all_gather(value_rows, "seq", axis=0, tiled=True),
        ),
    )
    attended_rows = head_rows((weighted / row_total[:, :, None]).astype(jnp.bfloat16))
    grad_rows = out_grad[0]
    grad_heads = split_heads(grad_rows)
    log_total = row_max + jnp.log(row_total)
    grad_dot = jnp.sum(
        grad_heads.astype(jnp.float32) * split_heads(attended_rows).astype(jnp.float32), axis=2
    )
    blank = jnp.zeros((HEADS, local_rows, HEAD_DIM), jnp.float32)
    query_step = query_fold(query_heads, grad_heads, log_total, grad_dot.T)
    query_grad = query_step(
        blank,
        (
            lax.all_gather(key_rows, "seq", axis=0, tiled=True),
            lax.all_gather(value_rows, "seq", axis=0, tiled=True),
        ),
        jnp.int32(0),
    )
    all_log, all_dot = (
        lax.all_gather(log_total.T, "seq", axis=0, tiled=True),
        lax.all_gather(grad_dot, "seq", axis=0, tiled=True),
    )
    key_grad, value_grad = key_fold(
        split_heads(key_rows),
        split_heads(value_rows),
        all_log,
        all_dot,
        (
            lax.all_gather(query_rows, "seq", axis=0, tiled=True),
            lax.all_gather(grad_rows, "seq", axis=0, tiled=True),
        ),
    )
    proj_grad = jnp.concatenate(
        [head_rows(query_grad), head_rows(key_grad), head_rows(value_grad)], axis=1
    ).astype(jnp.bfloat16)
    placed_grad = jnp.einsum(
        "rc,dc->rd", proj_grad, w_qkv, preferred_element_type=jnp.float32
    ).astype(jnp.bfloat16)
    partial_value = jnp.einsum(
        "rd,rc->dc", placed, proj_grad, preferred_element_type=jnp.float32
    ).astype(jnp.bfloat16)
    across = lax.psum_scatter(partial_value, "seq", scatter_dimension=0, tiled=True).astype(
        jnp.float32
    )
    weight_grad = lax.psum_scatter(
        across.astype(jnp.bfloat16), "clip", scatter_dimension=1, tiled=True
    ).astype(jnp.float32)
    back_rows = jnp.einsum(
        "rj,rd->jd", placer, placed_grad, preferred_element_type=jnp.float32
    ).astype(jnp.bfloat16)
    returned = lax.all_to_all(
        back_rows.reshape(shard_count, pair_cap, -1), "seq", split_axis=0, concat_axis=0, tiled=True
    )
    token_grad = jnp.einsum(
        "jt,jd->td",
        chooser_half,
        returned.reshape(shard_count * pair_cap, -1),
        preferred_element_type=jnp.float32,
    ).astype(jnp.bfloat16)
    patch_sums = jnp.einsum(
        "tp,td->pd", member_half, token_grad, preferred_element_type=jnp.float32
    )
    patch_count = jnp.sum(member.astype(jnp.float32) * counts[:, None], axis=0)
    patch_grad = (patch_sums / patch_count[:, None]).astype(jnp.bfloat16)
    return (attended_rows[None], patch_grad[None], weight_grad)


VMEM_LIMIT = 40 * 1024 * 1024
NN = (((1,), (0,)), ((), ()))
NT = (((1,), (1,)), ((), ()))
TN = (((0,), (0,)), ((), ()))


def dot(left, right, dims=NN):
    return lax.dot_general(left, right, dims, preferred_element_type=jnp.float32)


def call(body, outs, *args, scratch=(), space=None, limit=VMEM_LIMIT, flops=0):
    space = space or [pltpu.VMEM] * len(args)
    return pl.pallas_call(
        body,
        out_shape=outs,
        in_specs=[pl.BlockSpec(memory_space=each) for each in space],
        scratch_shapes=scratch,
        cost_estimate=pl.CostEstimate(flops=flops, bytes_accessed=0, transcendentals=0),
        compiler_params=pltpu.CompilerParams(vmem_limit_bytes=limit),
    )(*args)


def one_hot(condition):
    return jnp.where(condition, 1.0, 0.0).astype(jnp.bfloat16)


def fold_half(rows):
    half = rows.shape[0] // 2
    return jnp.concatenate([rows[:half], rows[half:]], axis=1)


def unfold_half(rows):
    width = rows.shape[1] // 2
    return jnp.concatenate([rows[:, :width], rows[:, width:]], axis=0)


def wide_row(row):
    short = 256 - row.shape[1]
    wide = row.astype(jnp.float32)
    wide = jnp.concatenate([wide, jnp.full((1, short), -1.0, jnp.float32)], axis=1)
    return wide[:, :128], wide[:, 128:]


def token_kernel(*refs):
    sources, refs = refs[:6], refs[6:]
    sends, refs = refs[:HEADS], refs[HEADS:]
    (target_ref, segment_out, held_ref), refs = refs[:3], refs[3:]
    segment_ref, patch_ref, shard_ref, slot_ref, grad_ref, w_ref, done = refs
    pairs = list(zip(sources, refs))[:-1]
    for part in range(3):
        columns = pl.ds(part * grad_ref.shape[1], grad_ref.shape[1])
        pairs.append((sources[5].at[:, columns], w_ref.at[part]))
    copies = [
        pltpu.make_async_copy(source, held, done.at[index])
        for index, (source, held) in enumerate(pairs)
    ]
    for copy in copies:
        copy.start()
    token_cap = shard_ref.shape[1]
    local_rows, inner = grad_ref.shape
    devices = len(sends)
    width = patch_ref.shape[1] // devices
    copies[0].wait()
    segment = segment_ref[...]
    segment_out[...] = segment
    member = lax.broadcasted_iota(jnp.int32, (token_cap, segment.shape[1]), 0) == segment
    counts = jnp.sum(jnp.where(member, 1.0, 0.0), axis=1, keepdims=True)
    copies[1].wait()
    token_sums = dot(one_hot(member), patch_ref[...])
    tokens = (token_sums / jnp.maximum(counts, 1.0)).astype(jnp.bfloat16)
    for copy in copies[2:5]:
        copy.wait()
    shard, slot = shard_ref[...], slot_ref[...]
    target_ref[...] = jnp.where(shard >= 0, shard * local_rows + slot, -1)
    shard_low, shard_high = wide_row(shard)
    slot_low, slot_high = wide_row(slot)
    line = lax.broadcasted_iota(jnp.int32, (16, 128), 0)
    where_to = jnp.where(
        line == 0,
        shard_low,
        jnp.where(line == 1, shard_high, jnp.where(line == 2, slot_low, slot_high)),
    ).astype(jnp.bfloat16)
    grads = grad_ref[...]
    half = token_cap + token_cap // 2
    for head in range(devices):
        first = head * HEAD_DIM
        start = half
        for piece in (
            where_to,
            fold_half(grads[:, first : first + HEAD_DIM]),
            tokens[:, head * width : (head + 1) * width],
        ):
            held_ref[head, start : start + piece.shape[0]] = piece
            start += piece.shape[0]
    for part, copy in enumerate(copies[5:]):
        copy.wait()
        projected = dot(tokens, w_ref[part]).astype(jnp.bfloat16)
        for head in range(devices):
            rows = projected[:, head * HEAD_DIM : (head + 1) * HEAD_DIM]
            if part < 2:
                held_ref[head, :token_cap, part * HEAD_DIM : (part + 1) * HEAD_DIM] = rows
            else:
                held_ref[head, token_cap:half] = fold_half(rows)
    me = lax.axis_index("seq")
    for flip, send in enumerate(sends):
        send[...] = held_ref[jnp.bitwise_xor(me, flip)]


def target_row(lines, token_cap, local_rows):
    lines = lines.astype(jnp.float32)
    shard = jnp.concatenate([lines[0:1], lines[1:2]], axis=1)[:, :token_cap]
    slot = jnp.concatenate([lines[2:3], lines[3:4]], axis=1)[:, :token_cap]
    return (shard * local_rows + slot).astype(jnp.int32)


def place_rows(token_cap, rows, pieces, target_ref, grad_ref):
    local_rows = grad_ref.shape[1]
    lines_at = token_cap + token_cap // 2
    targets, rows_in = [], []
    for index, piece in enumerate(pieces):
        target = target_row(piece[lines_at : lines_at + 16], token_cap, local_rows)
        target_ref[index] = target
        targets.append(target)
        value = unfold_half(piece[token_cap:lines_at])
        rows_in.append(jnp.concatenate([piece[:token_cap], value], axis=1))
        grad_ref[index] = unfold_half(piece[lines_at + 16 : lines_at + 16 + local_rows // 2])
    row_id = lax.broadcasted_iota(jnp.int32, (rows, len(pieces) * token_cap), 0)
    placer = one_hot(row_id == jnp.concatenate(targets, axis=1))
    return dot(placer, jnp.concatenate(rows_in, axis=0))


def early_kernel(token_cap, *refs):
    pieces, (total_ref, target_ref, grad_ref) = refs[:-3], refs[-3:]
    total = place_rows(token_cap, total_ref.shape[0], pieces, target_ref, grad_ref)
    total_ref[...] = total.astype(jnp.bfloat16)


def head_kernel(token_cap, flips, early_ref, early_grad_ref, *refs):
    early = early_grad_ref.shape[0]
    pieces, refs = refs[: HEADS - early], refs[HEADS - early :]
    outs, (target_ref, late_grad_ref, grad_ref, attended_ref) = refs[: HEADS // 2], refs[HEADS // 2 :]
    devices, local_rows = len(flips), grad_ref.shape[1]
    rows = devices * local_rows
    scaling = HEAD_DIM ** (-0.5)
    me = lax.axis_index("seq")
    total = place_rows(token_cap, rows, pieces, target_ref, late_grad_ref)
    total = total + early_ref[...].astype(jnp.float32)
    for index, flip in enumerate(flips):
        came = early_grad_ref[index] if index < early else late_grad_ref[index - early]
        grad_ref[jnp.bitwise_xor(me, flip)] = came
    projected = total.astype(jnp.bfloat16)
    query = projected[:, :HEAD_DIM]
    key = projected[:, HEAD_DIM : 2 * HEAD_DIM]
    value = projected[:, 2 * HEAD_DIM :]
    grad = jnp.concatenate([grad_ref[place] for place in range(devices)], axis=0)
    scores = dot(key, query, NT) * scaling
    weights = jnp.exp(scores - jnp.max(scores, axis=0, keepdims=True))
    row_total = jnp.sum(weights, axis=0, keepdims=True)
    attended = (dot(value, weights.astype(jnp.bfloat16), TN) / row_total).astype(jnp.bfloat16)
    attended = attended.astype(jnp.float32)
    grad_dot = jnp.sum(grad.astype(jnp.float32).T * attended, axis=0, keepdims=True)
    probability = weights * (1.0 / row_total)
    score_grad = (probability * (dot(value, grad, NT) - grad_dot)).astype(jnp.bfloat16)
    value_grad = dot(probability.astype(jnp.bfloat16), grad)
    key_grad = dot(score_grad, query) * scaling
    query_grad = (dot(key, score_grad, TN) * scaling).T
    attended = attended.T.astype(jnp.bfloat16)
    for place in range(devices):
        attended_ref[place] = fold_half(attended[place * local_rows : (place + 1) * local_rows])
    proj_grad = jnp.concatenate([query_grad, key_grad], axis=1).astype(jnp.bfloat16)
    value_grad = fold_half(value_grad.astype(jnp.bfloat16))
    end = rows + rows // 2
    for chip, out in enumerate(outs):
        out[:rows] = proj_grad
        out[rows:end] = value_grad
        for core in range(2):
            first = end + core * local_rows // 2
            place = jnp.bitwise_xor(me, 2 * chip + core)
            out[first : first + local_rows // 2] = attended_ref[place]


def block_kernel(early_ref, late_ref, *refs):
    pieces, placed_ref = refs[:-1], refs[-1]
    early, _, token_cap = early_ref.shape
    rows = placed_ref.shape[1]
    targets = [early_ref[index] for index in range(early)]
    targets += [late_ref[index] for index in range(len(pieces) - early)]
    row_id = lax.broadcasted_iota(jnp.int32, (rows, len(pieces) * token_cap), 0)
    placer = one_hot(row_id == jnp.concatenate(targets, axis=1))
    rows_in = [piece[piece.shape[0] - token_cap :] for piece in pieces]
    placed_ref[...] = dot(placer, jnp.concatenate(rows_in, axis=0)).T.astype(jnp.bfloat16)


def head_columns(left, pieces):
    rows = left.shape[1]
    half, end = rows // 2, rows + rows // 2
    wide = 2 * HEAD_DIM
    both = dot(left, jnp.concatenate([piece[:rows] for piece in pieces], axis=1))
    folded = jnp.concatenate([piece[rows:end] for piece in pieces], axis=1)
    low, high = dot(left[:, :half], folded), dot(left[:, half:], folded)
    columns = []
    for first in range(0, both.shape[1], wide):
        value = low[:, first : first + HEAD_DIM] + high[:, first + HEAD_DIM : first + wide]
        columns.append(jnp.concatenate([both[:, first : first + wide], value], axis=1))
    return columns


def in_order(held_ref):
    return jnp.concatenate(
        [
            held_ref[head, :, part * HEAD_DIM : (part + 1) * HEAD_DIM]
            for part in range(3)
            for head in range(held_ref.shape[0])
        ],
        axis=1,
    )


def near_kernel(placed_ref, *refs):
    pieces, out_ref = refs[:-1], refs[-1]
    for index, columns in enumerate(head_columns(placed_ref[...], pieces)):
        out_ref[index] = columns.astype(jnp.bfloat16)


def weight_kernel(flips, placed_ref, near_ref, *refs):
    count = len(flips) - near_ref.shape[0]
    pieces, outs, (held_ref, block_ref) = refs[:count], refs[count:-2], refs[-2:]
    seq, clip = lax.axis_index("seq"), lax.axis_index("clip")
    columns = [near_ref[index] for index in range(near_ref.shape[0])]
    columns += head_columns(placed_ref[...], pieces)
    for flip, each in zip(flips, columns):
        held_ref[jnp.bitwise_xor(seq, flip)] = each.astype(jnp.bfloat16)
    columns = in_order(held_ref)
    width = columns.shape[1] // len(outs)
    for index in range(len(outs)):
        block_ref[index] = columns[:, index * width : (index + 1) * width]
    for flip, out in enumerate(outs):
        out[...] = block_ref[jnp.bitwise_xor(clip, flip)]


def patch_kernel(flips, segment_ref, target_ref, w_hbm, *refs):
    pieces, (patch_ref, attended_ref, held_ref, part_ref, w_ref, done) = refs[:HEADS], refs[HEADS:]
    copy = pltpu.make_async_copy(w_hbm, w_ref, done)
    copy.start()
    token_cap = target_ref.shape[1]
    local_rows = attended_ref.shape[0]
    rows = HEADS * local_rows
    me = lax.axis_index("seq")
    for flip, piece in zip(flips, pieces):
        first = rows + rows // 2 + flip % 2 * local_rows // 2
        part_ref[jnp.bitwise_xor(me, flip)] = unfold_half(piece[first : first + local_rows // 2])
    attended_ref[...] = jnp.concatenate([part_ref[head] for head in range(HEADS)], axis=1)
    row_id = lax.broadcasted_iota(jnp.int32, (rows, token_cap), 0)
    chooser = jnp.where(row_id == target_ref[...], 1.0, 0.0).T.astype(jnp.bfloat16)
    for flip, columns in zip(flips, head_columns(chooser, pieces)):
        held_ref[jnp.bitwise_xor(me, flip)] = columns.astype(jnp.bfloat16)
    proj_grad = in_order(held_ref)
    copy.wait()
    token_grad = dot(proj_grad, w_ref[...], NT).astype(jnp.bfloat16).astype(jnp.float32)
    member = (
        lax.broadcasted_iota(jnp.int32, (token_cap, segment_ref.shape[1]), 0) == segment_ref[...]
    )
    counts = jnp.sum(jnp.where(member, 1.0, 0.0), axis=1, keepdims=True)
    shared = (token_grad / jnp.maximum(counts, 1.0)).astype(jnp.bfloat16)
    patch_ref[...] = dot(one_hot(member), shared, TN).astype(jnp.bfloat16)


def sum_kernel(*refs):
    total = refs[0][...].astype(jnp.float32)
    for ref in refs[1:-1]:
        total = total + ref[...].astype(jnp.float32)
    refs[-1][...] = total


def exchange(rows, axis, flip):
    count = lax.axis_size(axis)
    return lax.ppermute(rows, axis, [(index, index ^ flip) for index in range(count)])


def shape(*sizes, dtype=jnp.bfloat16):
    return jax.ShapeDtypeStruct(sizes, dtype)


def start_order(flip):
    steps = (flip // 2).bit_count()
    return flip > 0, -steps, flip % 2, -flip


def heads_plan(patches, segment, dest_shard, dest_slot, w_qkv, out_grad):
    devices = lax.axis_size("seq")
    clips = lax.axis_size("clip")
    token_cap = dest_shard.shape[1]
    local_rows, inner = out_grad.shape[1:]
    rows = devices * local_rows
    model = patches.shape[2]
    width = model // devices
    sent = token_cap + token_cap // 2 + 16 + local_rows // 2 + token_cap
    sources = (segment, patches[0], dest_shard, dest_slot, out_grad[0], w_qkv)
    outs = call(
        token_kernel,
        [shape(sent, 2 * HEAD_DIM)] * devices
        + [shape(1, token_cap, dtype=jnp.int32), shape(*segment.shape, dtype=jnp.int32)],
        *sources,
        scratch=[
            pltpu.VMEM((devices, sent, 2 * HEAD_DIM), jnp.bfloat16),
        ]
        + [pltpu.VMEM(source.shape, source.dtype) for source in sources[:-1]]
        + [
            pltpu.VMEM((3, model, inner), w_qkv.dtype),
            pltpu.SemaphoreType.DMA((len(sources) + 2,)),
        ],
        space=[pltpu.HBM] * len(sources),
        limit=62 * 1024 * 1024,
    )
    sends, (target, segment) = list(outs[:devices]), outs[devices:]
    order = sorted(range(devices), key=start_order)
    came = {0: sends[0]}
    for flip in order[1:]:
        came[flip] = exchange(sends[flip], "seq", flip)
    came = [came[flip] for flip in order]
    early = devices // 2
    placed, early_targets, early_grads = call(
        functools.partial(early_kernel, token_cap),
        [
            shape(rows, 3 * HEAD_DIM),
            shape(early, 1, token_cap, dtype=jnp.int32),
            shape(early, local_rows, HEAD_DIM),
        ],
        *came[:early],
        flops=1_000_000_000,
    )
    *proj, late_targets = call(
        functools.partial(head_kernel, token_cap, order),
        [shape(rows + rows // 2 + local_rows, 2 * HEAD_DIM)] * (devices // 2)
        + [shape(devices - early, 1, token_cap, dtype=jnp.int32)],
        placed,
        early_grads,
        *came[early:],
        scratch=[
            pltpu.VMEM((devices - early, local_rows, HEAD_DIM), jnp.bfloat16),
            pltpu.VMEM((devices, local_rows, HEAD_DIM), jnp.bfloat16),
            pltpu.VMEM((devices, local_rows // 2, 2 * HEAD_DIM), jnp.bfloat16),
        ],
    )
    pieces = {0: proj[0]}
    for flip in order[1:]:
        if flip % 2 == 0:
            pieces[flip] = exchange(proj[flip // 2], "seq", flip)
    for flip in list(pieces):
        pieces[flip + 1] = exchange(pieces[flip], "seq", 1)
    flips = order
    pieces = [pieces[flip] for flip in flips]
    placed = call(block_kernel, shape(width, rows), early_targets, late_targets, *came)
    near = [flip for flip in flips if flip % 2 == 0]
    far = [flip for flip in flips if flip % 2 == 1]
    columns = call(
        near_kernel,
        shape(len(near), width, 3 * HEAD_DIM),
        placed,
        *[pieces[flips.index(flip)] for flip in near],
    )
    weights = call(
        functools.partial(weight_kernel, near + far),
        [shape(width, 3 * inner // clips)] * clips,
        placed,
        columns,
        *[pieces[flips.index(flip)] for flip in far],
        scratch=[
            pltpu.VMEM((devices, width, 3 * HEAD_DIM), jnp.bfloat16),
            pltpu.VMEM((clips, width, 3 * inner // clips), jnp.bfloat16),
        ],
    )
    clip_flips = sorted(range(1, clips), key=lambda flip: (flip < clips // 2, flip))
    weights = [weights[0]] + [exchange(weights[flip], "clip", flip) for flip in clip_flips]
    patch_grad, attended = call(
        functools.partial(patch_kernel, flips),
        [shape(patches.shape[1], model), shape(local_rows, inner)],
        segment,
        target,
        w_qkv,
        *pieces,
        scratch=[
            pltpu.VMEM((devices, token_cap, 3 * HEAD_DIM), jnp.bfloat16),
            pltpu.VMEM((devices, local_rows, HEAD_DIM), jnp.bfloat16),
            pltpu.VMEM(w_qkv.shape, w_qkv.dtype),
            pltpu.SemaphoreType.DMA(()),
        ],
        space=[pltpu.VMEM] * 2 + [pltpu.HBM] + [pltpu.VMEM] * devices,
    )
    weight_grad = call(
        sum_kernel, shape(width, 3 * inner // clips, dtype=jnp.float32), *weights
    )
    return attended[None], patch_grad[None], weight_grad


def solution(mesh):
    devices, clips = mesh.shape["seq"], mesh.shape["clip"]
    one_head_each = devices == HEADS and clips in (1, 2, 4, 8)
    return jax.shard_map(
        heads_plan if one_head_each else rows_plan,
        mesh=mesh,
        in_specs=(
            P("clip", "seq", None),
            P("clip", "seq"),
            P("clip", "seq"),
            P("clip", "seq"),
            P(),
            P("clip", "seq", None),
        ),
        out_specs=(P("clip", "seq", None), P("clip", "seq", None), P("seq", "clip")),
        check_vma=False,
    )
```

```python
import functools

import jax
import jax.numpy as jnp
from jax import lax
from jax.experimental import pallas as pl
from jax.experimental.pallas import tpu as pltpu
from jax.sharding import PartitionSpec as P

HEADS = 8
HEAD_DIM = 64


neg_large = -1e30


def split_heads(rows_in):
    return rows_in.reshape(rows_in.shape[0], HEADS, HEAD_DIM)


def forward_fold(query_heads, running, pieces):
    scaling = HEAD_DIM ** (-0.5)
    row_max, row_total, weighted = running
    key_heads = split_heads(pieces[0])
    value_heads = split_heads(pieces[1])
    scores = (
        jnp.einsum("rhd,khd->hrk", query_heads, key_heads, preferred_element_type=jnp.float32)
        * scaling
    )
    new_max = jnp.maximum(row_max, jnp.max(scores, axis=2))
    weights = jnp.exp(scores - new_max[:, :, None])
    row_total = jnp.sum(weights, axis=2)
    weighted = jnp.einsum(
        "hrk,khd->hrd",
        weights.astype(jnp.bfloat16),
        value_heads,
        preferred_element_type=jnp.float32,
    )
    return (new_max, row_total, weighted)


def query_fold(query_heads, grad_heads, log_total, grad_dot):
    scaling = HEAD_DIM ** (-0.5)

    def combine_piece(running, pieces, offset):
        key_heads = split_heads(pieces[0])
        value_heads = split_heads(pieces[1])
        scores = (
            jnp.einsum("rhd,khd->hrk", query_heads, key_heads, preferred_element_type=jnp.float32)
            * scaling
        )
        probability = jnp.exp(scores - log_total[:, :, None])
        prob_grad = jnp.einsum(
            "rhd,khd->hrk", grad_heads, value_heads, preferred_element_type=jnp.float32
        )
        score_grad = (probability * (prob_grad - grad_dot[:, :, None])).astype(jnp.bfloat16)
        return (
            jnp.einsum("hrk,khd->hrd", score_grad, key_heads, preferred_element_type=jnp.float32)
            * scaling
        )

    return combine_piece


def key_fold(key_heads, value_heads, all_log, all_dot, pieces):
    scaling = HEAD_DIM ** (-0.5)
    piece_query = split_heads(pieces[0])
    piece_grad = split_heads(pieces[1])
    piece_log = all_log.T
    piece_dot = all_dot.T
    scores = (
        jnp.einsum("qhd,khd->hqk", piece_query, key_heads, preferred_element_type=jnp.float32)
        * scaling
    )
    probability = jnp.exp(scores - piece_log[:, :, None])
    value_grad = jnp.einsum(
        "hqk,qhd->hkd",
        probability.astype(jnp.bfloat16),
        piece_grad,
        preferred_element_type=jnp.float32,
    )
    prob_grad = jnp.einsum(
        "qhd,khd->hqk", piece_grad, value_heads, preferred_element_type=jnp.float32
    )
    score_grad = (probability * (prob_grad - piece_dot[:, :, None])).astype(jnp.bfloat16)
    key_grad = (
        jnp.einsum("hqk,qhd->hkd", score_grad, piece_query, preferred_element_type=jnp.float32)
        * scaling
    )
    return (key_grad, value_grad)


def head_rows(matrix):
    return matrix.transpose(1, 0, 2).reshape(matrix.shape[1], HEADS * HEAD_DIM)


def rows_plan(patches, segment, dest_shard, dest_slot, w_qkv, out_grad):
    shard_count = lax.axis_size("seq")
    patch_rows = patches[0]
    patch_token = segment[0]
    targets = dest_shard[0]
    slot_ids = dest_slot[0]
    token_cap = targets.shape[0]
    pair_cap = token_cap // shard_count
    local_rows = out_grad.shape[1]
    inner_width = HEADS * HEAD_DIM
    member = (
        lax.broadcasted_iota(jnp.int32, (token_cap, patch_token.shape[0]), 0)
        == patch_token[None, :]
    )
    member_half = member.astype(jnp.bfloat16)
    counts = jnp.sum(member.astype(jnp.float32), axis=1)
    token_sums = jnp.dot(member_half, patch_rows, preferred_element_type=jnp.float32)
    tokens = (token_sums / jnp.maximum(counts, 1.0)[:, None]).astype(jnp.bfloat16)
    to_shard = (
        targets[:, None] == lax.broadcasted_iota(jnp.int32, (token_cap, shard_count), 1)
    ).astype(jnp.int32)
    ranking = jnp.sum((jnp.cumsum(to_shard, axis=0) - 1) * to_shard, axis=1)
    position = jnp.where(targets >= 0, targets * pair_cap + ranking, -1)
    chooser = position[None, :] == lax.broadcasted_iota(
        jnp.int32, (shard_count * pair_cap, token_cap), 0
    )
    chooser_half = chooser.astype(jnp.bfloat16)
    send_rows = jnp.dot(chooser_half, tokens, preferred_element_type=jnp.float32).astype(
        jnp.bfloat16
    )
    send_slot = jnp.sum(chooser.astype(jnp.int32) * (slot_ids + 1)[None, :], axis=1) - 1
    came_rows, came_slot = (
        lax.all_to_all(
            send_rows.reshape(shard_count, pair_cap, -1),
            "seq",
            split_axis=0,
            concat_axis=0,
            tiled=True,
        ),
        lax.all_to_all(
            send_slot.reshape(shard_count, pair_cap), "seq", split_axis=0, concat_axis=0, tiled=True
        ),
    )
    came_slot = came_slot.reshape(-1)
    placer = (
        came_slot[None, :]
        == lax.broadcasted_iota(jnp.int32, (local_rows, shard_count * pair_cap), 0)
    ).astype(jnp.bfloat16)
    placed = jnp.dot(
        placer, came_rows.reshape(shard_count * pair_cap, -1), preferred_element_type=jnp.float32
    ).astype(jnp.bfloat16)
    projected = jnp.dot(placed, w_qkv, preferred_element_type=jnp.float32).astype(jnp.bfloat16)
    query_rows = projected[:, :inner_width]
    key_rows = projected[:, inner_width : 2 * inner_width]
    value_rows = projected[:, 2 * inner_width :]
    query_heads = split_heads(query_rows)
    initial = (
        jnp.full((HEADS, local_rows), neg_large, jnp.float32),
        jnp.zeros((HEADS, local_rows), jnp.float32),
        jnp.zeros((HEADS, local_rows, HEAD_DIM), jnp.float32),
    )
    row_max, row_total, weighted = forward_fold(
        query_heads,
        initial,
        (
            lax.all_gather(key_rows, "seq", axis=0, tiled=True),
            lax.all_gather(value_rows, "seq", axis=0, tiled=True),
        ),
    )
    attended_rows = head_rows((weighted / row_total[:, :, None]).astype(jnp.bfloat16))
    grad_rows = out_grad[0]
    grad_heads = split_heads(grad_rows)
    log_total = row_max + jnp.log(row_total)
    grad_dot = jnp.sum(
        grad_heads.astype(jnp.float32) * split_heads(attended_rows).astype(jnp.float32), axis=2
    )
    blank = jnp.zeros((HEADS, local_rows, HEAD_DIM), jnp.float32)
    query_step = query_fold(query_heads, grad_heads, log_total, grad_dot.T)
    query_grad = query_step(
        blank,
        (
            lax.all_gather(key_rows, "seq", axis=0, tiled=True),
            lax.all_gather(value_rows, "seq", axis=0, tiled=True),
        ),
        jnp.int32(0),
    )
    all_log, all_dot = (
        lax.all_gather(log_total.T, "seq", axis=0, tiled=True),
        lax.all_gather(grad_dot, "seq", axis=0, tiled=True),
    )
    key_grad, value_grad = key_fold(
        split_heads(key_rows),
        split_heads(value_rows),
        all_log,
        all_dot,
        (
            lax.all_gather(query_rows, "seq", axis=0, tiled=True),
            lax.all_gather(grad_rows, "seq", axis=0, tiled=True),
        ),
    )
    proj_grad = jnp.concatenate(
        [head_rows(query_grad), head_rows(key_grad), head_rows(value_grad)], axis=1
    ).astype(jnp.bfloat16)
    placed_grad = jnp.einsum(
        "rc,dc->rd", proj_grad, w_qkv, preferred_element_type=jnp.float32
    ).astype(jnp.bfloat16)
    partial_value = jnp.einsum(
        "rd,rc->dc", placed, proj_grad, preferred_element_type=jnp.float32
    ).astype(jnp.bfloat16)
    across = lax.psum_scatter(partial_value, "seq", scatter_dimension=0, tiled=True).astype(
        jnp.float32
    )
    weight_grad = lax.psum_scatter(
        across.astype(jnp.bfloat16), "clip", scatter_dimension=1, tiled=True
    ).astype(jnp.float32)
    back_rows = jnp.einsum(
        "rj,rd->jd", placer, placed_grad, preferred_element_type=jnp.float32
    ).astype(jnp.bfloat16)
    returned = lax.all_to_all(
        back_rows.reshape(shard_count, pair_cap, -1), "seq", split_axis=0, concat_axis=0, tiled=True
    )
    token_grad = jnp.einsum(
        "jt,jd->td",
        chooser_half,
        returned.reshape(shard_count * pair_cap, -1),
        preferred_element_type=jnp.float32,
    ).astype(jnp.bfloat16)
    patch_sums = jnp.einsum(
        "tp,td->pd", member_half, token_grad, preferred_element_type=jnp.float32
    )
    patch_count = jnp.sum(member.astype(jnp.float32) * counts[:, None], axis=0)
    patch_grad = (patch_sums / patch_count[:, None]).astype(jnp.bfloat16)
    return (attended_rows[None], patch_grad[None], weight_grad)


VMEM_LIMIT = 40 * 1024 * 1024
NN = (((1,), (0,)), ((), ()))
NT = (((1,), (1,)), ((), ()))
TN = (((0,), (0,)), ((), ()))


def dot(left, right, dims=NN):
    return lax.dot_general(left, right, dims, preferred_element_type=jnp.float32)


def call(body, outs, *args, scratch=(), space=None, limit=VMEM_LIMIT, outer=None, alias={}, flops=0):
    space = space or [pltpu.VMEM] * len(args)
    return pl.pallas_call(
        body,
        out_shape=outs,
        in_specs=[pl.BlockSpec(memory_space=each) for each in space],
        out_specs=jax.tree.map(lambda _: pl.BlockSpec(memory_space=outer or pltpu.VMEM), outs),
        input_output_aliases=alias,
        scratch_shapes=scratch,
        cost_estimate=pl.CostEstimate(flops=flops, bytes_accessed=0, transcendentals=0),
        compiler_params=pltpu.CompilerParams(vmem_limit_bytes=limit),
    )(*args)


def one_hot(condition):
    return jnp.where(condition, 1.0, 0.0).astype(jnp.bfloat16)


def fold_half(rows):
    half = rows.shape[0] // 2
    return jnp.concatenate([rows[:half], rows[half:]], axis=1)


def unfold_half(rows):
    width = rows.shape[1] // 2
    return jnp.concatenate([rows[:, :width], rows[:, width:]], axis=0)


def wide_row(row):
    short = 256 - row.shape[1]
    wide = row.astype(jnp.float32)
    wide = jnp.concatenate([wide, jnp.full((1, short), -1.0, jnp.float32)], axis=1)
    return wide[:, :128], wide[:, 128:]


def token_kernel(*refs):
    sources, refs = refs[:6], refs[6:]
    sends, refs = refs[:HEADS], refs[HEADS:]
    (target_ref, segment_out, held_ref), refs = refs[:3], refs[3:]
    segment_ref, patch_ref, shard_ref, slot_ref, grad_ref, w_ref, done = refs
    pairs = list(zip(sources, refs))[:-1]
    for part in range(3):
        columns = pl.ds(part * grad_ref.shape[1], grad_ref.shape[1])
        pairs.append((sources[5].at[:, columns], w_ref.at[part]))
    copies = [
        pltpu.make_async_copy(source, held, done.at[index])
        for index, (source, held) in enumerate(pairs)
    ]
    for copy in copies:
        copy.start()
    token_cap = shard_ref.shape[1]
    local_rows, inner = grad_ref.shape
    devices = len(sends)
    width = patch_ref.shape[1] // devices
    copies[0].wait()
    segment = segment_ref[...]
    segment_out[...] = segment
    member = lax.broadcasted_iota(jnp.int32, (token_cap, segment.shape[1]), 0) == segment
    counts = jnp.sum(jnp.where(member, 1.0, 0.0), axis=1, keepdims=True)
    copies[1].wait()
    token_sums = dot(one_hot(member), patch_ref[...])
    tokens = (token_sums / jnp.maximum(counts, 1.0)).astype(jnp.bfloat16)
    for copy in copies[2:5]:
        copy.wait()
    shard, slot = shard_ref[...], slot_ref[...]
    target_ref[...] = jnp.where(shard >= 0, shard * local_rows + slot, -1)
    shard_low, shard_high = wide_row(shard)
    slot_low, slot_high = wide_row(slot)
    line = lax.broadcasted_iota(jnp.int32, (16, 128), 0)
    where_to = jnp.where(
        line == 0,
        shard_low,
        jnp.where(line == 1, shard_high, jnp.where(line == 2, slot_low, slot_high)),
    ).astype(jnp.bfloat16)
    grads = grad_ref[...]
    half = token_cap + token_cap // 2
    for head in range(devices):
        first = head * HEAD_DIM
        start = half
        for piece in (
            where_to,
            fold_half(grads[:, first : first + HEAD_DIM]),
            tokens[:, head * width : (head + 1) * width],
        ):
            held_ref[head, start : start + piece.shape[0]] = piece
            start += piece.shape[0]
    for part, copy in enumerate(copies[5:]):
        copy.wait()
        projected = dot(tokens, w_ref[part]).astype(jnp.bfloat16)
        for head in range(devices):
            rows = projected[:, head * HEAD_DIM : (head + 1) * HEAD_DIM]
            if part < 2:
                held_ref[head, :token_cap, part * HEAD_DIM : (part + 1) * HEAD_DIM] = rows
            else:
                held_ref[head, token_cap:half] = fold_half(rows)
    me = lax.axis_index("seq")
    for flip, send in enumerate(sends):
        send[...] = held_ref[jnp.bitwise_xor(me, flip)]


def target_row(lines, token_cap, local_rows):
    lines = lines.astype(jnp.float32)
    shard = jnp.concatenate([lines[0:1], lines[1:2]], axis=1)[:, :token_cap]
    slot = jnp.concatenate([lines[2:3], lines[3:4]], axis=1)[:, :token_cap]
    return (shard * local_rows + slot).astype(jnp.int32)


def place_rows(token_cap, rows, pieces, target_ref, grad_ref):
    local_rows = grad_ref.shape[1]
    lines_at = token_cap + token_cap // 2
    targets, rows_in = [], []
    for index, piece in enumerate(pieces):
        target = target_row(piece[lines_at : lines_at + 16], token_cap, local_rows)
        target_ref[index] = target
        targets.append(target)
        value = unfold_half(piece[token_cap:lines_at])
        rows_in.append(jnp.concatenate([piece[:token_cap], value], axis=1))
        grad_ref[index] = unfold_half(piece[lines_at + 16 : lines_at + 16 + local_rows // 2])
    row_id = lax.broadcasted_iota(jnp.int32, (rows, len(pieces) * token_cap), 0)
    placer = one_hot(row_id == jnp.concatenate(targets, axis=1))
    return dot(placer, jnp.concatenate(rows_in, axis=0))


def early_kernel(token_cap, *refs):
    pieces, (total_ref, target_ref, grad_ref) = refs[:-3], refs[-3:]
    total = place_rows(token_cap, total_ref.shape[0], pieces, target_ref, grad_ref)
    total_ref[...] = total.astype(jnp.bfloat16)


def head_kernel(token_cap, flips, early_ref, early_grad_ref, *refs):
    early = early_grad_ref.shape[0]
    pieces, refs = refs[: HEADS - early], refs[HEADS - early :]
    outs, (target_ref, late_grad_ref, grad_ref, attended_ref) = refs[: HEADS // 2], refs[HEADS // 2 :]
    devices, local_rows = len(flips), grad_ref.shape[1]
    rows = devices * local_rows
    scaling = HEAD_DIM ** (-0.5)
    me = lax.axis_index("seq")
    total = place_rows(token_cap, rows, pieces, target_ref, late_grad_ref)
    total = total + early_ref[...].astype(jnp.float32)
    for index, flip in enumerate(flips):
        came = early_grad_ref[index] if index < early else late_grad_ref[index - early]
        grad_ref[jnp.bitwise_xor(me, flip)] = came
    projected = total.astype(jnp.bfloat16)
    query = projected[:, :HEAD_DIM]
    key = projected[:, HEAD_DIM : 2 * HEAD_DIM]
    value = projected[:, 2 * HEAD_DIM :]
    grad = jnp.concatenate([grad_ref[place] for place in range(devices)], axis=0)
    scores = dot(key, query, NT) * scaling
    weights = jnp.exp(scores - jnp.max(scores, axis=0, keepdims=True))
    row_total = jnp.sum(weights, axis=0, keepdims=True)
    attended = (dot(value, weights.astype(jnp.bfloat16), TN) / row_total).astype(jnp.bfloat16)
    attended = attended.astype(jnp.float32)
    grad_dot = jnp.sum(grad.astype(jnp.float32).T * attended, axis=0, keepdims=True)
    probability = weights * (1.0 / row_total)
    score_grad = (probability * (dot(value, grad, NT) - grad_dot)).astype(jnp.bfloat16)
    value_grad = dot(probability.astype(jnp.bfloat16), grad)
    key_grad = dot(score_grad, query) * scaling
    query_grad = (dot(key, score_grad, TN) * scaling).T
    attended = attended.T.astype(jnp.bfloat16)
    for place in range(devices):
        attended_ref[place] = fold_half(attended[place * local_rows : (place + 1) * local_rows])
    proj_grad = jnp.concatenate([query_grad, key_grad], axis=1).astype(jnp.bfloat16)
    value_grad = fold_half(value_grad.astype(jnp.bfloat16))
    end = rows + rows // 2
    for chip, out in enumerate(outs):
        out[:rows] = proj_grad
        out[rows:end] = value_grad
        for core in range(2):
            first = end + core * local_rows // 2
            place = jnp.bitwise_xor(me, 2 * chip + core)
            out[first : first + local_rows // 2] = attended_ref[place]


def block_kernel(early_ref, late_ref, *refs):
    pieces, placed_ref = refs[:-1], refs[-1]
    early, _, token_cap = early_ref.shape
    rows = placed_ref.shape[1]
    targets = [early_ref[index] for index in range(early)]
    targets += [late_ref[index] for index in range(len(pieces) - early)]
    row_id = lax.broadcasted_iota(jnp.int32, (rows, len(pieces) * token_cap), 0)
    placer = one_hot(row_id == jnp.concatenate(targets, axis=1))
    rows_in = [piece[piece.shape[0] - token_cap :] for piece in pieces]
    placed_ref[...] = dot(placer, jnp.concatenate(rows_in, axis=0)).T.astype(jnp.bfloat16)


def head_columns(left, pieces):
    rows = left.shape[1]
    half, end = rows // 2, rows + rows // 2
    wide = 2 * HEAD_DIM
    both = dot(left, jnp.concatenate([piece[:rows] for piece in pieces], axis=1))
    folded = jnp.concatenate([piece[rows:end] for piece in pieces], axis=1)
    low, high = dot(left[:, :half], folded), dot(left[:, half:], folded)
    columns = []
    for first in range(0, both.shape[1], wide):
        value = low[:, first : first + HEAD_DIM] + high[:, first + HEAD_DIM : first + wide]
        columns.append(jnp.concatenate([both[:, first : first + wide], value], axis=1))
    return columns


def in_order(held_ref):
    return jnp.concatenate(
        [
            held_ref[head, :, part * HEAD_DIM : (part + 1) * HEAD_DIM]
            for part in range(3)
            for head in range(held_ref.shape[0])
        ],
        axis=1,
    )


def near_kernel(placed_ref, *refs):
    pieces, out_ref = refs[:-1], refs[-1]
    for index, columns in enumerate(head_columns(placed_ref[...], pieces)):
        out_ref[index] = columns.astype(jnp.bfloat16)


def weight_kernel(flips, placed_ref, near_ref, *refs):
    count = len(flips) - near_ref.shape[0]
    pieces, outs, (held_ref, block_ref) = refs[:count], refs[count:-2], refs[-2:]
    seq, clip = lax.axis_index("seq"), lax.axis_index("clip")
    columns = [near_ref[index] for index in range(near_ref.shape[0])]
    columns += head_columns(placed_ref[...], pieces)
    for flip, each in zip(flips, columns):
        held_ref[jnp.bitwise_xor(seq, flip)] = each.astype(jnp.bfloat16)
    columns = in_order(held_ref)
    width = columns.shape[1] // len(outs)
    for index in range(len(outs)):
        block_ref[index] = columns[:, index * width : (index + 1) * width]
    for flip, out in enumerate(outs):
        out[...] = block_ref[jnp.bitwise_xor(clip, flip)]


def patch_kernel(flips, segment_ref, target_ref, w_hbm, *refs):
    pieces, (patch_ref, attended_ref, held_ref, part_ref, w_ref, done) = refs[:HEADS], refs[HEADS:]
    copy = pltpu.make_async_copy(w_hbm, w_ref, done)
    copy.start()
    token_cap = target_ref.shape[1]
    local_rows = attended_ref.shape[0]
    rows = HEADS * local_rows
    me = lax.axis_index("seq")
    for flip, piece in zip(flips, pieces):
        first = rows + rows // 2 + flip % 2 * local_rows // 2
        part_ref[jnp.bitwise_xor(me, flip)] = unfold_half(piece[first : first + local_rows // 2])
    attended_ref[...] = jnp.concatenate([part_ref[head] for head in range(HEADS)], axis=1)
    row_id = lax.broadcasted_iota(jnp.int32, (rows, token_cap), 0)
    chooser = jnp.where(row_id == target_ref[...], 1.0, 0.0).T.astype(jnp.bfloat16)
    for flip, columns in zip(flips, head_columns(chooser, pieces)):
        held_ref[jnp.bitwise_xor(me, flip)] = columns.astype(jnp.bfloat16)
    proj_grad = in_order(held_ref)
    copy.wait()
    token_grad = dot(proj_grad, w_ref[...], NT).astype(jnp.bfloat16).astype(jnp.float32)
    member = (
        lax.broadcasted_iota(jnp.int32, (token_cap, segment_ref.shape[1]), 0) == segment_ref[...]
    )
    counts = jnp.sum(jnp.where(member, 1.0, 0.0), axis=1, keepdims=True)
    shared = (token_grad / jnp.maximum(counts, 1.0)).astype(jnp.bfloat16)
    patch_ref[...] = dot(one_hot(member), shared, TN).astype(jnp.bfloat16)


def follow_kernel(*refs):
    pass


def sum_kernel(*refs):
    total = refs[0][...].astype(jnp.float32)
    for ref in refs[1:-1]:
        total = total + ref[...].astype(jnp.float32)
    refs[-1][...] = total


def exchange(rows, axis, flip):
    count = lax.axis_size(axis)
    return lax.ppermute(rows, axis, [(index, index ^ flip) for index in range(count)])


def shape(*sizes, dtype=jnp.bfloat16):
    return jax.ShapeDtypeStruct(sizes, dtype)


def start_order(flip):
    steps = (flip // 2).bit_count()
    return flip > 0, -steps, flip % 2, -flip


def heads_plan(patches, segment, dest_shard, dest_slot, w_qkv, out_grad):
    devices = lax.axis_size("seq")
    clips = lax.axis_size("clip")
    token_cap = dest_shard.shape[1]
    local_rows, inner = out_grad.shape[1:]
    rows = devices * local_rows
    model = patches.shape[2]
    width = model // devices
    sent = token_cap + token_cap // 2 + 16 + local_rows // 2 + token_cap
    sources = (segment, patches[0], dest_shard, dest_slot, out_grad[0], w_qkv)
    outs = call(
        token_kernel,
        [shape(sent, 2 * HEAD_DIM)] * devices
        + [shape(1, token_cap, dtype=jnp.int32), shape(*segment.shape, dtype=jnp.int32)],
        *sources,
        scratch=[
            pltpu.VMEM((devices, sent, 2 * HEAD_DIM), jnp.bfloat16),
        ]
        + [pltpu.VMEM(source.shape, source.dtype) for source in sources[:-1]]
        + [
            pltpu.VMEM((3, model, inner), w_qkv.dtype),
            pltpu.SemaphoreType.DMA((len(sources) + 2,)),
        ],
        space=[pltpu.HBM] * len(sources),
        limit=62 * 1024 * 1024,
    )
    sends, (target, segment) = list(outs[:devices]), outs[devices:]
    order = sorted(range(devices), key=start_order)
    came = {0: sends[0]}
    for flip in order[1:]:
        came[flip] = exchange(sends[flip], "seq", flip)
    came = [came[flip] for flip in order]
    early = devices // 2
    placed, early_targets, early_grads = call(
        functools.partial(early_kernel, token_cap),
        [
            shape(rows, 3 * HEAD_DIM),
            shape(early, 1, token_cap, dtype=jnp.int32),
            shape(early, local_rows, HEAD_DIM),
        ],
        *came[:early],
        flops=1_000_000_000,
    )
    *proj, late_targets = call(
        functools.partial(head_kernel, token_cap, order),
        [shape(rows + rows // 2 + local_rows, 2 * HEAD_DIM)] * (devices // 2)
        + [shape(devices - early, 1, token_cap, dtype=jnp.int32)],
        placed,
        early_grads,
        *came[early:],
        scratch=[
            pltpu.VMEM((devices - early, local_rows, HEAD_DIM), jnp.bfloat16),
            pltpu.VMEM((devices, local_rows, HEAD_DIM), jnp.bfloat16),
            pltpu.VMEM((devices, local_rows // 2, 2 * HEAD_DIM), jnp.bfloat16),
        ],
    )
    pieces = {0: proj[0]}
    for flip in order[1:]:
        if flip % 2 == 0:
            pieces[flip] = exchange(proj[flip // 2], "seq", flip)
    placed = call(block_kernel, shape(width, rows), early_targets, late_targets, *came)
    first = devices // 2
    pieces[first] = call(
        follow_kernel,
        shape(*pieces[first].shape),
        pieces[first],
        placed,
        space=[pl.ANY] * 2,
        outer=pl.ANY,
        alias={0: 0},
    )
    for flip in list(pieces):
        pieces[flip + 1] = exchange(pieces[flip], "seq", 1)
    flips = [chip ^ core for chip in range(devices - 2, -1, -2) for core in range(2)]
    pieces = [pieces[flip] for flip in flips]
    far = [devices - 1]
    near = [flip for flip in order if flip not in far]
    columns = call(
        near_kernel,
        shape(len(near), width, 3 * HEAD_DIM),
        placed,
        *[pieces[flips.index(flip)] for flip in near],
    )
    weights = call(
        functools.partial(weight_kernel, near + far),
        [shape(width, 3 * inner // clips)] * clips,
        placed,
        columns,
        *[pieces[flips.index(flip)] for flip in far],
        scratch=[
            pltpu.VMEM((devices, width, 3 * HEAD_DIM), jnp.bfloat16),
            pltpu.VMEM((clips, width, 3 * inner // clips), jnp.bfloat16),
        ],
    )
    clip_flips = sorted(range(1, clips), key=lambda flip: (flip != clips // 2, flip))
    weights = [weights[0]] + [exchange(weights[flip], "clip", flip) for flip in clip_flips]
    patch_grad, attended = call(
        functools.partial(patch_kernel, flips),
        [shape(patches.shape[1], model), shape(local_rows, inner)],
        segment,
        target,
        w_qkv,
        *pieces,
        scratch=[
            pltpu.VMEM((devices, token_cap, 3 * HEAD_DIM), jnp.bfloat16),
            pltpu.VMEM((devices, local_rows, HEAD_DIM), jnp.bfloat16),
            pltpu.VMEM(w_qkv.shape, w_qkv.dtype),
            pltpu.SemaphoreType.DMA(()),
        ],
        space=[pltpu.VMEM] * 2 + [pltpu.HBM] + [pltpu.VMEM] * devices,
    )
    weight_grad = call(
        sum_kernel, shape(width, 3 * inner // clips, dtype=jnp.float32), *weights
    )
    return attended[None], patch_grad[None], weight_grad


def solution(mesh):
    devices, clips = mesh.shape["seq"], mesh.shape["clip"]
    one_head_each = devices == HEADS and clips in (1, 2, 4, 8)
    return jax.shard_map(
        heads_plan if one_head_each else rows_plan,
        mesh=mesh,
        in_specs=(
            P("clip", "seq", None),
            P("clip", "seq"),
            P("clip", "seq"),
            P("clip", "seq"),
            P(),
            P("clip", "seq", None),
        ),
        out_specs=(P("clip", "seq", None), P("clip", "seq", None), P("seq", "clip")),
        check_vma=False,
    )
```

```python
import functools

import jax
import jax.numpy as jnp
from jax import lax
from jax.experimental import pallas as pl
from jax.experimental.pallas import tpu as pltpu
from jax.sharding import PartitionSpec as P

HEADS = 8
HEAD_DIM = 64


neg_large = -1e30


def split_heads(rows_in):
    return rows_in.reshape(rows_in.shape[0], HEADS, HEAD_DIM)


def forward_fold(query_heads, running, pieces):
    scaling = HEAD_DIM ** (-0.5)
    row_max, row_total, weighted = running
    key_heads = split_heads(pieces[0])
    value_heads = split_heads(pieces[1])
    scores = (
        jnp.einsum("rhd,khd->hrk", query_heads, key_heads, preferred_element_type=jnp.float32)
        * scaling
    )
    new_max = jnp.maximum(row_max, jnp.max(scores, axis=2))
    weights = jnp.exp(scores - new_max[:, :, None])
    row_total = jnp.sum(weights, axis=2)
    weighted = jnp.einsum(
        "hrk,khd->hrd",
        weights.astype(jnp.bfloat16),
        value_heads,
        preferred_element_type=jnp.float32,
    )
    return (new_max, row_total, weighted)


def query_fold(query_heads, grad_heads, log_total, grad_dot):
    scaling = HEAD_DIM ** (-0.5)

    def combine_piece(running, pieces, offset):
        key_heads = split_heads(pieces[0])
        value_heads = split_heads(pieces[1])
        scores = (
            jnp.einsum("rhd,khd->hrk", query_heads, key_heads, preferred_element_type=jnp.float32)
            * scaling
        )
        probability = jnp.exp(scores - log_total[:, :, None])
        prob_grad = jnp.einsum(
            "rhd,khd->hrk", grad_heads, value_heads, preferred_element_type=jnp.float32
        )
        score_grad = (probability * (prob_grad - grad_dot[:, :, None])).astype(jnp.bfloat16)
        return (
            jnp.einsum("hrk,khd->hrd", score_grad, key_heads, preferred_element_type=jnp.float32)
            * scaling
        )

    return combine_piece


def key_fold(key_heads, value_heads, all_log, all_dot, pieces):
    scaling = HEAD_DIM ** (-0.5)
    piece_query = split_heads(pieces[0])
    piece_grad = split_heads(pieces[1])
    piece_log = all_log.T
    piece_dot = all_dot.T
    scores = (
        jnp.einsum("qhd,khd->hqk", piece_query, key_heads, preferred_element_type=jnp.float32)
        * scaling
    )
    probability = jnp.exp(scores - piece_log[:, :, None])
    value_grad = jnp.einsum(
        "hqk,qhd->hkd",
        probability.astype(jnp.bfloat16),
        piece_grad,
        preferred_element_type=jnp.float32,
    )
    prob_grad = jnp.einsum(
        "qhd,khd->hqk", piece_grad, value_heads, preferred_element_type=jnp.float32
    )
    score_grad = (probability * (prob_grad - piece_dot[:, :, None])).astype(jnp.bfloat16)
    key_grad = (
        jnp.einsum("hqk,qhd->hkd", score_grad, piece_query, preferred_element_type=jnp.float32)
        * scaling
    )
    return (key_grad, value_grad)


def head_rows(matrix):
    return matrix.transpose(1, 0, 2).reshape(matrix.shape[1], HEADS * HEAD_DIM)


def rows_plan(patches, segment, dest_shard, dest_slot, w_qkv, out_grad):
    shard_count = lax.axis_size("seq")
    patch_rows = patches[0]
    patch_token = segment[0]
    targets = dest_shard[0]
    slot_ids = dest_slot[0]
    token_cap = targets.shape[0]
    pair_cap = token_cap // shard_count
    local_rows = out_grad.shape[1]
    inner_width = HEADS * HEAD_DIM
    member = (
        lax.broadcasted_iota(jnp.int32, (token_cap, patch_token.shape[0]), 0)
        == patch_token[None, :]
    )
    member_half = member.astype(jnp.bfloat16)
    counts = jnp.sum(member.astype(jnp.float32), axis=1)
    token_sums = jnp.dot(member_half, patch_rows, preferred_element_type=jnp.float32)
    tokens = (token_sums / jnp.maximum(counts, 1.0)[:, None]).astype(jnp.bfloat16)
    to_shard = (
        targets[:, None] == lax.broadcasted_iota(jnp.int32, (token_cap, shard_count), 1)
    ).astype(jnp.int32)
    ranking = jnp.sum((jnp.cumsum(to_shard, axis=0) - 1) * to_shard, axis=1)
    position = jnp.where(targets >= 0, targets * pair_cap + ranking, -1)
    chooser = position[None, :] == lax.broadcasted_iota(
        jnp.int32, (shard_count * pair_cap, token_cap), 0
    )
    chooser_half = chooser.astype(jnp.bfloat16)
    send_rows = jnp.dot(chooser_half, tokens, preferred_element_type=jnp.float32).astype(
        jnp.bfloat16
    )
    send_slot = jnp.sum(chooser.astype(jnp.int32) * (slot_ids + 1)[None, :], axis=1) - 1
    came_rows, came_slot = (
        lax.all_to_all(
            send_rows.reshape(shard_count, pair_cap, -1),
            "seq",
            split_axis=0,
            concat_axis=0,
            tiled=True,
        ),
        lax.all_to_all(
            send_slot.reshape(shard_count, pair_cap), "seq", split_axis=0, concat_axis=0, tiled=True
        ),
    )
    came_slot = came_slot.reshape(-1)
    placer = (
        came_slot[None, :]
        == lax.broadcasted_iota(jnp.int32, (local_rows, shard_count * pair_cap), 0)
    ).astype(jnp.bfloat16)
    placed = jnp.dot(
        placer, came_rows.reshape(shard_count * pair_cap, -1), preferred_element_type=jnp.float32
    ).astype(jnp.bfloat16)
    projected = jnp.dot(placed, w_qkv, preferred_element_type=jnp.float32).astype(jnp.bfloat16)
    query_rows = projected[:, :inner_width]
    key_rows = projected[:, inner_width : 2 * inner_width]
    value_rows = projected[:, 2 * inner_width :]
    query_heads = split_heads(query_rows)
    initial = (
        jnp.full((HEADS, local_rows), neg_large, jnp.float32),
        jnp.zeros((HEADS, local_rows), jnp.float32),
        jnp.zeros((HEADS, local_rows, HEAD_DIM), jnp.float32),
    )
    row_max, row_total, weighted = forward_fold(
        query_heads,
        initial,
        (
            lax.all_gather(key_rows, "seq", axis=0, tiled=True),
            lax.all_gather(value_rows, "seq", axis=0, tiled=True),
        ),
    )
    attended_rows = head_rows((weighted / row_total[:, :, None]).astype(jnp.bfloat16))
    grad_rows = out_grad[0]
    grad_heads = split_heads(grad_rows)
    log_total = row_max + jnp.log(row_total)
    grad_dot = jnp.sum(
        grad_heads.astype(jnp.float32) * split_heads(attended_rows).astype(jnp.float32), axis=2
    )
    blank = jnp.zeros((HEADS, local_rows, HEAD_DIM), jnp.float32)
    query_step = query_fold(query_heads, grad_heads, log_total, grad_dot.T)
    query_grad = query_step(
        blank,
        (
            lax.all_gather(key_rows, "seq", axis=0, tiled=True),
            lax.all_gather(value_rows, "seq", axis=0, tiled=True),
        ),
        jnp.int32(0),
    )
    all_log, all_dot = (
        lax.all_gather(log_total.T, "seq", axis=0, tiled=True),
        lax.all_gather(grad_dot, "seq", axis=0, tiled=True),
    )
    key_grad, value_grad = key_fold(
        split_heads(key_rows),
        split_heads(value_rows),
        all_log,
        all_dot,
        (
            lax.all_gather(query_rows, "seq", axis=0, tiled=True),
            lax.all_gather(grad_rows, "seq", axis=0, tiled=True),
        ),
    )
    proj_grad = jnp.concatenate(
        [head_rows(query_grad), head_rows(key_grad), head_rows(value_grad)], axis=1
    ).astype(jnp.bfloat16)
    placed_grad = jnp.einsum(
        "rc,dc->rd", proj_grad, w_qkv, preferred_element_type=jnp.float32
    ).astype(jnp.bfloat16)
    partial_value = jnp.einsum(
        "rd,rc->dc", placed, proj_grad, preferred_element_type=jnp.float32
    ).astype(jnp.bfloat16)
    across = lax.psum_scatter(partial_value, "seq", scatter_dimension=0, tiled=True).astype(
        jnp.float32
    )
    weight_grad = lax.psum_scatter(
        across.astype(jnp.bfloat16), "clip", scatter_dimension=1, tiled=True
    ).astype(jnp.float32)
    back_rows = jnp.einsum(
        "rj,rd->jd", placer, placed_grad, preferred_element_type=jnp.float32
    ).astype(jnp.bfloat16)
    returned = lax.all_to_all(
        back_rows.reshape(shard_count, pair_cap, -1), "seq", split_axis=0, concat_axis=0, tiled=True
    )
    token_grad = jnp.einsum(
        "jt,jd->td",
        chooser_half,
        returned.reshape(shard_count * pair_cap, -1),
        preferred_element_type=jnp.float32,
    ).astype(jnp.bfloat16)
    patch_sums = jnp.einsum(
        "tp,td->pd", member_half, token_grad, preferred_element_type=jnp.float32
    )
    patch_count = jnp.sum(member.astype(jnp.float32) * counts[:, None], axis=0)
    patch_grad = (patch_sums / patch_count[:, None]).astype(jnp.bfloat16)
    return (attended_rows[None], patch_grad[None], weight_grad)


VMEM_LIMIT = 40 * 1024 * 1024
NN = (((1,), (0,)), ((), ()))
NT = (((1,), (1,)), ((), ()))
TN = (((0,), (0,)), ((), ()))


def dot(left, right, dims=NN):
    return lax.dot_general(left, right, dims, preferred_element_type=jnp.float32)


def call(body, outs, *args, scratch=(), space=None, limit=VMEM_LIMIT, outer=None, alias={}, flops=0):
    space = space or [pltpu.VMEM] * len(args)
    return pl.pallas_call(
        body,
        out_shape=outs,
        in_specs=[pl.BlockSpec(memory_space=each) for each in space],
        out_specs=jax.tree.map(lambda _: pl.BlockSpec(memory_space=outer or pltpu.VMEM), outs),
        input_output_aliases=alias,
        scratch_shapes=scratch,
        cost_estimate=pl.CostEstimate(flops=flops, bytes_accessed=0, transcendentals=0),
        compiler_params=pltpu.CompilerParams(vmem_limit_bytes=limit),
    )(*args)


def one_hot(condition):
    return jnp.where(condition, 1.0, 0.0).astype(jnp.bfloat16)


def fold_half(rows):
    half = rows.shape[0] // 2
    return jnp.concatenate([rows[:half], rows[half:]], axis=1)


def unfold_half(rows):
    width = rows.shape[1] // 2
    return jnp.concatenate([rows[:, :width], rows[:, width:]], axis=0)


def wide_row(row):
    short = 256 - row.shape[1]
    wide = row.astype(jnp.float32)
    wide = jnp.concatenate([wide, jnp.full((1, short), -1.0, jnp.float32)], axis=1)
    return wide[:, :128], wide[:, 128:]


def token_kernel(*refs):
    sources, refs = refs[:6], refs[6:]
    sends, refs = refs[:HEADS], refs[HEADS:]
    (target_ref, segment_out, held_ref), refs = refs[:3], refs[3:]
    segment_ref, patch_ref, shard_ref, slot_ref, grad_ref, w_ref, done = refs
    pairs = list(zip(sources, refs))[:-1]
    for part in range(3):
        columns = pl.ds(part * grad_ref.shape[1], grad_ref.shape[1])
        pairs.append((sources[5].at[:, columns], w_ref.at[part]))
    copies = [
        pltpu.make_async_copy(source, held, done.at[index])
        for index, (source, held) in enumerate(pairs)
    ]
    for copy in copies:
        copy.start()
    token_cap = shard_ref.shape[1]
    local_rows, inner = grad_ref.shape
    devices = len(sends)
    width = patch_ref.shape[1] // devices
    copies[0].wait()
    segment = segment_ref[...]
    segment_out[...] = segment
    member = lax.broadcasted_iota(jnp.int32, (token_cap, segment.shape[1]), 0) == segment
    counts = jnp.sum(jnp.where(member, 1.0, 0.0), axis=1, keepdims=True)
    copies[1].wait()
    token_sums = dot(one_hot(member), patch_ref[...])
    tokens = (token_sums / jnp.maximum(counts, 1.0)).astype(jnp.bfloat16)
    for copy in copies[2:5]:
        copy.wait()
    shard, slot = shard_ref[...], slot_ref[...]
    target_ref[...] = jnp.where(shard >= 0, shard * local_rows + slot, -1)
    shard_low, shard_high = wide_row(shard)
    slot_low, slot_high = wide_row(slot)
    line = lax.broadcasted_iota(jnp.int32, (16, 128), 0)
    where_to = jnp.where(
        line == 0,
        shard_low,
        jnp.where(line == 1, shard_high, jnp.where(line == 2, slot_low, slot_high)),
    ).astype(jnp.bfloat16)
    grads = grad_ref[...]
    half = token_cap + token_cap // 2
    for head in range(devices):
        first = head * HEAD_DIM
        start = half
        for piece in (
            where_to,
            fold_half(grads[:, first : first + HEAD_DIM]),
            tokens[:, head * width : (head + 1) * width],
        ):
            held_ref[head, start : start + piece.shape[0]] = piece
            start += piece.shape[0]
    for part, copy in enumerate(copies[5:]):
        copy.wait()
        projected = dot(tokens, w_ref[part]).astype(jnp.bfloat16)
        for head in range(devices):
            rows = projected[:, head * HEAD_DIM : (head + 1) * HEAD_DIM]
            if part < 2:
                held_ref[head, :token_cap, part * HEAD_DIM : (part + 1) * HEAD_DIM] = rows
            else:
                held_ref[head, token_cap:half] = fold_half(rows)
    me = lax.axis_index("seq")
    for flip, send in enumerate(sends):
        send[...] = held_ref[jnp.bitwise_xor(me, flip)]


def target_row(lines, token_cap, local_rows):
    lines = lines.astype(jnp.float32)
    shard = jnp.concatenate([lines[0:1], lines[1:2]], axis=1)[:, :token_cap]
    slot = jnp.concatenate([lines[2:3], lines[3:4]], axis=1)[:, :token_cap]
    return (shard * local_rows + slot).astype(jnp.int32)


def place_rows(token_cap, rows, pieces, target_ref, grad_ref):
    local_rows = grad_ref.shape[1]
    lines_at = token_cap + token_cap // 2
    targets, rows_in = [], []
    for index, piece in enumerate(pieces):
        target = target_row(piece[lines_at : lines_at + 16], token_cap, local_rows)
        target_ref[index] = target
        targets.append(target)
        value = unfold_half(piece[token_cap:lines_at])
        rows_in.append(jnp.concatenate([piece[:token_cap], value], axis=1))
        grad_ref[index] = unfold_half(piece[lines_at + 16 : lines_at + 16 + local_rows // 2])
    row_id = lax.broadcasted_iota(jnp.int32, (rows, len(pieces) * token_cap), 0)
    placer = one_hot(row_id == jnp.concatenate(targets, axis=1))
    return dot(placer, jnp.concatenate(rows_in, axis=0))


def early_kernel(token_cap, *refs):
    pieces, (total_ref, target_ref, grad_ref) = refs[:-3], refs[-3:]
    total = place_rows(token_cap, total_ref.shape[0], pieces, target_ref, grad_ref)
    total_ref[...] = total.astype(jnp.bfloat16)


def head_kernel(token_cap, flips, early_ref, early_grad_ref, *refs):
    early = early_grad_ref.shape[0]
    pieces, refs = refs[: HEADS - early], refs[HEADS - early :]
    outs, (target_ref, late_grad_ref, grad_ref, attended_ref) = refs[: HEADS // 2], refs[HEADS // 2 :]
    devices, local_rows = len(flips), grad_ref.shape[1]
    rows = devices * local_rows
    scaling = HEAD_DIM ** (-0.5)
    me = lax.axis_index("seq")
    total = place_rows(token_cap, rows, pieces, target_ref, late_grad_ref)
    total = total + early_ref[...].astype(jnp.float32)
    for index, flip in enumerate(flips):
        came = early_grad_ref[index] if index < early else late_grad_ref[index - early]
        grad_ref[jnp.bitwise_xor(me, flip)] = came
    projected = total.astype(jnp.bfloat16)
    query = projected[:, :HEAD_DIM]
    key = projected[:, HEAD_DIM : 2 * HEAD_DIM]
    value = projected[:, 2 * HEAD_DIM :]
    grad = jnp.concatenate([grad_ref[place] for place in range(devices)], axis=0)
    query = query * jnp.bfloat16(scaling)
    scores = dot(key, query, NT)
    weights = jnp.exp(scores - jnp.max(scores, axis=0, keepdims=True))
    row_total = jnp.sum(weights, axis=0, keepdims=True)
    inverse = 1.0 / row_total
    attended = (dot(value, weights.astype(jnp.bfloat16), TN) * inverse).astype(jnp.bfloat16)
    products = grad.T.astype(jnp.float32) * attended.astype(jnp.float32)
    grad_dot = jnp.sum(products, axis=0, keepdims=True)
    probability = weights * inverse
    score_grad = (probability * (dot(value, grad, NT) - grad_dot)).astype(jnp.bfloat16)
    value_grad = dot(probability.astype(jnp.bfloat16), grad)
    key_grad = dot(score_grad, query)
    query_grad = (dot(key, score_grad, TN) * scaling).astype(jnp.bfloat16).T
    attended = attended.T
    for place in range(devices):
        attended_ref[place] = fold_half(attended[place * local_rows : (place + 1) * local_rows])
    proj_grad = jnp.concatenate([query_grad, key_grad.astype(jnp.bfloat16)], axis=1)
    value_grad = fold_half(value_grad.astype(jnp.bfloat16))
    end = rows + rows // 2
    for chip, out in enumerate(outs):
        out[:rows] = proj_grad
        out[rows:end] = value_grad
        for core in range(2):
            first = end + core * local_rows // 2
            place = jnp.bitwise_xor(me, 2 * chip + core)
            out[first : first + local_rows // 2] = attended_ref[place]


def block_kernel(early_ref, late_ref, *refs):
    pieces, placed_ref = refs[:-1], refs[-1]
    early, _, token_cap = early_ref.shape
    rows = placed_ref.shape[1]
    targets = [early_ref[index] for index in range(early)]
    targets += [late_ref[index] for index in range(len(pieces) - early)]
    row_id = lax.broadcasted_iota(jnp.int32, (rows, len(pieces) * token_cap), 0)
    placer = one_hot(row_id == jnp.concatenate(targets, axis=1))
    rows_in = [piece[piece.shape[0] - token_cap :] for piece in pieces]
    placed_ref[...] = dot(placer, jnp.concatenate(rows_in, axis=0)).T.astype(jnp.bfloat16)


def head_columns(left, pieces):
    rows = left.shape[1]
    half, end = rows // 2, rows + rows // 2
    wide = 2 * HEAD_DIM
    both = dot(left, jnp.concatenate([piece[:rows] for piece in pieces], axis=1))
    folded = jnp.concatenate([piece[rows:end] for piece in pieces], axis=1)
    low, high = dot(left[:, :half], folded), dot(left[:, half:], folded)
    columns = []
    for first in range(0, both.shape[1], wide):
        value = low[:, first : first + HEAD_DIM] + high[:, first + HEAD_DIM : first + wide]
        columns.append(jnp.concatenate([both[:, first : first + wide], value], axis=1))
    return columns


def in_order(held_ref):
    return jnp.concatenate(
        [
            held_ref[head, :, part * HEAD_DIM : (part + 1) * HEAD_DIM]
            for part in range(3)
            for head in range(held_ref.shape[0])
        ],
        axis=1,
    )


def near_kernel(flips, last, placed_ref, *refs):
    pieces, outs, (held_ref, block_ref) = refs[: len(flips)], refs[len(flips) : -2], refs[-2:]
    seq, clip = lax.axis_index("seq"), lax.axis_index("clip")
    held_ref[jnp.bitwise_xor(seq, last)] = jnp.zeros(held_ref.shape[1:], held_ref.dtype)
    for flip, columns in zip(flips, head_columns(placed_ref[...], pieces)):
        held_ref[jnp.bitwise_xor(seq, flip)] = columns.astype(jnp.bfloat16)
    columns = in_order(held_ref)
    width = columns.shape[1] // len(outs)
    for index in range(len(outs)):
        block_ref[index] = columns[:, index * width : (index + 1) * width]
    for flip, out in enumerate(outs):
        out[...] = block_ref[jnp.bitwise_xor(clip, flip)]


def weight_kernel(last, placed_ref, piece_ref, *refs):
    count = len(refs) // 2
    head = jnp.bitwise_xor(lax.axis_index("seq"), last)
    columns = head_columns(placed_ref[...], [piece_ref])[0]
    width = refs[0].shape[1]
    groups = width // HEAD_DIM
    wide = [
        jnp.concatenate([columns[:, part * HEAD_DIM : (part + 1) * HEAD_DIM]] * groups, axis=1)
        for part in range(3)
    ]
    lane = lax.broadcasted_iota(jnp.int32, (1, width), 1)
    for flip in range(count):
        place = jnp.bitwise_xor(lax.axis_index("clip"), flip) * width + lane
        others = refs[flip][...].astype(jnp.float32)
        for part in range(3):
            first = (part * HEADS + head) * HEAD_DIM
            mine = (place >= first) & (place < first + HEAD_DIM)
            others = jnp.where(mine, wide[part], others)
        refs[count + flip][...] = others.astype(jnp.bfloat16)


def patch_kernel(flips, segment_ref, target_ref, w_hbm, *refs):
    pieces, (patch_ref, attended_ref, held_ref, part_ref, w_ref, done) = refs[:HEADS], refs[HEADS:]
    copy = pltpu.make_async_copy(w_hbm, w_ref, done)
    copy.start()
    token_cap = target_ref.shape[1]
    local_rows = attended_ref.shape[0]
    rows = HEADS * local_rows
    me = lax.axis_index("seq")
    for flip, piece in zip(flips, pieces):
        first = rows + rows // 2 + flip % 2 * local_rows // 2
        part_ref[jnp.bitwise_xor(me, flip)] = unfold_half(piece[first : first + local_rows // 2])
    attended_ref[...] = jnp.concatenate([part_ref[head] for head in range(HEADS)], axis=1)
    row_id = lax.broadcasted_iota(jnp.int32, (rows, token_cap), 0)
    chooser = jnp.where(row_id == target_ref[...], 1.0, 0.0).T.astype(jnp.bfloat16)
    for flip, columns in zip(flips, head_columns(chooser, pieces)):
        held_ref[jnp.bitwise_xor(me, flip)] = columns.astype(jnp.bfloat16)
    proj_grad = in_order(held_ref)
    copy.wait()
    token_grad = dot(proj_grad, w_ref[...], NT).astype(jnp.bfloat16).astype(jnp.float32)
    member = (
        lax.broadcasted_iota(jnp.int32, (token_cap, segment_ref.shape[1]), 0) == segment_ref[...]
    )
    counts = jnp.sum(jnp.where(member, 1.0, 0.0), axis=1, keepdims=True)
    shared = (token_grad / jnp.maximum(counts, 1.0)).astype(jnp.bfloat16)
    patch_ref[...] = dot(one_hot(member), shared, TN).astype(jnp.bfloat16)


def follow_kernel(*refs):
    pass


def sum_kernel(*refs):
    total = refs[0][...].astype(jnp.float32)
    for ref in refs[1:-1]:
        total = total + ref[...].astype(jnp.float32)
    refs[-1][...] = total


def exchange(rows, axis, flip):
    count = lax.axis_size(axis)
    return lax.ppermute(rows, axis, [(index, index ^ flip) for index in range(count)])


def shape(*sizes, dtype=jnp.bfloat16):
    return jax.ShapeDtypeStruct(sizes, dtype)


def start_order(flip):
    steps = (flip // 2).bit_count()
    return flip > 0, -steps, flip % 2, -flip


def heads_plan(patches, segment, dest_shard, dest_slot, w_qkv, out_grad):
    devices = lax.axis_size("seq")
    clips = lax.axis_size("clip")
    token_cap = dest_shard.shape[1]
    local_rows, inner = out_grad.shape[1:]
    rows = devices * local_rows
    model = patches.shape[2]
    width = model // devices
    sent = token_cap + token_cap // 2 + 16 + local_rows // 2 + token_cap
    sources = (segment, patches[0], dest_shard, dest_slot, out_grad[0], w_qkv)
    outs = call(
        token_kernel,
        [shape(sent, 2 * HEAD_DIM)] * devices
        + [shape(1, token_cap, dtype=jnp.int32), shape(*segment.shape, dtype=jnp.int32)],
        *sources,
        scratch=[
            pltpu.VMEM((devices, sent, 2 * HEAD_DIM), jnp.bfloat16),
        ]
        + [pltpu.VMEM(source.shape, source.dtype) for source in sources[:-1]]
        + [
            pltpu.VMEM((3, model, inner), w_qkv.dtype),
            pltpu.SemaphoreType.DMA((len(sources) + 2,)),
        ],
        space=[pltpu.HBM] * len(sources),
        limit=62 * 1024 * 1024,
    )
    sends, (target, segment) = list(outs[:devices]), outs[devices:]
    order = sorted(range(devices), key=start_order)
    came = {0: sends[0]}
    for flip in order[1:]:
        came[flip] = exchange(sends[flip], "seq", flip)
    came = [came[flip] for flip in order]
    early = devices // 2
    placed, early_targets, early_grads = call(
        functools.partial(early_kernel, token_cap),
        [
            shape(rows, 3 * HEAD_DIM),
            shape(early, 1, token_cap, dtype=jnp.int32),
            shape(early, local_rows, HEAD_DIM),
        ],
        *came[:early],
        flops=1_000_000_000,
    )
    *proj, late_targets = call(
        functools.partial(head_kernel, token_cap, order),
        [shape(rows + rows // 2 + local_rows, 2 * HEAD_DIM)] * (devices // 2)
        + [shape(devices - early, 1, token_cap, dtype=jnp.int32)],
        placed,
        early_grads,
        *came[early:],
        scratch=[
            pltpu.VMEM((devices - early, local_rows, HEAD_DIM), jnp.bfloat16),
            pltpu.VMEM((devices, local_rows, HEAD_DIM), jnp.bfloat16),
            pltpu.VMEM((devices, local_rows // 2, 2 * HEAD_DIM), jnp.bfloat16),
        ],
    )
    pieces = {0: proj[0]}
    for flip in order[1:]:
        if flip % 2 == 0:
            pieces[flip] = exchange(proj[flip // 2], "seq", flip)
    placed = call(block_kernel, shape(width, rows), early_targets, late_targets, *came)
    first = devices // 2
    pieces[first] = call(
        follow_kernel,
        shape(*pieces[first].shape),
        pieces[first],
        placed,
        space=[pl.ANY] * 2,
        outer=pl.ANY,
        alias={0: 0},
    )
    for flip in list(pieces):
        pieces[flip + 1] = exchange(pieces[flip], "seq", 1)
    flips = [chip ^ core for chip in range(devices - 2, -1, -2) for core in range(2)]
    pieces = [pieces[flip] for flip in flips]
    last = devices - 1
    near = [flip for flip in order if flip != last]
    blocks = [shape(width, 3 * inner // clips)] * clips
    weights = call(
        functools.partial(near_kernel, near, last),
        blocks,
        placed,
        *[pieces[flips.index(flip)] for flip in near],
        scratch=[
            pltpu.VMEM((devices, width, 3 * HEAD_DIM), jnp.bfloat16),
            pltpu.VMEM((clips, width, 3 * inner // clips), jnp.bfloat16),
        ],
    )
    weights = call(
        functools.partial(weight_kernel, last),
        blocks,
        placed,
        pieces[flips.index(last)],
        *weights,
    )
    clip_flips = sorted(range(1, clips), key=lambda flip: (flip != clips // 2, flip))
    weights = [weights[0]] + [exchange(weights[flip], "clip", flip) for flip in clip_flips]
    patch_grad, attended = call(
        functools.partial(patch_kernel, flips),
        [shape(patches.shape[1], model), shape(local_rows, inner)],
        segment,
        target,
        w_qkv,
        *pieces,
        scratch=[
            pltpu.VMEM((devices, token_cap, 3 * HEAD_DIM), jnp.bfloat16),
            pltpu.VMEM((devices, local_rows, HEAD_DIM), jnp.bfloat16),
            pltpu.VMEM(w_qkv.shape, w_qkv.dtype),
            pltpu.SemaphoreType.DMA(()),
        ],
        space=[pltpu.VMEM] * 2 + [pltpu.HBM] + [pltpu.VMEM] * devices,
    )
    weight_grad = call(
        sum_kernel, shape(width, 3 * inner // clips, dtype=jnp.float32), *weights
    )
    return attended[None], patch_grad[None], weight_grad


def solution(mesh):
    devices, clips = mesh.shape["seq"], mesh.shape["clip"]
    one_head_each = devices == HEADS and clips in (1, 2, 4, 8)
    return jax.shard_map(
        heads_plan if one_head_each else rows_plan,
        mesh=mesh,
        in_specs=(
            P("clip", "seq", None),
            P("clip", "seq"),
            P("clip", "seq"),
            P("clip", "seq"),
            P(),
            P("clip", "seq", None),
        ),
        out_specs=(P("clip", "seq", None), P("clip", "seq", None), P("seq", "clip")),
        check_vma=False,
    )
```

```python
import functools

import jax
import jax.numpy as jnp
from jax import lax
from jax.experimental import pallas as pl
from jax.experimental.pallas import tpu as pltpu
from jax.sharding import PartitionSpec as P

HEADS = 8
HEAD_DIM = 64


neg_large = -1e30


def split_heads(rows_in):
    return rows_in.reshape(rows_in.shape[0], HEADS, HEAD_DIM)


def forward_fold(query_heads, running, pieces):
    scaling = HEAD_DIM ** (-0.5)
    row_max, row_total, weighted = running
    key_heads = split_heads(pieces[0])
    value_heads = split_heads(pieces[1])
    scores = (
        jnp.einsum("rhd,khd->hrk", query_heads, key_heads, preferred_element_type=jnp.float32)
        * scaling
    )
    new_max = jnp.maximum(row_max, jnp.max(scores, axis=2))
    weights = jnp.exp(scores - new_max[:, :, None])
    row_total = jnp.sum(weights, axis=2)
    weighted = jnp.einsum(
        "hrk,khd->hrd",
        weights.astype(jnp.bfloat16),
        value_heads,
        preferred_element_type=jnp.float32,
    )
    return (new_max, row_total, weighted)


def query_fold(query_heads, grad_heads, log_total, grad_dot):
    scaling = HEAD_DIM ** (-0.5)

    def combine_piece(running, pieces, offset):
        key_heads = split_heads(pieces[0])
        value_heads = split_heads(pieces[1])
        scores = (
            jnp.einsum("rhd,khd->hrk", query_heads, key_heads, preferred_element_type=jnp.float32)
            * scaling
        )
        probability = jnp.exp(scores - log_total[:, :, None])
        prob_grad = jnp.einsum(
            "rhd,khd->hrk", grad_heads, value_heads, preferred_element_type=jnp.float32
        )
        score_grad = (probability * (prob_grad - grad_dot[:, :, None])).astype(jnp.bfloat16)
        return (
            jnp.einsum("hrk,khd->hrd", score_grad, key_heads, preferred_element_type=jnp.float32)
            * scaling
        )

    return combine_piece


def key_fold(key_heads, value_heads, all_log, all_dot, pieces):
    scaling = HEAD_DIM ** (-0.5)
    piece_query = split_heads(pieces[0])
    piece_grad = split_heads(pieces[1])
    piece_log = all_log.T
    piece_dot = all_dot.T
    scores = (
        jnp.einsum("qhd,khd->hqk", piece_query, key_heads, preferred_element_type=jnp.float32)
        * scaling
    )
    probability = jnp.exp(scores - piece_log[:, :, None])
    value_grad = jnp.einsum(
        "hqk,qhd->hkd",
        probability.astype(jnp.bfloat16),
        piece_grad,
        preferred_element_type=jnp.float32,
    )
    prob_grad = jnp.einsum(
        "qhd,khd->hqk", piece_grad, value_heads, preferred_element_type=jnp.float32
    )
    score_grad = (probability * (prob_grad - piece_dot[:, :, None])).astype(jnp.bfloat16)
    key_grad = (
        jnp.einsum("hqk,qhd->hkd", score_grad, piece_query, preferred_element_type=jnp.float32)
        * scaling
    )
    return (key_grad, value_grad)


def head_rows(matrix):
    return matrix.transpose(1, 0, 2).reshape(matrix.shape[1], HEADS * HEAD_DIM)


def rows_plan(patches, segment, dest_shard, dest_slot, w_qkv, out_grad):
    shard_count = lax.axis_size("seq")
    patch_rows = patches[0]
    patch_token = segment[0]
    targets = dest_shard[0]
    slot_ids = dest_slot[0]
    token_cap = targets.shape[0]
    pair_cap = token_cap // shard_count
    local_rows = out_grad.shape[1]
    inner_width = HEADS * HEAD_DIM
    member = (
        lax.broadcasted_iota(jnp.int32, (token_cap, patch_token.shape[0]), 0)
        == patch_token[None, :]
    )
    member_half = member.astype(jnp.bfloat16)
    counts = jnp.sum(member.astype(jnp.float32), axis=1)
    token_sums = jnp.dot(member_half, patch_rows, preferred_element_type=jnp.float32)
    tokens = (token_sums / jnp.maximum(counts, 1.0)[:, None]).astype(jnp.bfloat16)
    to_shard = (
        targets[:, None] == lax.broadcasted_iota(jnp.int32, (token_cap, shard_count), 1)
    ).astype(jnp.int32)
    ranking = jnp.sum((jnp.cumsum(to_shard, axis=0) - 1) * to_shard, axis=1)
    position = jnp.where(targets >= 0, targets * pair_cap + ranking, -1)
    chooser = position[None, :] == lax.broadcasted_iota(
        jnp.int32, (shard_count * pair_cap, token_cap), 0
    )
    chooser_half = chooser.astype(jnp.bfloat16)
    send_rows = jnp.dot(chooser_half, tokens, preferred_element_type=jnp.float32).astype(
        jnp.bfloat16
    )
    send_slot = jnp.sum(chooser.astype(jnp.int32) * (slot_ids + 1)[None, :], axis=1) - 1
    came_rows, came_slot = (
        lax.all_to_all(
            send_rows.reshape(shard_count, pair_cap, -1),
            "seq",
            split_axis=0,
            concat_axis=0,
            tiled=True,
        ),
        lax.all_to_all(
            send_slot.reshape(shard_count, pair_cap), "seq", split_axis=0, concat_axis=0, tiled=True
        ),
    )
    came_slot = came_slot.reshape(-1)
    placer = (
        came_slot[None, :]
        == lax.broadcasted_iota(jnp.int32, (local_rows, shard_count * pair_cap), 0)
    ).astype(jnp.bfloat16)
    placed = jnp.dot(
        placer, came_rows.reshape(shard_count * pair_cap, -1), preferred_element_type=jnp.float32
    ).astype(jnp.bfloat16)
    projected = jnp.dot(placed, w_qkv, preferred_element_type=jnp.float32).astype(jnp.bfloat16)
    query_rows = projected[:, :inner_width]
    key_rows = projected[:, inner_width : 2 * inner_width]
    value_rows = projected[:, 2 * inner_width :]
    query_heads = split_heads(query_rows)
    initial = (
        jnp.full((HEADS, local_rows), neg_large, jnp.float32),
        jnp.zeros((HEADS, local_rows), jnp.float32),
        jnp.zeros((HEADS, local_rows, HEAD_DIM), jnp.float32),
    )
    row_max, row_total, weighted = forward_fold(
        query_heads,
        initial,
        (
            lax.all_gather(key_rows, "seq", axis=0, tiled=True),
            lax.all_gather(value_rows, "seq", axis=0, tiled=True),
        ),
    )
    attended_rows = head_rows((weighted / row_total[:, :, None]).astype(jnp.bfloat16))
    grad_rows = out_grad[0]
    grad_heads = split_heads(grad_rows)
    log_total = row_max + jnp.log(row_total)
    grad_dot = jnp.sum(
        grad_heads.astype(jnp.float32) * split_heads(attended_rows).astype(jnp.float32), axis=2
    )
    blank = jnp.zeros((HEADS, local_rows, HEAD_DIM), jnp.float32)
    query_step = query_fold(query_heads, grad_heads, log_total, grad_dot.T)
    query_grad = query_step(
        blank,
        (
            lax.all_gather(key_rows, "seq", axis=0, tiled=True),
            lax.all_gather(value_rows, "seq", axis=0, tiled=True),
        ),
        jnp.int32(0),
    )
    all_log, all_dot = (
        lax.all_gather(log_total.T, "seq", axis=0, tiled=True),
        lax.all_gather(grad_dot, "seq", axis=0, tiled=True),
    )
    key_grad, value_grad = key_fold(
        split_heads(key_rows),
        split_heads(value_rows),
        all_log,
        all_dot,
        (
            lax.all_gather(query_rows, "seq", axis=0, tiled=True),
            lax.all_gather(grad_rows, "seq", axis=0, tiled=True),
        ),
    )
    proj_grad = jnp.concatenate(
        [head_rows(query_grad), head_rows(key_grad), head_rows(value_grad)], axis=1
    ).astype(jnp.bfloat16)
    placed_grad = jnp.einsum(
        "rc,dc->rd", proj_grad, w_qkv, preferred_element_type=jnp.float32
    ).astype(jnp.bfloat16)
    partial_value = jnp.einsum(
        "rd,rc->dc", placed, proj_grad, preferred_element_type=jnp.float32
    ).astype(jnp.bfloat16)
    across = lax.psum_scatter(partial_value, "seq", scatter_dimension=0, tiled=True).astype(
        jnp.float32
    )
    weight_grad = lax.psum_scatter(
        across.astype(jnp.bfloat16), "clip", scatter_dimension=1, tiled=True
    ).astype(jnp.float32)
    back_rows = jnp.einsum(
        "rj,rd->jd", placer, placed_grad, preferred_element_type=jnp.float32
    ).astype(jnp.bfloat16)
    returned = lax.all_to_all(
        back_rows.reshape(shard_count, pair_cap, -1), "seq", split_axis=0, concat_axis=0, tiled=True
    )
    token_grad = jnp.einsum(
        "jt,jd->td",
        chooser_half,
        returned.reshape(shard_count * pair_cap, -1),
        preferred_element_type=jnp.float32,
    ).astype(jnp.bfloat16)
    patch_sums = jnp.einsum(
        "tp,td->pd", member_half, token_grad, preferred_element_type=jnp.float32
    )
    patch_count = jnp.sum(member.astype(jnp.float32) * counts[:, None], axis=0)
    patch_grad = (patch_sums / patch_count[:, None]).astype(jnp.bfloat16)
    return (attended_rows[None], patch_grad[None], weight_grad)


VMEM_LIMIT = 40 * 1024 * 1024
NN = (((1,), (0,)), ((), ()))
NT = (((1,), (1,)), ((), ()))
TN = (((0,), (0,)), ((), ()))


def dot(left, right, dims=NN):
    return lax.dot_general(left, right, dims, preferred_element_type=jnp.float32)


def call(body, outs, *args, scratch=(), space=None, limit=VMEM_LIMIT, outer=None, alias={}, flops=0):
    space = space or [pltpu.VMEM] * len(args)
    return pl.pallas_call(
        body,
        out_shape=outs,
        in_specs=[pl.BlockSpec(memory_space=each) for each in space],
        out_specs=jax.tree.map(lambda _: pl.BlockSpec(memory_space=outer or pltpu.VMEM), outs),
        input_output_aliases=alias,
        scratch_shapes=scratch,
        cost_estimate=pl.CostEstimate(flops=flops, bytes_accessed=0, transcendentals=0),
        compiler_params=pltpu.CompilerParams(vmem_limit_bytes=limit),
    )(*args)


def one_hot(condition):
    return jnp.where(condition, 1.0, 0.0).astype(jnp.bfloat16)


def fold_half(rows):
    half = rows.shape[0] // 2
    return jnp.concatenate([rows[:half], rows[half:]], axis=1)


def unfold_half(rows):
    width = rows.shape[1] // 2
    return jnp.concatenate([rows[:, :width], rows[:, width:]], axis=0)


def wide_row(row):
    short = 256 - row.shape[1]
    wide = row.astype(jnp.float32)
    wide = jnp.concatenate([wide, jnp.full((1, short), -1.0, jnp.float32)], axis=1)
    return wide[:, :128], wide[:, 128:]


def token_kernel(*refs):
    sources, refs = refs[:6], refs[6:]
    sends, refs = refs[:HEADS], refs[HEADS:]
    (target_ref, segment_out, held_ref), refs = refs[:3], refs[3:]
    segment_ref, patch_ref, shard_ref, slot_ref, grad_ref, w_ref, done = refs
    pairs = list(zip(sources, refs))[:-1]
    for part in range(3):
        columns = pl.ds(part * grad_ref.shape[1], grad_ref.shape[1])
        pairs.append((sources[5].at[:, columns], w_ref.at[part]))
    copies = [
        pltpu.make_async_copy(source, held, done.at[index])
        for index, (source, held) in enumerate(pairs)
    ]
    for copy in copies:
        copy.start()
    token_cap = shard_ref.shape[1]
    local_rows, inner = grad_ref.shape
    devices = len(sends)
    width = patch_ref.shape[1] // devices
    copies[0].wait()
    segment = segment_ref[...]
    segment_out[...] = segment
    member = lax.broadcasted_iota(jnp.int32, (token_cap, segment.shape[1]), 0) == segment
    counts = jnp.sum(jnp.where(member, 1.0, 0.0), axis=1, keepdims=True)
    copies[1].wait()
    token_sums = dot(one_hot(member), patch_ref[...])
    tokens = (token_sums / jnp.maximum(counts, 1.0)).astype(jnp.bfloat16)
    for copy in copies[2:5]:
        copy.wait()
    shard, slot = shard_ref[...], slot_ref[...]
    target_ref[...] = jnp.where(shard >= 0, shard * local_rows + slot, -1)
    shard_low, shard_high = wide_row(shard)
    slot_low, slot_high = wide_row(slot)
    line = lax.broadcasted_iota(jnp.int32, (16, 128), 0)
    where_to = jnp.where(
        line == 0,
        shard_low,
        jnp.where(line == 1, shard_high, jnp.where(line == 2, slot_low, slot_high)),
    ).astype(jnp.bfloat16)
    grads = grad_ref[...]
    half = token_cap + token_cap // 2
    for head in range(devices):
        first = head * HEAD_DIM
        start = half
        for piece in (
            where_to,
            fold_half(grads[:, first : first + HEAD_DIM]),
            tokens[:, head * width : (head + 1) * width],
        ):
            held_ref[head, start : start + piece.shape[0]] = piece
            start += piece.shape[0]
    for part, copy in enumerate(copies[5:]):
        copy.wait()
        projected = dot(tokens, w_ref[part]).astype(jnp.bfloat16)
        for head in range(devices):
            rows = projected[:, head * HEAD_DIM : (head + 1) * HEAD_DIM]
            if part < 2:
                held_ref[head, :token_cap, part * HEAD_DIM : (part + 1) * HEAD_DIM] = rows
            else:
                held_ref[head, token_cap:half] = fold_half(rows)
    me = lax.axis_index("seq")
    for flip, send in enumerate(sends):
        send[...] = held_ref[jnp.bitwise_xor(me, flip)]


def target_row(lines, token_cap, local_rows):
    lines = lines.astype(jnp.float32)
    shard = jnp.concatenate([lines[0:1], lines[1:2]], axis=1)[:, :token_cap]
    slot = jnp.concatenate([lines[2:3], lines[3:4]], axis=1)[:, :token_cap]
    return (shard * local_rows + slot).astype(jnp.int32)


def place_rows(token_cap, rows, pieces, target_ref, grad_ref):
    local_rows = grad_ref.shape[1]
    lines_at = token_cap + token_cap // 2
    targets, rows_in = [], []
    for index, piece in enumerate(pieces):
        target = target_row(piece[lines_at : lines_at + 16], token_cap, local_rows)
        target_ref[index] = target
        targets.append(target)
        value = unfold_half(piece[token_cap:lines_at])
        rows_in.append(jnp.concatenate([piece[:token_cap], value], axis=1))
        grad_ref[index] = unfold_half(piece[lines_at + 16 : lines_at + 16 + local_rows // 2])
    row_id = lax.broadcasted_iota(jnp.int32, (rows, len(pieces) * token_cap), 0)
    placer = one_hot(row_id == jnp.concatenate(targets, axis=1))
    return dot(placer, jnp.concatenate(rows_in, axis=0))


def early_kernel(token_cap, *refs):
    pieces, (total_ref, target_ref, grad_ref) = refs[:-3], refs[-3:]
    total = place_rows(token_cap, total_ref.shape[0], pieces, target_ref, grad_ref)
    total_ref[...] = total.astype(jnp.bfloat16)


def head_kernel(token_cap, flips, early_ref, early_grad_ref, *refs):
    early = early_grad_ref.shape[0]
    pieces, refs = refs[: HEADS - early], refs[HEADS - early :]
    outs, (target_ref, late_grad_ref, grad_ref, attended_ref) = refs[: HEADS // 2], refs[HEADS // 2 :]
    devices, local_rows = len(flips), grad_ref.shape[1]
    rows = devices * local_rows
    scaling = HEAD_DIM ** (-0.5)
    me = lax.axis_index("seq")
    total = place_rows(token_cap, rows, pieces, target_ref, late_grad_ref)
    total = total + early_ref[...].astype(jnp.float32)
    for index, flip in enumerate(flips):
        came = early_grad_ref[index] if index < early else late_grad_ref[index - early]
        grad_ref[jnp.bitwise_xor(me, flip)] = came
    projected = total.astype(jnp.bfloat16)
    query = projected[:, :HEAD_DIM]
    key = projected[:, HEAD_DIM : 2 * HEAD_DIM]
    value = projected[:, 2 * HEAD_DIM :]
    grad = jnp.concatenate([grad_ref[place] for place in range(devices)], axis=0)
    query = query * jnp.bfloat16(scaling)
    scores = dot(key, query, NT)
    weights = jnp.exp(scores - jnp.max(scores, axis=0, keepdims=True))
    row_total = jnp.sum(weights, axis=0, keepdims=True)
    inverse = 1.0 / row_total
    attended = (dot(value, weights.astype(jnp.bfloat16), TN) * inverse).astype(jnp.bfloat16)
    products = grad.T.astype(jnp.float32) * attended.astype(jnp.float32)
    grad_dot = jnp.sum(products, axis=0, keepdims=True)
    probability = weights * inverse
    score_grad = (probability * (dot(value, grad, NT) - grad_dot)).astype(jnp.bfloat16)
    value_grad = dot(probability.astype(jnp.bfloat16), grad)
    key_grad = dot(score_grad, query)
    query_grad = (dot(key, score_grad, TN) * scaling).astype(jnp.bfloat16).T
    attended = attended.T
    for place in range(devices):
        attended_ref[place] = fold_half(attended[place * local_rows : (place + 1) * local_rows])
    proj_grad = jnp.concatenate([query_grad, key_grad.astype(jnp.bfloat16)], axis=1)
    value_grad = fold_half(value_grad.astype(jnp.bfloat16))
    end = rows + rows // 2
    for chip, out in enumerate(outs):
        out[:rows] = proj_grad
        out[rows:end] = value_grad
        for core in range(2):
            first = end + core * local_rows // 2
            place = jnp.bitwise_xor(me, 2 * chip + core)
            out[first : first + local_rows // 2] = attended_ref[place]


def block_kernel(early_ref, late_ref, *refs):
    pieces, placed_ref = refs[:-1], refs[-1]
    early, _, token_cap = early_ref.shape
    rows = placed_ref.shape[1]
    targets = [early_ref[index] for index in range(early)]
    targets += [late_ref[index] for index in range(len(pieces) - early)]
    row_id = lax.broadcasted_iota(jnp.int32, (rows, len(pieces) * token_cap), 0)
    placer = one_hot(row_id == jnp.concatenate(targets, axis=1))
    rows_in = [piece[piece.shape[0] - token_cap :] for piece in pieces]
    placed_ref[...] = dot(placer, jnp.concatenate(rows_in, axis=0)).T.astype(jnp.bfloat16)


def head_columns(left, pieces):
    rows = left.shape[1]
    half, end = rows // 2, rows + rows // 2
    wide = 2 * HEAD_DIM
    both = dot(left, jnp.concatenate([piece[:rows] for piece in pieces], axis=1))
    folded = jnp.concatenate([piece[rows:end] for piece in pieces], axis=1)
    low, high = dot(left[:, :half], folded), dot(left[:, half:], folded)
    columns = []
    for first in range(0, both.shape[1], wide):
        value = low[:, first : first + HEAD_DIM] + high[:, first + HEAD_DIM : first + wide]
        columns.append(jnp.concatenate([both[:, first : first + wide], value], axis=1))
    return columns


def in_order(held_ref):
    return jnp.concatenate(
        [
            held_ref[head, :, part * HEAD_DIM : (part + 1) * HEAD_DIM]
            for part in range(3)
            for head in range(held_ref.shape[0])
        ],
        axis=1,
    )


def near_kernel(flips, last, placed_ref, *refs):
    pieces, outs, (held_ref, block_ref) = refs[: len(flips)], refs[len(flips) : -2], refs[-2:]
    seq, clip = lax.axis_index("seq"), lax.axis_index("clip")
    held_ref[jnp.bitwise_xor(seq, last)] = jnp.zeros(held_ref.shape[1:], held_ref.dtype)
    for flip, columns in zip(flips, head_columns(placed_ref[...], pieces)):
        held_ref[jnp.bitwise_xor(seq, flip)] = columns.astype(jnp.bfloat16)
    columns = in_order(held_ref)
    width = columns.shape[1] // len(outs)
    for index in range(len(outs)):
        block_ref[index] = columns[:, index * width : (index + 1) * width]
    for flip, out in enumerate(outs):
        out[...] = block_ref[jnp.bitwise_xor(clip, flip)]


def weight_kernel(last, placed_ref, piece_ref, *refs):
    count = len(refs) // 2
    head = jnp.bitwise_xor(lax.axis_index("seq"), last)
    columns = head_columns(placed_ref[...], [piece_ref])[0]
    width = refs[0].shape[1]
    groups = width // HEAD_DIM
    wide = [
        jnp.concatenate([columns[:, part * HEAD_DIM : (part + 1) * HEAD_DIM]] * groups, axis=1)
        for part in range(3)
    ]
    lane = lax.broadcasted_iota(jnp.int32, (1, width), 1)
    for flip in range(count):
        place = jnp.bitwise_xor(lax.axis_index("clip"), flip) * width + lane
        others = refs[flip][...].astype(jnp.float32)
        for part in range(3):
            first = (part * HEADS + head) * HEAD_DIM
            mine = (place >= first) & (place < first + HEAD_DIM)
            others = jnp.where(mine, wide[part], others)
        refs[count + flip][...] = others.astype(jnp.bfloat16)


def patch_kernel(flips, segment_ref, target_ref, w_hbm, *refs):
    pieces, (patch_ref, attended_ref, held_ref, part_ref, w_ref, done) = refs[:HEADS], refs[HEADS:]
    copy = pltpu.make_async_copy(w_hbm, w_ref, done)
    copy.start()
    token_cap = target_ref.shape[1]
    local_rows = attended_ref.shape[0]
    rows = HEADS * local_rows
    me = lax.axis_index("seq")
    for flip, piece in zip(flips, pieces):
        first = rows + rows // 2 + flip % 2 * local_rows // 2
        part_ref[jnp.bitwise_xor(me, flip)] = unfold_half(piece[first : first + local_rows // 2])
    attended_ref[...] = jnp.concatenate([part_ref[head] for head in range(HEADS)], axis=1)
    row_id = lax.broadcasted_iota(jnp.int32, (rows, token_cap), 0)
    chooser = jnp.where(row_id == target_ref[...], 1.0, 0.0).T.astype(jnp.bfloat16)
    for flip, columns in zip(flips, head_columns(chooser, pieces)):
        held_ref[jnp.bitwise_xor(me, flip)] = columns.astype(jnp.bfloat16)
    proj_grad = in_order(held_ref)
    copy.wait()
    token_grad = dot(proj_grad, w_ref[...], NT).astype(jnp.bfloat16).astype(jnp.float32)
    member = (
        lax.broadcasted_iota(jnp.int32, (token_cap, segment_ref.shape[1]), 0) == segment_ref[...]
    )
    counts = jnp.sum(jnp.where(member, 1.0, 0.0), axis=1, keepdims=True)
    shared = (token_grad / jnp.maximum(counts, 1.0)).astype(jnp.bfloat16)
    patch_ref[...] = dot(one_hot(member), shared, TN).astype(jnp.bfloat16)


def follow_kernel(*refs):
    pass


def sum_kernel(*refs):
    total = refs[0][...].astype(jnp.float32)
    for ref in refs[1:-1]:
        total = total + ref[...].astype(jnp.float32)
    refs[-1][...] = total


def exchange(rows, axis, flip):
    count = lax.axis_size(axis)
    return lax.ppermute(rows, axis, [(index, index ^ flip) for index in range(count)])


def shape(*sizes, dtype=jnp.bfloat16):
    return jax.ShapeDtypeStruct(sizes, dtype)


def start_order(flip):
    steps = (flip // 2).bit_count()
    return flip > 0, -steps, flip % 2, -flip


def heads_plan(patches, segment, dest_shard, dest_slot, w_qkv, out_grad):
    devices = lax.axis_size("seq")
    clips = lax.axis_size("clip")
    token_cap = dest_shard.shape[1]
    local_rows, inner = out_grad.shape[1:]
    rows = devices * local_rows
    model = patches.shape[2]
    width = model // devices
    sent = token_cap + token_cap // 2 + 16 + local_rows // 2 + token_cap
    sources = (segment, patches[0], dest_shard, dest_slot, out_grad[0], w_qkv)
    outs = call(
        token_kernel,
        [shape(sent, 2 * HEAD_DIM)] * devices
        + [shape(1, token_cap, dtype=jnp.int32), shape(*segment.shape, dtype=jnp.int32)],
        *sources,
        scratch=[
            pltpu.VMEM((devices, sent, 2 * HEAD_DIM), jnp.bfloat16),
        ]
        + [pltpu.VMEM(source.shape, source.dtype) for source in sources[:-1]]
        + [
            pltpu.VMEM((3, model, inner), w_qkv.dtype),
            pltpu.SemaphoreType.DMA((len(sources) + 2,)),
        ],
        space=[pltpu.HBM] * len(sources),
        limit=62 * 1024 * 1024,
    )
    sends, (target, segment) = list(outs[:devices]), outs[devices:]
    order = sorted(range(devices), key=start_order)
    came = {0: sends[0]}
    for flip in order[1:]:
        came[flip] = exchange(sends[flip], "seq", flip)
    came = [came[flip] for flip in order]
    early = devices // 2 + 1
    placed, early_targets, early_grads = call(
        functools.partial(early_kernel, token_cap),
        [
            shape(rows, 3 * HEAD_DIM),
            shape(early, 1, token_cap, dtype=jnp.int32),
            shape(early, local_rows, HEAD_DIM),
        ],
        *came[:early],
        flops=1_000_000_000,
    )
    *proj, late_targets = call(
        functools.partial(head_kernel, token_cap, order),
        [shape(rows + rows // 2 + local_rows, 2 * HEAD_DIM)] * (devices // 2)
        + [shape(devices - early, 1, token_cap, dtype=jnp.int32)],
        placed,
        early_grads,
        *came[early:],
        scratch=[
            pltpu.VMEM((devices - early, local_rows, HEAD_DIM), jnp.bfloat16),
            pltpu.VMEM((devices, local_rows, HEAD_DIM), jnp.bfloat16),
            pltpu.VMEM((devices, local_rows // 2, 2 * HEAD_DIM), jnp.bfloat16),
        ],
    )
    pieces = {0: proj[0]}
    for flip in order[1:]:
        if flip % 2 == 0:
            pieces[flip] = exchange(proj[flip // 2], "seq", flip)
    placed = call(block_kernel, shape(width, rows), early_targets, late_targets, *came)
    first = devices // 2
    pieces[first] = call(
        follow_kernel,
        shape(*pieces[first].shape),
        pieces[first],
        placed,
        space=[pl.ANY] * 2,
        outer=pl.ANY,
        alias={0: 0},
    )
    for flip in list(pieces):
        pieces[flip + 1] = exchange(pieces[flip], "seq", 1)
    flips = [chip ^ core for chip in range(devices - 2, -1, -2) for core in range(2)]
    pieces = [pieces[flip] for flip in flips]
    last = devices - 1
    near = [flip for flip in order if flip != last]
    blocks = [shape(width, 3 * inner // clips)] * clips
    weights = call(
        functools.partial(near_kernel, near, last),
        blocks,
        placed,
        *[pieces[flips.index(flip)] for flip in near],
        scratch=[
            pltpu.VMEM((devices, width, 3 * HEAD_DIM), jnp.bfloat16),
            pltpu.VMEM((clips, width, 3 * inner // clips), jnp.bfloat16),
        ],
    )
    weights = call(
        functools.partial(weight_kernel, last),
        blocks,
        placed,
        pieces[flips.index(last)],
        *weights,
    )
    clip_flips = sorted(range(1, clips), key=lambda flip: (flip != clips // 2, flip))
    weights = [weights[0]] + [exchange(weights[flip], "clip", flip) for flip in clip_flips]
    patch_grad, attended = call(
        functools.partial(patch_kernel, flips),
        [shape(patches.shape[1], model), shape(local_rows, inner)],
        segment,
        target,
        w_qkv,
        *pieces,
        scratch=[
            pltpu.VMEM((devices, token_cap, 3 * HEAD_DIM), jnp.bfloat16),
            pltpu.VMEM((devices, local_rows, HEAD_DIM), jnp.bfloat16),
            pltpu.VMEM(w_qkv.shape, w_qkv.dtype),
            pltpu.SemaphoreType.DMA(()),
        ],
        space=[pltpu.VMEM] * 2 + [pltpu.HBM] + [pltpu.VMEM] * devices,
    )
    weight_grad = call(
        sum_kernel, shape(width, 3 * inner // clips, dtype=jnp.float32), *weights
    )
    return attended[None], patch_grad[None], weight_grad


def solution(mesh):
    devices, clips = mesh.shape["seq"], mesh.shape["clip"]
    one_head_each = devices == HEADS and clips in (1, 2, 4, 8)
    return jax.shard_map(
        heads_plan if one_head_each else rows_plan,
        mesh=mesh,
        in_specs=(
            P("clip", "seq", None),
            P("clip", "seq"),
            P("clip", "seq"),
            P("clip", "seq"),
            P(),
            P("clip", "seq", None),
        ),
        out_specs=(P("clip", "seq", None), P("clip", "seq", None), P("seq", "clip")),
        check_vma=False,
    )
```

```python
import functools

import jax
import jax.numpy as jnp
from jax import lax
from jax.experimental import pallas as pl
from jax.experimental.pallas import tpu as pltpu
from jax.sharding import PartitionSpec as P

HEADS = 8
HEAD_DIM = 64


neg_large = -1e30


def split_heads(rows_in):
    return rows_in.reshape(rows_in.shape[0], HEADS, HEAD_DIM)


def forward_fold(query_heads, running, pieces):
    scaling = HEAD_DIM ** (-0.5)
    row_max, row_total, weighted = running
    key_heads = split_heads(pieces[0])
    value_heads = split_heads(pieces[1])
    scores = (
        jnp.einsum("rhd,khd->hrk", query_heads, key_heads, preferred_element_type=jnp.float32)
        * scaling
    )
    new_max = jnp.maximum(row_max, jnp.max(scores, axis=2))
    weights = jnp.exp(scores - new_max[:, :, None])
    row_total = jnp.sum(weights, axis=2)
    weighted = jnp.einsum(
        "hrk,khd->hrd",
        weights.astype(jnp.bfloat16),
        value_heads,
        preferred_element_type=jnp.float32,
    )
    return (new_max, row_total, weighted)


def query_fold(query_heads, grad_heads, log_total, grad_dot):
    scaling = HEAD_DIM ** (-0.5)

    def combine_piece(running, pieces, offset):
        key_heads = split_heads(pieces[0])
        value_heads = split_heads(pieces[1])
        scores = (
            jnp.einsum("rhd,khd->hrk", query_heads, key_heads, preferred_element_type=jnp.float32)
            * scaling
        )
        probability = jnp.exp(scores - log_total[:, :, None])
        prob_grad = jnp.einsum(
            "rhd,khd->hrk", grad_heads, value_heads, preferred_element_type=jnp.float32
        )
        score_grad = (probability * (prob_grad - grad_dot[:, :, None])).astype(jnp.bfloat16)
        return (
            jnp.einsum("hrk,khd->hrd", score_grad, key_heads, preferred_element_type=jnp.float32)
            * scaling
        )

    return combine_piece


def key_fold(key_heads, value_heads, all_log, all_dot, pieces):
    scaling = HEAD_DIM ** (-0.5)
    piece_query = split_heads(pieces[0])
    piece_grad = split_heads(pieces[1])
    piece_log = all_log.T
    piece_dot = all_dot.T
    scores = (
        jnp.einsum("qhd,khd->hqk", piece_query, key_heads, preferred_element_type=jnp.float32)
        * scaling
    )
    probability = jnp.exp(scores - piece_log[:, :, None])
    value_grad = jnp.einsum(
        "hqk,qhd->hkd",
        probability.astype(jnp.bfloat16),
        piece_grad,
        preferred_element_type=jnp.float32,
    )
    prob_grad = jnp.einsum(
        "qhd,khd->hqk", piece_grad, value_heads, preferred_element_type=jnp.float32
    )
    score_grad = (probability * (prob_grad - piece_dot[:, :, None])).astype(jnp.bfloat16)
    key_grad = (
        jnp.einsum("hqk,qhd->hkd", score_grad, piece_query, preferred_element_type=jnp.float32)
        * scaling
    )
    return (key_grad, value_grad)


def head_rows(matrix):
    return matrix.transpose(1, 0, 2).reshape(matrix.shape[1], HEADS * HEAD_DIM)


def rows_plan(patches, segment, dest_shard, dest_slot, w_qkv, out_grad):
    shard_count = lax.axis_size("seq")
    patch_rows = patches[0]
    patch_token = segment[0]
    targets = dest_shard[0]
    slot_ids = dest_slot[0]
    token_cap = targets.shape[0]
    pair_cap = token_cap // shard_count
    local_rows = out_grad.shape[1]
    inner_width = HEADS * HEAD_DIM
    member = (
        lax.broadcasted_iota(jnp.int32, (token_cap, patch_token.shape[0]), 0)
        == patch_token[None, :]
    )
    member_half = member.astype(jnp.bfloat16)
    counts = jnp.sum(member.astype(jnp.float32), axis=1)
    token_sums = jnp.dot(member_half, patch_rows, preferred_element_type=jnp.float32)
    tokens = (token_sums / jnp.maximum(counts, 1.0)[:, None]).astype(jnp.bfloat16)
    to_shard = (
        targets[:, None] == lax.broadcasted_iota(jnp.int32, (token_cap, shard_count), 1)
    ).astype(jnp.int32)
    ranking = jnp.sum((jnp.cumsum(to_shard, axis=0) - 1) * to_shard, axis=1)
    position = jnp.where(targets >= 0, targets * pair_cap + ranking, -1)
    chooser = position[None, :] == lax.broadcasted_iota(
        jnp.int32, (shard_count * pair_cap, token_cap), 0
    )
    chooser_half = chooser.astype(jnp.bfloat16)
    send_rows = jnp.dot(chooser_half, tokens, preferred_element_type=jnp.float32).astype(
        jnp.bfloat16
    )
    send_slot = jnp.sum(chooser.astype(jnp.int32) * (slot_ids + 1)[None, :], axis=1) - 1
    came_rows, came_slot = (
        lax.all_to_all(
            send_rows.reshape(shard_count, pair_cap, -1),
            "seq",
            split_axis=0,
            concat_axis=0,
            tiled=True,
        ),
        lax.all_to_all(
            send_slot.reshape(shard_count, pair_cap), "seq", split_axis=0, concat_axis=0, tiled=True
        ),
    )
    came_slot = came_slot.reshape(-1)
    placer = (
        came_slot[None, :]
        == lax.broadcasted_iota(jnp.int32, (local_rows, shard_count * pair_cap), 0)
    ).astype(jnp.bfloat16)
    placed = jnp.dot(
        placer, came_rows.reshape(shard_count * pair_cap, -1), preferred_element_type=jnp.float32
    ).astype(jnp.bfloat16)
    projected = jnp.dot(placed, w_qkv, preferred_element_type=jnp.float32).astype(jnp.bfloat16)
    query_rows = projected[:, :inner_width]
    key_rows = projected[:, inner_width : 2 * inner_width]
    value_rows = projected[:, 2 * inner_width :]
    query_heads = split_heads(query_rows)
    initial = (
        jnp.full((HEADS, local_rows), neg_large, jnp.float32),
        jnp.zeros((HEADS, local_rows), jnp.float32),
        jnp.zeros((HEADS, local_rows, HEAD_DIM), jnp.float32),
    )
    row_max, row_total, weighted = forward_fold(
        query_heads,
        initial,
        (
            lax.all_gather(key_rows, "seq", axis=0, tiled=True),
            lax.all_gather(value_rows, "seq", axis=0, tiled=True),
        ),
    )
    attended_rows = head_rows((weighted / row_total[:, :, None]).astype(jnp.bfloat16))
    grad_rows = out_grad[0]
    grad_heads = split_heads(grad_rows)
    log_total = row_max + jnp.log(row_total)
    grad_dot = jnp.sum(
        grad_heads.astype(jnp.float32) * split_heads(attended_rows).astype(jnp.float32), axis=2
    )
    blank = jnp.zeros((HEADS, local_rows, HEAD_DIM), jnp.float32)
    query_step = query_fold(query_heads, grad_heads, log_total, grad_dot.T)
    query_grad = query_step(
        blank,
        (
            lax.all_gather(key_rows, "seq", axis=0, tiled=True),
            lax.all_gather(value_rows, "seq", axis=0, tiled=True),
        ),
        jnp.int32(0),
    )
    all_log, all_dot = (
        lax.all_gather(log_total.T, "seq", axis=0, tiled=True),
        lax.all_gather(grad_dot, "seq", axis=0, tiled=True),
    )
    key_grad, value_grad = key_fold(
        split_heads(key_rows),
        split_heads(value_rows),
        all_log,
        all_dot,
        (
            lax.all_gather(query_rows, "seq", axis=0, tiled=True),
            lax.all_gather(grad_rows, "seq", axis=0, tiled=True),
        ),
    )
    proj_grad = jnp.concatenate(
        [head_rows(query_grad), head_rows(key_grad), head_rows(value_grad)], axis=1
    ).astype(jnp.bfloat16)
    placed_grad = jnp.einsum(
        "rc,dc->rd", proj_grad, w_qkv, preferred_element_type=jnp.float32
    ).astype(jnp.bfloat16)
    partial_value = jnp.einsum(
        "rd,rc->dc", placed, proj_grad, preferred_element_type=jnp.float32
    ).astype(jnp.bfloat16)
    across = lax.psum_scatter(partial_value, "seq", scatter_dimension=0, tiled=True).astype(
        jnp.float32
    )
    weight_grad = lax.psum_scatter(
        across.astype(jnp.bfloat16), "clip", scatter_dimension=1, tiled=True
    ).astype(jnp.float32)
    back_rows = jnp.einsum(
        "rj,rd->jd", placer, placed_grad, preferred_element_type=jnp.float32
    ).astype(jnp.bfloat16)
    returned = lax.all_to_all(
        back_rows.reshape(shard_count, pair_cap, -1), "seq", split_axis=0, concat_axis=0, tiled=True
    )
    token_grad = jnp.einsum(
        "jt,jd->td",
        chooser_half,
        returned.reshape(shard_count * pair_cap, -1),
        preferred_element_type=jnp.float32,
    ).astype(jnp.bfloat16)
    patch_sums = jnp.einsum(
        "tp,td->pd", member_half, token_grad, preferred_element_type=jnp.float32
    )
    patch_count = jnp.sum(member.astype(jnp.float32) * counts[:, None], axis=0)
    patch_grad = (patch_sums / patch_count[:, None]).astype(jnp.bfloat16)
    return (attended_rows[None], patch_grad[None], weight_grad)


VMEM_LIMIT = 40 * 1024 * 1024
NN = (((1,), (0,)), ((), ()))
NT = (((1,), (1,)), ((), ()))
TN = (((0,), (0,)), ((), ()))


def dot(left, right, dims=NN):
    return lax.dot_general(left, right, dims, preferred_element_type=jnp.float32)


def call(body, outs, *args, scratch=(), space=None, limit=VMEM_LIMIT, outer=None, alias={}, flops=0):
    space = space or [pltpu.VMEM] * len(args)
    return pl.pallas_call(
        body,
        out_shape=outs,
        in_specs=[pl.BlockSpec(memory_space=each) for each in space],
        out_specs=jax.tree.map(lambda _: pl.BlockSpec(memory_space=outer or pltpu.VMEM), outs),
        input_output_aliases=alias,
        scratch_shapes=scratch,
        cost_estimate=pl.CostEstimate(flops=flops, bytes_accessed=0, transcendentals=0),
        compiler_params=pltpu.CompilerParams(vmem_limit_bytes=limit),
    )(*args)


def one_hot(condition):
    return jnp.where(condition, 1.0, 0.0).astype(jnp.bfloat16)


def fold_half(rows):
    half = rows.shape[0] // 2
    return jnp.concatenate([rows[:half], rows[half:]], axis=1)


def unfold_half(rows):
    width = rows.shape[1] // 2
    return jnp.concatenate([rows[:, :width], rows[:, width:]], axis=0)


def wide_row(row):
    short = 256 - row.shape[1]
    wide = row.astype(jnp.float32)
    wide = jnp.concatenate([wide, jnp.full((1, short), -1.0, jnp.float32)], axis=1)
    return wide[:, :128], wide[:, 128:]


def token_kernel(*refs):
    sources, refs = refs[:6], refs[6:]
    sends, refs = refs[:HEADS], refs[HEADS:]
    (target_ref, segment_out, held_ref), refs = refs[:3], refs[3:]
    segment_ref, patch_ref, shard_ref, slot_ref, grad_ref, w_ref, done = refs
    pairs = list(zip(sources, refs))[:-1]
    for part in range(3):
        columns = pl.ds(part * grad_ref.shape[1], grad_ref.shape[1])
        pairs.append((sources[5].at[:, columns], w_ref.at[part]))
    copies = [
        pltpu.make_async_copy(source, held, done.at[index])
        for index, (source, held) in enumerate(pairs)
    ]
    for copy in copies:
        copy.start()
    token_cap = shard_ref.shape[1]
    local_rows, inner = grad_ref.shape
    devices = len(sends)
    width = patch_ref.shape[1] // devices
    copies[0].wait()
    segment = segment_ref[...]
    segment_out[...] = segment
    member = lax.broadcasted_iota(jnp.int32, (token_cap, segment.shape[1]), 0) == segment
    counts = jnp.sum(jnp.where(member, 1.0, 0.0), axis=1, keepdims=True)
    copies[1].wait()
    token_sums = dot(one_hot(member), patch_ref[...])
    tokens = (token_sums / jnp.maximum(counts, 1.0)).astype(jnp.bfloat16)
    for copy in copies[2:5]:
        copy.wait()
    shard, slot = shard_ref[...], slot_ref[...]
    target_ref[...] = jnp.where(shard >= 0, shard * local_rows + slot, -1)
    shard_low, shard_high = wide_row(shard)
    slot_low, slot_high = wide_row(slot)
    line = lax.broadcasted_iota(jnp.int32, (16, 128), 0)
    where_to = jnp.where(
        line == 0,
        shard_low,
        jnp.where(line == 1, shard_high, jnp.where(line == 2, slot_low, slot_high)),
    ).astype(jnp.bfloat16)
    grads = grad_ref[...]
    half = token_cap + token_cap // 2
    for head in range(devices):
        first = head * HEAD_DIM
        start = half
        for piece in (
            where_to,
            fold_half(grads[:, first : first + HEAD_DIM]),
            tokens[:, head * width : (head + 1) * width],
        ):
            held_ref[head, start : start + piece.shape[0]] = piece
            start += piece.shape[0]
    for part, copy in enumerate(copies[5:]):
        copy.wait()
        projected = dot(tokens, w_ref[part]).astype(jnp.bfloat16)
        for head in range(devices):
            rows = projected[:, head * HEAD_DIM : (head + 1) * HEAD_DIM]
            if part < 2:
                held_ref[head, :token_cap, part * HEAD_DIM : (part + 1) * HEAD_DIM] = rows
            else:
                held_ref[head, token_cap:half] = fold_half(rows)
    me = lax.axis_index("seq")
    for flip, send in enumerate(sends):
        send[...] = held_ref[jnp.bitwise_xor(me, flip)]


def target_row(lines, token_cap, local_rows):
    lines = lines.astype(jnp.float32)
    shard = jnp.concatenate([lines[0:1], lines[1:2]], axis=1)[:, :token_cap]
    slot = jnp.concatenate([lines[2:3], lines[3:4]], axis=1)[:, :token_cap]
    return (shard * local_rows + slot).astype(jnp.int32)


def place_rows(token_cap, rows, pieces, target_ref, grad_ref):
    local_rows = grad_ref.shape[1]
    lines_at = token_cap + token_cap // 2
    targets, rows_in = [], []
    for index, piece in enumerate(pieces):
        target = target_row(piece[lines_at : lines_at + 16], token_cap, local_rows)
        target_ref[index] = target
        targets.append(target)
        value = unfold_half(piece[token_cap:lines_at])
        rows_in.append(jnp.concatenate([piece[:token_cap], value], axis=1))
        grad_ref[index] = unfold_half(piece[lines_at + 16 : lines_at + 16 + local_rows // 2])
    row_id = lax.broadcasted_iota(jnp.int32, (rows, len(pieces) * token_cap), 0)
    placer = one_hot(row_id == jnp.concatenate(targets, axis=1))
    return dot(placer, jnp.concatenate(rows_in, axis=0))


def early_kernel(token_cap, *refs):
    pieces, (total_ref, target_ref, grad_ref) = refs[:-3], refs[-3:]
    total = place_rows(token_cap, total_ref.shape[0], pieces, target_ref, grad_ref)
    total_ref[...] = total.astype(jnp.bfloat16)


def head_kernel(token_cap, flips, early_ref, early_grad_ref, *refs):
    early = early_grad_ref.shape[0]
    pieces, refs = refs[: HEADS - early], refs[HEADS - early :]
    outs, (target_ref, late_grad_ref, grad_ref, attended_ref) = refs[: HEADS // 2], refs[HEADS // 2 :]
    devices, local_rows = len(flips), grad_ref.shape[1]
    rows = devices * local_rows
    scaling = HEAD_DIM ** (-0.5)
    me = lax.axis_index("seq")
    total = place_rows(token_cap, rows, pieces, target_ref, late_grad_ref)
    total = total + early_ref[...].astype(jnp.float32)
    for index, flip in enumerate(flips):
        came = early_grad_ref[index] if index < early else late_grad_ref[index - early]
        grad_ref[jnp.bitwise_xor(me, flip)] = came
    projected = total.astype(jnp.bfloat16)
    query = projected[:, :HEAD_DIM]
    key = projected[:, HEAD_DIM : 2 * HEAD_DIM]
    value = projected[:, 2 * HEAD_DIM :]
    grad = jnp.concatenate([grad_ref[place] for place in range(devices)], axis=0)
    query = query * jnp.bfloat16(scaling)
    scores = dot(key, query, NT)
    weights = jnp.exp(scores - jnp.max(scores, axis=0, keepdims=True))
    row_total = jnp.sum(weights, axis=0, keepdims=True)
    inverse = 1.0 / row_total
    attended = (dot(value, weights.astype(jnp.bfloat16), TN) * inverse).astype(jnp.bfloat16)
    products = grad.T.astype(jnp.float32) * attended.astype(jnp.float32)
    grad_dot = jnp.sum(products, axis=0, keepdims=True)
    probability = weights * inverse
    score_grad = (probability * (dot(value, grad, NT) - grad_dot)).astype(jnp.bfloat16)
    value_grad = dot(probability.astype(jnp.bfloat16), grad)
    key_grad = dot(score_grad, query)
    query_grad = (dot(key, score_grad, TN) * scaling).astype(jnp.bfloat16).T
    attended = attended.T
    for place in range(devices):
        attended_ref[place] = fold_half(attended[place * local_rows : (place + 1) * local_rows])
    proj_grad = jnp.concatenate([query_grad, key_grad.astype(jnp.bfloat16)], axis=1)
    value_grad = fold_half(value_grad.astype(jnp.bfloat16))
    end = rows + rows // 2
    for chip, out in enumerate(outs):
        out[:rows] = proj_grad
        out[rows:end] = value_grad
        for core in range(2):
            first = end + core * local_rows // 2
            place = jnp.bitwise_xor(me, 2 * chip + core)
            out[first : first + local_rows // 2] = attended_ref[place]


def block_kernel(early_ref, late_ref, *refs):
    pieces, placed_ref = refs[:-1], refs[-1]
    early, _, token_cap = early_ref.shape
    rows = placed_ref.shape[1]
    targets = [early_ref[index] for index in range(early)]
    targets += [late_ref[index] for index in range(len(pieces) - early)]
    row_id = lax.broadcasted_iota(jnp.int32, (rows, len(pieces) * token_cap), 0)
    placer = one_hot(row_id == jnp.concatenate(targets, axis=1))
    rows_in = [piece[piece.shape[0] - token_cap :] for piece in pieces]
    placed_ref[...] = dot(placer, jnp.concatenate(rows_in, axis=0)).T.astype(jnp.bfloat16)


def head_columns(left, pieces):
    rows = left.shape[1]
    half, end = rows // 2, rows + rows // 2
    wide = 2 * HEAD_DIM
    both = dot(left, jnp.concatenate([piece[:rows] for piece in pieces], axis=1))
    folded = jnp.concatenate([piece[rows:end] for piece in pieces], axis=1)
    low, high = dot(left[:, :half], folded), dot(left[:, half:], folded)
    columns = []
    for first in range(0, both.shape[1], wide):
        value = low[:, first : first + HEAD_DIM] + high[:, first + HEAD_DIM : first + wide]
        columns.append(jnp.concatenate([both[:, first : first + wide], value], axis=1))
    return columns


def in_order(held_ref):
    return jnp.concatenate(
        [
            held_ref[head, :, part * HEAD_DIM : (part + 1) * HEAD_DIM]
            for part in range(3)
            for head in range(held_ref.shape[0])
        ],
        axis=1,
    )


def near_kernel(flips, last, placed_ref, *refs):
    pieces, outs, (held_ref, block_ref) = refs[: len(flips)], refs[len(flips) : -2], refs[-2:]
    seq, clip = lax.axis_index("seq"), lax.axis_index("clip")
    held_ref[jnp.bitwise_xor(seq, last)] = jnp.zeros(held_ref.shape[1:], held_ref.dtype)
    for flip, columns in zip(flips, head_columns(placed_ref[...], pieces)):
        held_ref[jnp.bitwise_xor(seq, flip)] = columns.astype(jnp.bfloat16)
    columns = in_order(held_ref)
    width = columns.shape[1] // len(outs)
    for index in range(len(outs)):
        block_ref[index] = columns[:, index * width : (index + 1) * width]
    for flip, out in enumerate(outs):
        out[...] = block_ref[jnp.bitwise_xor(clip, flip)]


def weight_kernel(last, placed_ref, piece_ref, *refs):
    count = len(refs) // 2
    head = jnp.bitwise_xor(lax.axis_index("seq"), last)
    columns = head_columns(placed_ref[...], [piece_ref])[0].astype(jnp.bfloat16)
    width = refs[0].shape[1]
    groups = width // HEAD_DIM
    wide = [
        jnp.concatenate([columns[:, part * HEAD_DIM : (part + 1) * HEAD_DIM]] * groups, axis=1)
        for part in range(3)
    ]
    lane = lax.broadcasted_iota(jnp.int32, (1, width), 1)
    for flip in range(count):
        place = jnp.bitwise_xor(lax.axis_index("clip"), flip) * width + lane
        others = refs[flip][...]
        for part in range(3):
            first = (part * HEADS + head) * HEAD_DIM
            mine = (place >= first) & (place < first + HEAD_DIM)
            others = jnp.where(mine, wide[part], others)
        refs[count + flip][...] = others


def patch_kernel(flips, segment_ref, target_ref, w_hbm, *refs):
    pieces, (patch_ref, attended_ref, held_ref, part_ref, w_ref, done) = refs[:HEADS], refs[HEADS:]
    copy = pltpu.make_async_copy(w_hbm, w_ref, done)
    copy.start()
    token_cap = target_ref.shape[1]
    local_rows = attended_ref.shape[0]
    rows = HEADS * local_rows
    me = lax.axis_index("seq")
    for flip, piece in zip(flips, pieces):
        first = rows + rows // 2 + flip % 2 * local_rows // 2
        part_ref[jnp.bitwise_xor(me, flip)] = unfold_half(piece[first : first + local_rows // 2])
    attended_ref[...] = jnp.concatenate([part_ref[head] for head in range(HEADS)], axis=1)
    row_id = lax.broadcasted_iota(jnp.int32, (rows, token_cap), 0)
    chooser = jnp.where(row_id == target_ref[...], 1.0, 0.0).T.astype(jnp.bfloat16)
    for flip, columns in zip(flips, head_columns(chooser, pieces)):
        held_ref[jnp.bitwise_xor(me, flip)] = columns.astype(jnp.bfloat16)
    proj_grad = in_order(held_ref)
    copy.wait()
    token_grad = dot(proj_grad, w_ref[...], NT).astype(jnp.bfloat16).astype(jnp.float32)
    member = (
        lax.broadcasted_iota(jnp.int32, (token_cap, segment_ref.shape[1]), 0) == segment_ref[...]
    )
    counts = jnp.sum(jnp.where(member, 1.0, 0.0), axis=1, keepdims=True)
    shared = (token_grad / jnp.maximum(counts, 1.0)).astype(jnp.bfloat16)
    patch_ref[...] = dot(one_hot(member), shared, TN).astype(jnp.bfloat16)


def follow_kernel(*refs):
    pass


def sum_kernel(*refs):
    total = refs[0][...].astype(jnp.float32)
    for ref in refs[1:-1]:
        total = total + ref[...].astype(jnp.float32)
    refs[-1][...] = total


def exchange(rows, axis, flip):
    count = lax.axis_size(axis)
    return lax.ppermute(rows, axis, [(index, index ^ flip) for index in range(count)])


def shape(*sizes, dtype=jnp.bfloat16):
    return jax.ShapeDtypeStruct(sizes, dtype)


def start_order(flip):
    steps = (flip // 2).bit_count()
    return flip > 0, -steps, flip % 2, -flip


def heads_plan(patches, segment, dest_shard, dest_slot, w_qkv, out_grad):
    devices = lax.axis_size("seq")
    clips = lax.axis_size("clip")
    token_cap = dest_shard.shape[1]
    local_rows, inner = out_grad.shape[1:]
    rows = devices * local_rows
    model = patches.shape[2]
    width = model // devices
    sent = token_cap + token_cap // 2 + 16 + local_rows // 2 + token_cap
    sources = (segment, patches[0], dest_shard, dest_slot, out_grad[0], w_qkv)
    outs = call(
        token_kernel,
        [shape(sent, 2 * HEAD_DIM)] * devices
        + [shape(1, token_cap, dtype=jnp.int32), shape(*segment.shape, dtype=jnp.int32)],
        *sources,
        scratch=[
            pltpu.VMEM((devices, sent, 2 * HEAD_DIM), jnp.bfloat16),
        ]
        + [pltpu.VMEM(source.shape, source.dtype) for source in sources[:-1]]
        + [
            pltpu.VMEM((3, model, inner), w_qkv.dtype),
            pltpu.SemaphoreType.DMA((len(sources) + 2,)),
        ],
        space=[pltpu.HBM] * len(sources),
        limit=62 * 1024 * 1024,
    )
    sends, (target, segment) = list(outs[:devices]), outs[devices:]
    order = sorted(range(devices), key=start_order)
    came = {0: sends[0]}
    for flip in order[1:]:
        came[flip] = exchange(sends[flip], "seq", flip)
    came = [came[flip] for flip in order]
    early = devices // 2 + 1
    placed, early_targets, early_grads = call(
        functools.partial(early_kernel, token_cap),
        [
            shape(rows, 3 * HEAD_DIM),
            shape(early, 1, token_cap, dtype=jnp.int32),
            shape(early, local_rows, HEAD_DIM),
        ],
        *came[:early],
        flops=1_000_000_000,
    )
    *proj, late_targets = call(
        functools.partial(head_kernel, token_cap, order),
        [shape(rows + rows // 2 + local_rows, 2 * HEAD_DIM)] * (devices // 2)
        + [shape(devices - early, 1, token_cap, dtype=jnp.int32)],
        placed,
        early_grads,
        *came[early:],
        scratch=[
            pltpu.VMEM((devices - early, local_rows, HEAD_DIM), jnp.bfloat16),
            pltpu.VMEM((devices, local_rows, HEAD_DIM), jnp.bfloat16),
            pltpu.VMEM((devices, local_rows // 2, 2 * HEAD_DIM), jnp.bfloat16),
        ],
    )
    pieces = {0: proj[0]}
    for flip in order[1:]:
        if flip % 2 == 0:
            pieces[flip] = exchange(proj[flip // 2], "seq", flip)
    placed = call(block_kernel, shape(width, rows), early_targets, late_targets, *came)
    first = devices // 2
    pieces[first] = call(
        follow_kernel,
        shape(*pieces[first].shape),
        pieces[first],
        placed,
        space=[pl.ANY] * 2,
        outer=pl.ANY,
        alias={0: 0},
    )
    for flip in list(pieces):
        pieces[flip + 1] = exchange(pieces[flip], "seq", 1)
    flips = [chip ^ core for chip in range(devices - 2, -1, -2) for core in range(2)]
    pieces = [pieces[flip] for flip in flips]
    last = devices - 1
    near = [flip for flip in order if flip != last]
    blocks = [shape(width, 3 * inner // clips)] * clips
    weights = call(
        functools.partial(near_kernel, near, last),
        blocks,
        placed,
        *[pieces[flips.index(flip)] for flip in near],
        scratch=[
            pltpu.VMEM((devices, width, 3 * HEAD_DIM), jnp.bfloat16),
            pltpu.VMEM((clips, width, 3 * inner // clips), jnp.bfloat16),
        ],
    )
    weights = call(
        functools.partial(weight_kernel, last),
        blocks,
        placed,
        pieces[flips.index(last)],
        *weights,
    )
    clip_flips = sorted(range(1, clips), key=lambda flip: (flip != clips // 2, flip))
    weights = [weights[0]] + [exchange(weights[flip], "clip", flip) for flip in clip_flips]
    patch_grad, attended = call(
        functools.partial(patch_kernel, flips),
        [shape(patches.shape[1], model), shape(local_rows, inner)],
        segment,
        target,
        w_qkv,
        *pieces,
        scratch=[
            pltpu.VMEM((devices, token_cap, 3 * HEAD_DIM), jnp.bfloat16),
            pltpu.VMEM((devices, local_rows, HEAD_DIM), jnp.bfloat16),
            pltpu.VMEM(w_qkv.shape, w_qkv.dtype),
            pltpu.SemaphoreType.DMA(()),
        ],
        space=[pltpu.VMEM] * 2 + [pltpu.HBM] + [pltpu.VMEM] * devices,
    )
    weight_grad = call(
        sum_kernel, shape(width, 3 * inner // clips, dtype=jnp.float32), *weights
    )
    return attended[None], patch_grad[None], weight_grad


def solution(mesh):
    devices, clips = mesh.shape["seq"], mesh.shape["clip"]
    one_head_each = devices == HEADS and clips in (1, 2, 4, 8)
    return jax.shard_map(
        heads_plan if one_head_each else rows_plan,
        mesh=mesh,
        in_specs=(
            P("clip", "seq", None),
            P("clip", "seq"),
            P("clip", "seq"),
            P("clip", "seq"),
            P(),
            P("clip", "seq", None),
        ),
        out_specs=(P("clip", "seq", None), P("clip", "seq", None), P("seq", "clip")),
        check_vma=False,
    )
```

```python
import functools

import jax
import jax.numpy as jnp
from jax import lax
from jax.experimental import pallas as pl
from jax.experimental.pallas import tpu as pltpu
from jax.sharding import PartitionSpec as P

HEADS = 8
HEAD_DIM = 64


neg_large = -1e30


def split_heads(rows_in):
    return rows_in.reshape(rows_in.shape[0], HEADS, HEAD_DIM)


def forward_fold(query_heads, running, pieces):
    scaling = HEAD_DIM ** (-0.5)
    row_max, row_total, weighted = running
    key_heads = split_heads(pieces[0])
    value_heads = split_heads(pieces[1])
    scores = (
        jnp.einsum("rhd,khd->hrk", query_heads, key_heads, preferred_element_type=jnp.float32)
        * scaling
    )
    new_max = jnp.maximum(row_max, jnp.max(scores, axis=2))
    weights = jnp.exp(scores - new_max[:, :, None])
    row_total = jnp.sum(weights, axis=2)
    weighted = jnp.einsum(
        "hrk,khd->hrd",
        weights.astype(jnp.bfloat16),
        value_heads,
        preferred_element_type=jnp.float32,
    )
    return (new_max, row_total, weighted)


def query_fold(query_heads, grad_heads, log_total, grad_dot):
    scaling = HEAD_DIM ** (-0.5)

    def combine_piece(running, pieces, offset):
        key_heads = split_heads(pieces[0])
        value_heads = split_heads(pieces[1])
        scores = (
            jnp.einsum("rhd,khd->hrk", query_heads, key_heads, preferred_element_type=jnp.float32)
            * scaling
        )
        probability = jnp.exp(scores - log_total[:, :, None])
        prob_grad = jnp.einsum(
            "rhd,khd->hrk", grad_heads, value_heads, preferred_element_type=jnp.float32
        )
        score_grad = (probability * (prob_grad - grad_dot[:, :, None])).astype(jnp.bfloat16)
        return (
            jnp.einsum("hrk,khd->hrd", score_grad, key_heads, preferred_element_type=jnp.float32)
            * scaling
        )

    return combine_piece


def key_fold(key_heads, value_heads, all_log, all_dot, pieces):
    scaling = HEAD_DIM ** (-0.5)
    piece_query = split_heads(pieces[0])
    piece_grad = split_heads(pieces[1])
    piece_log = all_log.T
    piece_dot = all_dot.T
    scores = (
        jnp.einsum("qhd,khd->hqk", piece_query, key_heads, preferred_element_type=jnp.float32)
        * scaling
    )
    probability = jnp.exp(scores - piece_log[:, :, None])
    value_grad = jnp.einsum(
        "hqk,qhd->hkd",
        probability.astype(jnp.bfloat16),
        piece_grad,
        preferred_element_type=jnp.float32,
    )
    prob_grad = jnp.einsum(
        "qhd,khd->hqk", piece_grad, value_heads, preferred_element_type=jnp.float32
    )
    score_grad = (probability * (prob_grad - piece_dot[:, :, None])).astype(jnp.bfloat16)
    key_grad = (
        jnp.einsum("hqk,qhd->hkd", score_grad, piece_query, preferred_element_type=jnp.float32)
        * scaling
    )
    return (key_grad, value_grad)


def head_rows(matrix):
    return matrix.transpose(1, 0, 2).reshape(matrix.shape[1], HEADS * HEAD_DIM)


def rows_plan(patches, segment, dest_shard, dest_slot, w_qkv, out_grad):
    shard_count = lax.axis_size("seq")
    patch_rows = patches[0]
    patch_token = segment[0]
    targets = dest_shard[0]
    slot_ids = dest_slot[0]
    token_cap = targets.shape[0]
    pair_cap = token_cap // shard_count
    local_rows = out_grad.shape[1]
    inner_width = HEADS * HEAD_DIM
    member = (
        lax.broadcasted_iota(jnp.int32, (token_cap, patch_token.shape[0]), 0)
        == patch_token[None, :]
    )
    member_half = member.astype(jnp.bfloat16)
    counts = jnp.sum(member.astype(jnp.float32), axis=1)
    token_sums = jnp.dot(member_half, patch_rows, preferred_element_type=jnp.float32)
    tokens = (token_sums / jnp.maximum(counts, 1.0)[:, None]).astype(jnp.bfloat16)
    to_shard = (
        targets[:, None] == lax.broadcasted_iota(jnp.int32, (token_cap, shard_count), 1)
    ).astype(jnp.int32)
    ranking = jnp.sum((jnp.cumsum(to_shard, axis=0) - 1) * to_shard, axis=1)
    position = jnp.where(targets >= 0, targets * pair_cap + ranking, -1)
    chooser = position[None, :] == lax.broadcasted_iota(
        jnp.int32, (shard_count * pair_cap, token_cap), 0
    )
    chooser_half = chooser.astype(jnp.bfloat16)
    send_rows = jnp.dot(chooser_half, tokens, preferred_element_type=jnp.float32).astype(
        jnp.bfloat16
    )
    send_slot = jnp.sum(chooser.astype(jnp.int32) * (slot_ids + 1)[None, :], axis=1) - 1
    came_rows, came_slot = (
        lax.all_to_all(
            send_rows.reshape(shard_count, pair_cap, -1),
            "seq",
            split_axis=0,
            concat_axis=0,
            tiled=True,
        ),
        lax.all_to_all(
            send_slot.reshape(shard_count, pair_cap), "seq", split_axis=0, concat_axis=0, tiled=True
        ),
    )
    came_slot = came_slot.reshape(-1)
    placer = (
        came_slot[None, :]
        == lax.broadcasted_iota(jnp.int32, (local_rows, shard_count * pair_cap), 0)
    ).astype(jnp.bfloat16)
    placed = jnp.dot(
        placer, came_rows.reshape(shard_count * pair_cap, -1), preferred_element_type=jnp.float32
    ).astype(jnp.bfloat16)
    projected = jnp.dot(placed, w_qkv, preferred_element_type=jnp.float32).astype(jnp.bfloat16)
    query_rows = projected[:, :inner_width]
    key_rows = projected[:, inner_width : 2 * inner_width]
    value_rows = projected[:, 2 * inner_width :]
    query_heads = split_heads(query_rows)
    initial = (
        jnp.full((HEADS, local_rows), neg_large, jnp.float32),
        jnp.zeros((HEADS, local_rows), jnp.float32),
        jnp.zeros((HEADS, local_rows, HEAD_DIM), jnp.float32),
    )
    row_max, row_total, weighted = forward_fold(
        query_heads,
        initial,
        (
            lax.all_gather(key_rows, "seq", axis=0, tiled=True),
            lax.all_gather(value_rows, "seq", axis=0, tiled=True),
        ),
    )
    attended_rows = head_rows((weighted / row_total[:, :, None]).astype(jnp.bfloat16))
    grad_rows = out_grad[0]
    grad_heads = split_heads(grad_rows)
    log_total = row_max + jnp.log(row_total)
    grad_dot = jnp.sum(
        grad_heads.astype(jnp.float32) * split_heads(attended_rows).astype(jnp.float32), axis=2
    )
    blank = jnp.zeros((HEADS, local_rows, HEAD_DIM), jnp.float32)
    query_step = query_fold(query_heads, grad_heads, log_total, grad_dot.T)
    query_grad = query_step(
        blank,
        (
            lax.all_gather(key_rows, "seq", axis=0, tiled=True),
            lax.all_gather(value_rows, "seq", axis=0, tiled=True),
        ),
        jnp.int32(0),
    )
    all_log, all_dot = (
        lax.all_gather(log_total.T, "seq", axis=0, tiled=True),
        lax.all_gather(grad_dot, "seq", axis=0, tiled=True),
    )
    key_grad, value_grad = key_fold(
        split_heads(key_rows),
        split_heads(value_rows),
        all_log,
        all_dot,
        (
            lax.all_gather(query_rows, "seq", axis=0, tiled=True),
            lax.all_gather(grad_rows, "seq", axis=0, tiled=True),
        ),
    )
    proj_grad = jnp.concatenate(
        [head_rows(query_grad), head_rows(key_grad), head_rows(value_grad)], axis=1
    ).astype(jnp.bfloat16)
    placed_grad = jnp.einsum(
        "rc,dc->rd", proj_grad, w_qkv, preferred_element_type=jnp.float32
    ).astype(jnp.bfloat16)
    partial_value = jnp.einsum(
        "rd,rc->dc", placed, proj_grad, preferred_element_type=jnp.float32
    ).astype(jnp.bfloat16)
    across = lax.psum_scatter(partial_value, "seq", scatter_dimension=0, tiled=True).astype(
        jnp.float32
    )
    weight_grad = lax.psum_scatter(
        across.astype(jnp.bfloat16), "clip", scatter_dimension=1, tiled=True
    ).astype(jnp.float32)
    back_rows = jnp.einsum(
        "rj,rd->jd", placer, placed_grad, preferred_element_type=jnp.float32
    ).astype(jnp.bfloat16)
    returned = lax.all_to_all(
        back_rows.reshape(shard_count, pair_cap, -1), "seq", split_axis=0, concat_axis=0, tiled=True
    )
    token_grad = jnp.einsum(
        "jt,jd->td",
        chooser_half,
        returned.reshape(shard_count * pair_cap, -1),
        preferred_element_type=jnp.float32,
    ).astype(jnp.bfloat16)
    patch_sums = jnp.einsum(
        "tp,td->pd", member_half, token_grad, preferred_element_type=jnp.float32
    )
    patch_count = jnp.sum(member.astype(jnp.float32) * counts[:, None], axis=0)
    patch_grad = (patch_sums / patch_count[:, None]).astype(jnp.bfloat16)
    return (attended_rows[None], patch_grad[None], weight_grad)


VMEM_LIMIT = 40 * 1024 * 1024
NN = (((1,), (0,)), ((), ()))
NT = (((1,), (1,)), ((), ()))
TN = (((0,), (0,)), ((), ()))


def dot(left, right, dims=NN):
    return lax.dot_general(left, right, dims, preferred_element_type=jnp.float32)


def call(body, outs, *args, scratch=(), space=None, limit=VMEM_LIMIT, outer=None, alias={}, flops=0):
    space = space or [pltpu.VMEM] * len(args)
    return pl.pallas_call(
        body,
        out_shape=outs,
        in_specs=[pl.BlockSpec(memory_space=each) for each in space],
        out_specs=jax.tree.map(lambda _: pl.BlockSpec(memory_space=outer or pltpu.VMEM), outs),
        input_output_aliases=alias,
        scratch_shapes=scratch,
        cost_estimate=pl.CostEstimate(flops=flops, bytes_accessed=0, transcendentals=0),
        compiler_params=pltpu.CompilerParams(vmem_limit_bytes=limit),
    )(*args)


def one_hot(condition):
    return jnp.where(condition, 1.0, 0.0).astype(jnp.bfloat16)


def fold_half(rows):
    half = rows.shape[0] // 2
    return jnp.concatenate([rows[:half], rows[half:]], axis=1)


def unfold_half(rows):
    width = rows.shape[1] // 2
    return jnp.concatenate([rows[:, :width], rows[:, width:]], axis=0)


def wide_row(row):
    short = 256 - row.shape[1]
    wide = row.astype(jnp.float32)
    wide = jnp.concatenate([wide, jnp.full((1, short), -1.0, jnp.float32)], axis=1)
    return wide[:, :128], wide[:, 128:]


def token_kernel(*refs):
    sources, refs = refs[:6], refs[6:]
    sends, refs = refs[:HEADS], refs[HEADS:]
    (target_ref, segment_out, held_ref), refs = refs[:3], refs[3:]
    segment_ref, patch_ref, shard_ref, slot_ref, grad_ref, w_ref, done = refs
    pairs = list(zip(sources, refs))[:-1]
    for part in range(3):
        columns = pl.ds(part * grad_ref.shape[1], grad_ref.shape[1])
        pairs.append((sources[5].at[:, columns], w_ref.at[part]))
    copies = [
        pltpu.make_async_copy(source, held, done.at[index])
        for index, (source, held) in enumerate(pairs)
    ]
    for copy in copies:
        copy.start()
    token_cap = shard_ref.shape[1]
    local_rows, inner = grad_ref.shape
    devices = len(sends)
    width = patch_ref.shape[1] // devices
    copies[0].wait()
    segment = segment_ref[...]
    segment_out[...] = segment
    member = lax.broadcasted_iota(jnp.int32, (token_cap, segment.shape[1]), 0) == segment
    counts = jnp.sum(jnp.where(member, 1.0, 0.0), axis=1, keepdims=True)
    copies[1].wait()
    token_sums = dot(one_hot(member), patch_ref[...])
    tokens = (token_sums * (1.0 / jnp.maximum(counts, 1.0))).astype(jnp.bfloat16)
    for copy in copies[2:5]:
        copy.wait()
    shard, slot = shard_ref[...], slot_ref[...]
    target_ref[...] = jnp.where(shard >= 0, shard * local_rows + slot, -1)
    shard_low, shard_high = wide_row(shard)
    slot_low, slot_high = wide_row(slot)
    line = lax.broadcasted_iota(jnp.int32, (16, 128), 0)
    where_to = jnp.where(
        line == 0,
        shard_low,
        jnp.where(line == 1, shard_high, jnp.where(line == 2, slot_low, slot_high)),
    ).astype(jnp.bfloat16)
    grads = grad_ref[...]
    half = token_cap + token_cap // 2
    for head in range(devices):
        first = head * HEAD_DIM
        start = half
        for piece in (
            where_to,
            fold_half(grads[:, first : first + HEAD_DIM]),
            tokens[:, head * width : (head + 1) * width],
        ):
            held_ref[head, start : start + piece.shape[0]] = piece
            start += piece.shape[0]
    for part, copy in enumerate(copies[5:]):
        copy.wait()
        projected = dot(tokens, w_ref[part]).astype(jnp.bfloat16)
        for head in range(devices):
            rows = projected[:, head * HEAD_DIM : (head + 1) * HEAD_DIM]
            if part < 2:
                held_ref[head, :token_cap, part * HEAD_DIM : (part + 1) * HEAD_DIM] = rows
            else:
                held_ref[head, token_cap:half] = fold_half(rows)
    me = lax.axis_index("seq")
    for flip, send in enumerate(sends):
        send[...] = held_ref[jnp.bitwise_xor(me, flip)]


def target_row(lines, token_cap, local_rows):
    lines = lines.astype(jnp.float32)
    shard = jnp.concatenate([lines[0:1], lines[1:2]], axis=1)[:, :token_cap]
    slot = jnp.concatenate([lines[2:3], lines[3:4]], axis=1)[:, :token_cap]
    return (shard * local_rows + slot).astype(jnp.int32)


def place_rows(token_cap, rows, pieces, target_ref, grad_ref):
    local_rows = grad_ref.shape[1]
    lines_at = token_cap + token_cap // 2
    targets, rows_in = [], []
    for index, piece in enumerate(pieces):
        target = target_row(piece[lines_at : lines_at + 16], token_cap, local_rows)
        target_ref[index] = target
        targets.append(target)
        value = unfold_half(piece[token_cap:lines_at])
        rows_in.append(jnp.concatenate([piece[:token_cap], value], axis=1))
        grad_ref[index] = unfold_half(piece[lines_at + 16 : lines_at + 16 + local_rows // 2])
    row_id = lax.broadcasted_iota(jnp.int32, (rows, len(pieces) * token_cap), 0)
    placer = one_hot(row_id == jnp.concatenate(targets, axis=1))
    return dot(placer, jnp.concatenate(rows_in, axis=0))


def early_kernel(token_cap, *refs):
    pieces, (total_ref, target_ref, grad_ref) = refs[:-3], refs[-3:]
    total = place_rows(token_cap, total_ref.shape[0], pieces, target_ref, grad_ref)
    total_ref[...] = total.astype(jnp.bfloat16)


def head_kernel(token_cap, flips, early_ref, early_grad_ref, *refs):
    early = early_grad_ref.shape[0]
    pieces, refs = refs[: HEADS - early], refs[HEADS - early :]
    outs, (target_ref, late_grad_ref, grad_ref, attended_ref) = refs[: HEADS // 2], refs[HEADS // 2 :]
    devices, local_rows = len(flips), grad_ref.shape[1]
    rows = devices * local_rows
    scaling = HEAD_DIM ** (-0.5)
    me = lax.axis_index("seq")
    total = place_rows(token_cap, rows, pieces, target_ref, late_grad_ref)
    total = total + early_ref[...].astype(jnp.float32)
    for index, flip in enumerate(flips):
        came = early_grad_ref[index] if index < early else late_grad_ref[index - early]
        grad_ref[jnp.bitwise_xor(me, flip)] = came
    projected = total.astype(jnp.bfloat16)
    query = projected[:, :HEAD_DIM]
    key = projected[:, HEAD_DIM : 2 * HEAD_DIM]
    value = projected[:, 2 * HEAD_DIM :]
    grad = jnp.concatenate([grad_ref[place] for place in range(devices)], axis=0)
    query = query * jnp.bfloat16(scaling)
    scores = dot(key, query, NT)
    weights = jnp.exp(scores - jnp.max(scores, axis=0, keepdims=True))
    row_total = jnp.sum(weights, axis=0, keepdims=True)
    inverse = 1.0 / row_total
    attended = (dot(value, weights.astype(jnp.bfloat16), TN) * inverse).astype(jnp.bfloat16)
    products = grad.T.astype(jnp.float32) * attended.astype(jnp.float32)
    grad_dot = jnp.sum(products, axis=0, keepdims=True)
    probability = weights * inverse
    score_grad = (probability * (dot(value, grad, NT) - grad_dot)).astype(jnp.bfloat16)
    value_grad = dot(probability.astype(jnp.bfloat16), grad)
    key_grad = dot(score_grad, query)
    query_grad = (dot(key, score_grad, TN) * scaling).astype(jnp.bfloat16).T
    attended = attended.T
    for place in range(devices):
        attended_ref[place] = fold_half(attended[place * local_rows : (place + 1) * local_rows])
    proj_grad = jnp.concatenate([query_grad, key_grad.astype(jnp.bfloat16)], axis=1)
    value_grad = fold_half(value_grad.astype(jnp.bfloat16))
    end = rows + rows // 2
    for chip, out in enumerate(outs):
        out[:rows] = proj_grad
        out[rows:end] = value_grad
        for core in range(2):
            first = end + core * local_rows // 2
            place = jnp.bitwise_xor(me, 2 * chip + core)
            out[first : first + local_rows // 2] = attended_ref[place]


def block_kernel(early_ref, late_ref, *refs):
    pieces, placed_ref = refs[:-1], refs[-1]
    early, _, token_cap = early_ref.shape
    rows = placed_ref.shape[1]
    targets = [early_ref[index] for index in range(early)]
    targets += [late_ref[index] for index in range(len(pieces) - early)]
    row_id = lax.broadcasted_iota(jnp.int32, (rows, len(pieces) * token_cap), 0)
    placer = one_hot(row_id == jnp.concatenate(targets, axis=1))
    rows_in = [piece[piece.shape[0] - token_cap :] for piece in pieces]
    placed_ref[...] = dot(placer, jnp.concatenate(rows_in, axis=0)).T.astype(jnp.bfloat16)


def head_columns(left, pieces):
    rows = left.shape[1]
    half, end = rows // 2, rows + rows // 2
    wide = 2 * HEAD_DIM
    both = dot(left, jnp.concatenate([piece[:rows] for piece in pieces], axis=1))
    folded = jnp.concatenate([piece[rows:end] for piece in pieces], axis=1)
    low, high = dot(left[:, :half], folded), dot(left[:, half:], folded)
    columns = []
    for first in range(0, both.shape[1], wide):
        value = low[:, first : first + HEAD_DIM] + high[:, first + HEAD_DIM : first + wide]
        columns.append(jnp.concatenate([both[:, first : first + wide], value], axis=1))
    return columns


def in_order(held_ref):
    return jnp.concatenate(
        [
            held_ref[head, :, part * HEAD_DIM : (part + 1) * HEAD_DIM]
            for part in range(3)
            for head in range(held_ref.shape[0])
        ],
        axis=1,
    )


def near_kernel(flips, last, placed_ref, *refs):
    pieces, outs, (held_ref, block_ref) = refs[: len(flips)], refs[len(flips) : -2], refs[-2:]
    seq, clip = lax.axis_index("seq"), lax.axis_index("clip")
    held_ref[jnp.bitwise_xor(seq, last)] = jnp.zeros(held_ref.shape[1:], held_ref.dtype)
    for flip, columns in zip(flips, head_columns(placed_ref[...], pieces)):
        held_ref[jnp.bitwise_xor(seq, flip)] = columns.astype(jnp.bfloat16)
    columns = in_order(held_ref)
    width = columns.shape[1] // len(outs)
    for index in range(len(outs)):
        block_ref[index] = columns[:, index * width : (index + 1) * width]
    for flip, out in enumerate(outs):
        out[...] = block_ref[jnp.bitwise_xor(clip, flip)]


def weight_kernel(last, placed_ref, piece_ref, *refs):
    count = len(refs) // 2
    head = jnp.bitwise_xor(lax.axis_index("seq"), last)
    columns = head_columns(placed_ref[...], [piece_ref])[0].astype(jnp.bfloat16)
    width = refs[0].shape[1]
    groups = width // HEAD_DIM
    wide = [
        jnp.concatenate([columns[:, part * HEAD_DIM : (part + 1) * HEAD_DIM]] * groups, axis=1)
        for part in range(3)
    ]
    lane = lax.broadcasted_iota(jnp.int32, (1, width), 1)
    for flip in range(count):
        place = jnp.bitwise_xor(lax.axis_index("clip"), flip) * width + lane
        others = refs[flip][...]
        for part in range(3):
            first = (part * HEADS + head) * HEAD_DIM
            mine = (place >= first) & (place < first + HEAD_DIM)
            others = jnp.where(mine, wide[part], others)
        refs[count + flip][...] = others


def patch_kernel(flips, segment_ref, target_ref, w_hbm, *refs):
    pieces, (patch_ref, attended_ref, held_ref, part_ref, w_ref, done) = refs[:HEADS], refs[HEADS:]
    copy = pltpu.make_async_copy(w_hbm, w_ref, done)
    copy.start()
    token_cap = target_ref.shape[1]
    local_rows = attended_ref.shape[0]
    rows = HEADS * local_rows
    me = lax.axis_index("seq")
    for flip, piece in zip(flips, pieces):
        first = rows + rows // 2 + flip % 2 * local_rows // 2
        part_ref[jnp.bitwise_xor(me, flip)] = unfold_half(piece[first : first + local_rows // 2])
    attended_ref[...] = jnp.concatenate([part_ref[head] for head in range(HEADS)], axis=1)
    row_id = lax.broadcasted_iota(jnp.int32, (rows, token_cap), 0)
    chooser = jnp.where(row_id == target_ref[...], 1.0, 0.0).T.astype(jnp.bfloat16)
    for flip, columns in zip(flips, head_columns(chooser, pieces)):
        held_ref[jnp.bitwise_xor(me, flip)] = columns.astype(jnp.bfloat16)
    proj_grad = in_order(held_ref)
    copy.wait()
    token_grad = dot(proj_grad, w_ref[...], NT).astype(jnp.bfloat16).astype(jnp.float32)
    member = (
        lax.broadcasted_iota(jnp.int32, (token_cap, segment_ref.shape[1]), 0) == segment_ref[...]
    )
    counts = jnp.sum(jnp.where(member, 1.0, 0.0), axis=1, keepdims=True)
    shared = (token_grad / jnp.maximum(counts, 1.0)).astype(jnp.bfloat16)
    patch_ref[...] = dot(one_hot(member), shared, TN).astype(jnp.bfloat16)


def follow_kernel(*refs):
    pass


def sum_kernel(*refs):
    total = refs[0][...].astype(jnp.float32)
    for ref in refs[1:-1]:
        total = total + ref[...].astype(jnp.float32)
    refs[-1][...] = total


def exchange(rows, axis, flip):
    count = lax.axis_size(axis)
    return lax.ppermute(rows, axis, [(index, index ^ flip) for index in range(count)])


def shape(*sizes, dtype=jnp.bfloat16):
    return jax.ShapeDtypeStruct(sizes, dtype)


def start_order(flip):
    steps = (flip // 2).bit_count()
    return flip > 0, -steps, flip % 2, -flip


def heads_plan(patches, segment, dest_shard, dest_slot, w_qkv, out_grad):
    devices = lax.axis_size("seq")
    clips = lax.axis_size("clip")
    token_cap = dest_shard.shape[1]
    local_rows, inner = out_grad.shape[1:]
    rows = devices * local_rows
    model = patches.shape[2]
    width = model // devices
    sent = token_cap + token_cap // 2 + 16 + local_rows // 2 + token_cap
    sources = (segment, patches[0], dest_shard, dest_slot, out_grad[0], w_qkv)
    outs = call(
        token_kernel,
        [shape(sent, 2 * HEAD_DIM)] * devices
        + [shape(1, token_cap, dtype=jnp.int32), shape(*segment.shape, dtype=jnp.int32)],
        *sources,
        scratch=[
            pltpu.VMEM((devices, sent, 2 * HEAD_DIM), jnp.bfloat16),
        ]
        + [pltpu.VMEM(source.shape, source.dtype) for source in sources[:-1]]
        + [
            pltpu.VMEM((3, model, inner), w_qkv.dtype),
            pltpu.SemaphoreType.DMA((len(sources) + 2,)),
        ],
        space=[pltpu.HBM] * len(sources),
        limit=62 * 1024 * 1024,
    )
    sends, (target, segment) = list(outs[:devices]), outs[devices:]
    order = sorted(range(devices), key=start_order)
    came = {0: sends[0]}
    for flip in order[1:]:
        came[flip] = exchange(sends[flip], "seq", flip)
    came = [came[flip] for flip in order]
    early = devices // 2 + 1
    placed, early_targets, early_grads = call(
        functools.partial(early_kernel, token_cap),
        [
            shape(rows, 3 * HEAD_DIM),
            shape(early, 1, token_cap, dtype=jnp.int32),
            shape(early, local_rows, HEAD_DIM),
        ],
        *came[:early],
        flops=1_000_000_000,
    )
    *proj, late_targets = call(
        functools.partial(head_kernel, token_cap, order),
        [shape(rows + rows // 2 + local_rows, 2 * HEAD_DIM)] * (devices // 2)
        + [shape(devices - early, 1, token_cap, dtype=jnp.int32)],
        placed,
        early_grads,
        *came[early:],
        scratch=[
            pltpu.VMEM((devices - early, local_rows, HEAD_DIM), jnp.bfloat16),
            pltpu.VMEM((devices, local_rows, HEAD_DIM), jnp.bfloat16),
            pltpu.VMEM((devices, local_rows // 2, 2 * HEAD_DIM), jnp.bfloat16),
        ],
    )
    pieces = {0: proj[0]}
    for flip in order[1:]:
        if flip % 2 == 0:
            pieces[flip] = exchange(proj[flip // 2], "seq", flip)
    placed = call(block_kernel, shape(width, rows), early_targets, late_targets, *came)
    first = devices // 2
    pieces[first] = call(
        follow_kernel,
        shape(*pieces[first].shape),
        pieces[first],
        placed,
        space=[pl.ANY] * 2,
        outer=pl.ANY,
        alias={0: 0},
    )
    for flip in list(pieces):
        pieces[flip + 1] = exchange(pieces[flip], "seq", 1)
    flips = [chip ^ core for chip in range(devices - 2, -1, -2) for core in range(2)]
    pieces = [pieces[flip] for flip in flips]
    last = devices - 1
    near = [flip for flip in order if flip != last]
    blocks = [shape(width, 3 * inner // clips)] * clips
    weights = call(
        functools.partial(near_kernel, near, last),
        blocks,
        placed,
        *[pieces[flips.index(flip)] for flip in near],
        scratch=[
            pltpu.VMEM((devices, width, 3 * HEAD_DIM), jnp.bfloat16),
            pltpu.VMEM((clips, width, 3 * inner // clips), jnp.bfloat16),
        ],
    )
    weights = call(
        functools.partial(weight_kernel, last),
        blocks,
        placed,
        pieces[flips.index(last)],
        *weights,
    )
    clip_flips = sorted(range(1, clips), key=lambda flip: (flip != clips // 2, flip))
    weights = [weights[0]] + [exchange(weights[flip], "clip", flip) for flip in clip_flips]
    patch_grad, attended = call(
        functools.partial(patch_kernel, flips),
        [shape(patches.shape[1], model), shape(local_rows, inner)],
        segment,
        target,
        w_qkv,
        *pieces,
        scratch=[
            pltpu.VMEM((devices, token_cap, 3 * HEAD_DIM), jnp.bfloat16),
            pltpu.VMEM((devices, local_rows, HEAD_DIM), jnp.bfloat16),
            pltpu.VMEM(w_qkv.shape, w_qkv.dtype),
            pltpu.SemaphoreType.DMA(()),
        ],
        space=[pltpu.VMEM] * 2 + [pltpu.HBM] + [pltpu.VMEM] * devices,
    )
    weight_grad = call(
        sum_kernel, shape(width, 3 * inner // clips, dtype=jnp.float32), *weights
    )
    return attended[None], patch_grad[None], weight_grad


def solution(mesh):
    devices, clips = mesh.shape["seq"], mesh.shape["clip"]
    one_head_each = devices == HEADS and clips in (1, 2, 4, 8)
    return jax.shard_map(
        heads_plan if one_head_each else rows_plan,
        mesh=mesh,
        in_specs=(
            P("clip", "seq", None),
            P("clip", "seq"),
            P("clip", "seq"),
            P("clip", "seq"),
            P(),
            P("clip", "seq", None),
        ),
        out_specs=(P("clip", "seq", None), P("clip", "seq", None), P("seq", "clip")),
        check_vma=False,
    )
```
